256 devices in a mesh: lat: 16 (over z, core), lon: 16 (over y, x).
Axes of the slice: x: 4, y: 4, z: 8, core: 2. Of those that a mesh axis runs over, the one named last changes fastest.
Arguments:
- tile_counts: int32 [16, 16], P('lat', 'lon'), may hold values from 1 to 2, as said below
- obs_pos: float32 [16, 16, 3, 1024], P('lat', 'lon'), as said below
- innovation: float32 [16, 16, 3, 1024], P('lat', 'lon'), may hold values from -6 to 6
- bg_std_obs: float32 [16, 16, 3, 1024], P('lat', 'lon'), may hold values from 0.05 to 0.2
- obs_std: float32 [16, 16, 3, 1024], P('lat', 'lon'), may hold values from 0.3 to 1
- channel_corr: float32 [3, 3], replicated, as said below
- bg_std_grid: float32 [16, 16, 3, 512], P('lat', 'lon'), may hold values from 0.05 to 0.2
Outputs:
- analysis_weights: float32 [16, 16, 3, 1024], P('lat', 'lon')
- increment: float32 [16, 16, 3, 512], P('lat', 'lon')
The draws below stay inside these ranges and needn't reach their ends.
Inputs may be any that keep to these rules, and one draw needn't show every extreme that they name: Region (i, j) holds tile_counts[i, j] live tiles of 512 observations at its first slots; the other slots are padding. Some region holds 2 tiles in every draw. `obs_pos`: unit vectors; every slot of region (i, j), padding too, lies in that region: sine of latitude in -0.9 + 1.8 i / 16 to -0.9 + 1.8 (i + 1) / 16, longitude in 2 pi j / 16 to 2 pi (j + 1) / 16. `channel_corr`: Symmetric, unit diagonal, off-diagonal entries between 0.3 and 0.7.
All inputs are finite; a program needn't handle non-finite values.
Results may differ from the reference program's by a relative error of at most 0.0003.
Values sent between devices are 32-bit elements; how exact they have to be, the bound alone decides.
No kernel may reach another device: no remote copies, remote signals or barrier semaphores. Data moves between devices by JAX's collectives and lax.ppermute only.
A program may use at most 64 MiB of HBM per device.

```python
import math
import jax
import jax.numpy as jnp
from jax import lax

OBS_TILE = 512
TILES_DEV = 2
GRID_DEV = 512
GRID_ROWS = 16
ITERS = 3
OBS_DEV = 1024
N_LAT = 16
N_LON = 16


def draw_tile_counts(key, part):
    key = jax.random.fold_in(key, 11)
    key_one, key_two, key_top, key_low = jax.random.split(key, 4)
    first = jax.random.randint(key_one, (N_LAT * N_LON,), 1, TILES_DEV + 1)
    second = jax.random.randint(key_two, (N_LAT * N_LON,), 1, TILES_DEV + 1)
    counts = jnp.minimum(first, second)
    regions = N_LAT * N_LON
    top = jax.random.randint(key_top, (), 0, regions)
    low = (top + 1 + jax.random.randint(key_low, (), 0, regions - 1)) % regions
    counts = counts.at[top].set(TILES_DEV).at[low].set(1)
    return counts.reshape(N_LAT, N_LON).astype(jnp.int32)


def draw_obs_pos(key, part):
    key = jax.random.fold_in(key, 5)
    key_lat, key_lon, key_angle, key_radius = jax.random.split(key, 4)
    shape = (N_LAT, N_LON, OBS_DEV)
    frac_lat = jax.random.uniform(key_lat, shape, jnp.float32)
    frac_lon = jax.random.uniform(key_lon, shape, jnp.float32)
    band = jnp.arange(N_LAT, dtype=jnp.float32)[:, None, None]
    sector = jnp.arange(N_LON, dtype=jnp.float32)[None, :, None]
    sinlat = -0.9 + 1.8 * (band + frac_lat) / N_LAT
    longitude = 2.0 * math.pi * (sector + frac_lon) / N_LON
    coslat = jnp.sqrt(1.0 - sinlat * sinlat)
    spread_pos = jnp.stack([coslat * jnp.cos(longitude), coslat * jnp.sin(longitude), sinlat], axis=2)
    columns = GRID_DEV // GRID_ROWS
    centre_lat = (GRID_ROWS // 2 + 0.5) / GRID_ROWS
    centre_lon = (columns // 2 + 0.5) / columns
    centre_sin = jnp.broadcast_to(-0.9 + 1.8 * (band + centre_lat) / N_LAT, (N_LAT, N_LON, 1))
    centre_long = jnp.broadcast_to(2.0 * math.pi * (sector + centre_lon) / N_LON, (N_LAT, N_LON, 1))
    centre_cos = jnp.sqrt(1.0 - centre_sin * centre_sin)
    centre = [centre_cos * jnp.cos(centre_long), centre_cos * jnp.sin(centre_long), centre_sin]
    north = [-centre_sin * jnp.cos(centre_long), -centre_sin * jnp.sin(centre_long), centre_cos]
    east = [-jnp.sin(centre_long), jnp.cos(centre_long), jnp.zeros_like(centre_long)]
    angle = 2.0 * math.pi * jax.random.uniform(key_angle, shape, jnp.float32)
    chord = (1.805 + 0.01 * jax.random.uniform(key_radius, shape, jnp.float32)) * 0.3 / N_LAT
    theta = 2.0 * jnp.arcsin(0.5 * chord)
    cycle_parts = []
    for comp in range(3):
        cycle_parts.append(jnp.cos(theta) * centre[comp] + jnp.sin(theta) * (jnp.cos(angle) * north[comp] + jnp.sin(angle) * east[comp]))
    cycle_pos = jnp.stack(cycle_parts, axis=2)
    on_cycle = (jnp.arange(OBS_DEV, dtype=jnp.int32) % 2 == 0)[None, None, None, :]
    return jnp.where(on_cycle, cycle_pos, spread_pos).astype(jnp.float32)


def draw_innovation(key, part):
    key = jax.random.fold_in(key, 13)
    key_mean, key_noise = jax.random.split(key)
    shape = (N_LAT, N_LON, 3, OBS_DEV)
    band = jnp.arange(N_LAT, dtype=jnp.float32)[:, None, None, None]
    sector = jnp.arange(N_LON, dtype=jnp.float32)[None, :, None, None]
    region_scale = 0.5 + (band + sector) / (N_LAT + N_LON - 2)
    level = jax.random.uniform(key_mean, (3,), jnp.float32, 2.0, 2.5)[None, None, :, None]
    noise = 0.8 * jax.random.normal(key_noise, shape, jnp.float32)
    return jnp.clip(region_scale * level + noise, -6.0, 6.0).astype(jnp.float32)


def draw_channel_corr(key, part):
    key = jax.random.fold_in(key, 7)
    offdiag = jax.random.uniform(key, (3,), jnp.float32, 0.3, 0.7)
    row_zero = jnp.stack([jnp.float32(1.0), offdiag[0], offdiag[1]])
    row_one = jnp.stack([offdiag[0], jnp.float32(1.0), offdiag[2]])
    row_two = jnp.stack([offdiag[1], offdiag[2], jnp.float32(1.0)])
    return jnp.stack([row_zero, row_one, row_two]).astype(jnp.float32)


def level_of(rng, extent, cuts, smallest, top_value):
    gain = 1.0
    for dim, shards_of in cuts:
        draws = jax.random.uniform(jax.random.fold_in(jax.random.fold_in(rng, 6), dim), (shards_of,), jnp.float32, smallest / len(cuts), top_value / len(cuts))
        gain = gain * jnp.repeat(jnp.exp(draws), extent[dim] // shards_of).reshape((-1,) + (1,) * (len(extent) - 1 - dim))
    return gain


def setup_inputs(seed: int = 0) -> dict:
    key_list = jax.random.split(jax.random.key(seed), 8)
    return {
        "tile_counts": draw_tile_counts(jax.random.fold_in(key_list[7], 71), 0),
        "obs_pos": draw_obs_pos(jax.random.fold_in(key_list[7], 71), 0),
        "innovation": draw_innovation(jax.random.fold_in(key_list[7], 71), 0),
        "bg_std_obs": jnp.clip(jnp.exp(math.log(0.2) - 1.3862944 * jax.random.uniform(key_list[3], (N_LAT, N_LON, 3, OBS_DEV), jnp.float32) ** level_of(key_list[3], (N_LAT, N_LON, 3, OBS_DEV), ((0, 16), (1, 16)), -0.2, 0.2)), 0.05, 0.2),
        "obs_std": jnp.clip(jnp.exp(math.log(1.0) - 1.2039728 * jax.random.uniform(key_list[4], (N_LAT, N_LON, 3, OBS_DEV), jnp.float32) ** level_of(key_list[4], (N_LAT, N_LON, 3, OBS_DEV), ((0, 16), (1, 16)), -0.2, 0.2)), 0.3, 1.0),
        "channel_corr": draw_channel_corr(jax.random.fold_in(key_list[7], 71), 0),
        "bg_std_grid": jnp.clip(jnp.exp(math.log(0.2) - 1.3862944 * jax.random.uniform(key_list[6], (N_LAT, N_LON, 3, GRID_DEV), jnp.float32) ** level_of(key_list[6], (N_LAT, N_LON, 3, GRID_DEV), ((0, 16), (1, 16)), -0.2, 0.2)), 0.05, 0.2),
    }


def sphere_point(frac_lat, frac_lon):
    band = jnp.arange(N_LAT, dtype=jnp.float32)[:, None, None]
    sector = jnp.arange(N_LON, dtype=jnp.float32)[None, :, None]
    sinlat = -0.9 + 1.8 * (band + frac_lat) / N_LAT
    longitude = 2.0 * math.pi * (sector + frac_lon) / N_LON
    full_shape = (N_LAT, N_LON, longitude.shape[2])
    sinlat = jnp.broadcast_to(sinlat, full_shape)
    longitude = jnp.broadcast_to(longitude, full_shape)
    coslat = jnp.sqrt(1.0 - sinlat * sinlat)
    return jnp.stack([coslat * jnp.cos(longitude), coslat * jnp.sin(longitude), sinlat], axis=2)

def gaspari(dist2, half):
    z = jnp.sqrt(dist2) / half
    inner = (((-0.25 * z + 0.5) * z + 0.625) * z - 5.0 / 3.0) * z * z + 1.0
    safe = jnp.maximum(z, 1.0)
    outer = ((((z / 12.0 - 0.5) * z + 0.625) * z + 5.0 / 3.0) * z - 5.0) * z + 4.0 - 2.0 / (3.0 * safe)
    return jnp.where(z <= 1.0, inner, jnp.where(z < 2.0, outer, 0.0))

def correlate(target_pos, near_pos, near_val, half):
    shifts = [(a, b) for a in (-1, 0, 1) for b in (-1, 0, 1)]
    stacked_pos = jnp.stack([jnp.roll(near_pos, s, axis=(0, 1)) for s in shifts], axis=2)
    stacked_val = jnp.stack([jnp.roll(near_val, s, axis=(0, 1)) for s in shifts], axis=2)
    regions = N_LAT * N_LON
    targets = target_pos.reshape(regions, 3, target_pos.shape[3])
    npos = stacked_pos.reshape(regions, 9, 3, near_pos.shape[3])
    nval = stacked_val.reshape(regions, 9, 3, near_pos.shape[3])

    def one_region(items):
        tpos, ppos, pval = items

        def step(acc, k):
            dist2 = jnp.zeros((tpos.shape[1], ppos.shape[2]), jnp.float32)
            for comp in range(3):
                delta = tpos[comp][:, None] - ppos[k, comp][None, :]
                dist2 = dist2 + delta * delta
            rho = gaspari(dist2, half)
            return (acc + jnp.einsum('cj,ij->ci', pval[k], rho, precision=lax.Precision.HIGHEST), None)
        acc, _ = lax.scan(step, jnp.zeros((3, tpos.shape[1]), jnp.float32), jnp.arange(9, dtype=jnp.int32))
        return acc
    out = lax.map(one_region, (targets, npos, nval))
    return out.reshape(N_LAT, N_LON, 3, target_pos.shape[3])

def reference(tile_counts, obs_pos, innovation, bg_std_obs, obs_std, channel_corr, bg_std_grid):
    half = 0.3 / N_LAT
    slot = jnp.arange(OBS_DEV, dtype=jnp.int32)
    live = (slot[None, None, :] < tile_counts[:, :, None] * OBS_TILE).astype(jnp.float32)[:, :, None, :]
    variance = obs_std * obs_std

    def operate(field):
        acc = correlate(obs_pos, obs_pos, bg_std_obs * field, half)
        mixed = jnp.einsum('ab,xybi->xyai', channel_corr, acc, precision=lax.Precision.HIGHEST)
        return live * (bg_std_obs * mixed + variance * field)
    weights = jnp.zeros_like(innovation)
    residual = live * innovation
    direction = residual
    norm_now = jnp.sum(residual * residual)
    for step in range(ITERS):
        image = operate(direction)
        alpha = norm_now / jnp.sum(direction * image)
        weights = weights + alpha * direction
        residual = residual - alpha * image
        norm_next = jnp.sum(residual * residual)
        direction = residual + norm_next / norm_now * direction
        norm_now = norm_next
    columns = GRID_DEV // GRID_ROWS
    cell = jnp.arange(GRID_DEV, dtype=jnp.int32)
    frac_lat = ((cell // columns).astype(jnp.float32) + 0.5) / GRID_ROWS
    frac_lon = ((cell % columns).astype(jnp.float32) + 0.5) / columns
    grid_pos = sphere_point(frac_lat[None, None, :], frac_lon[None, None, :])
    acc = correlate(grid_pos, obs_pos, bg_std_obs * weights, half)
    increment = bg_std_grid * jnp.einsum('ab,xybi->xyai', channel_corr, acc, precision=lax.Precision.HIGHEST)
    return (weights, increment)
```

```python
import math

import jax
import jax.numpy as jnp
import numpy as np
from jax import lax
from jax.experimental import pallas as pl
from jax.experimental.pallas import tpu as pltpu
from jax.sharding import PartitionSpec as P

OBS_TILE = 512
GRID_ROWS = 16
BLK = 128
SHIFT = 0.5
FAR = 64.0
NT = (((1,), (1,)), ((), ()))
NN = (((1,), (0,)), ((), ()))
F32 = jnp.float32
BF16 = jnp.bfloat16
VLIM = 48 * 1024 * 1024


def split3(x):
    hi = x.astype(BF16)
    rest = x - hi.astype(F32)
    mid = rest.astype(BF16)
    low = (rest - mid.astype(F32)).astype(BF16)
    return jnp.concatenate([hi, mid, low], axis=0)


def col_of(row):
    return jnp.transpose(jnp.broadcast_to(row, (8, row.shape[1])))[:, 0:1]


def rank_of(key, slots):
    col = col_of(key)
    parts = []
    for j in range(slots // BLK):
        kj = key[:, j * BLK : (j + 1) * BLK]
        total = jnp.zeros((8, BLK), F32)
        for i in range(slots // BLK):
            ki = jnp.broadcast_to(col[i * BLK : (i + 1) * BLK, :], (BLK, BLK))
            if i < j:
                before = ki <= kj
            elif i > j:
                before = ki < kj
            else:
                first = lax.broadcasted_iota(jnp.int32, (BLK, BLK), 0) < lax.broadcasted_iota(
                    jnp.int32, (BLK, BLK), 1
                )
                before = (ki < kj) | ((ki == kj) & first)
            ones = jnp.where(before, 1.0, 0.0).astype(F32)
            total = total + jnp.sum(ones.reshape(BLK // 8, 8, BLK), axis=0)
        parts.append(jnp.sum(total, axis=0, keepdims=True))
    return jnp.concatenate(parts, axis=1)


def onehot_of(rank, slots):
    place = lax.broadcasted_iota(jnp.int32, (slots, slots), 0).astype(F32)
    return jnp.where(place == rank, 1.0, 0.0).astype(BF16)


def sort_kernel(count, frame, pos, innov, bg, std, hb_out, own_out, rank_out):
    slots = pos.shape[3]
    live_n = count[0, 0] * OBS_TILE
    lane = lax.broadcasted_iota(jnp.int32, (1, slots), 1)
    live = lane < live_n
    px, py, pz = pos[0, 0, 0:1, :], pos[0, 0, 1:2, :], pos[0, 0, 2:3, :]
    key = jnp.where(live, pz, 10.0)
    first = rank_of(key, slots)
    strip = jnp.where(first * 2.0 >= live_n.astype(F32), 8.0, 0.0)
    east = frame[0:1, 0:1] * px + frame[0:1, 1:2] * py
    east = east * lax.rsqrt(jnp.maximum(1.0 - pz * pz, 1e-6)) * (0.3 / 16)
    rank = rank_of(jnp.where(live, strip + east, 100.0), slots)
    rank_out[...] = rank
    maskf = jnp.where(live, 1.0, 0.0).astype(F32)
    where3 = jnp.where(live, pos[0, 0], FAR)
    dev = bg[0, 0] * maskf
    start = innov[0, 0] * maskf
    var = std[0, 0] * std[0, 0] * maskf
    pad = jnp.zeros((4, slots), F32)
    vals = jnp.concatenate([where3, dev, start, var, pad], axis=0)
    got = lax.dot_general(split3(vals), onehot_of(rank, slots), NT, preferred_element_type=F32)
    got = got[0:16] + got[16:32] + got[32:48]
    dev, start = got[3:6], got[6:9]
    own_out[...] = got
    hb_out[...] = jnp.concatenate([dev * start, got[0:3], pad[0:2]], axis=0)


def rho_of(tcol, sx, sy, sz):
    dx, dy, dz = tcol[0] - sx, tcol[1] - sy, tcol[2] - sz
    s = dx * dx + dy * dy + dz * dz
    r = lax.rsqrt(jnp.maximum(s, 1e-30))
    z = s * r
    inner = s * (((-0.25 * z + 0.5) * z + 0.625) * z - 5.0 / 3.0) + 1.0
    t = jnp.maximum(2.0 - z, 0.0)
    t = t * t
    u = z + 1.0
    outer = (t * t) * (u * u * (1.0 / 12.0) - 0.125) * r
    return jnp.where(s <= 1.0, inner, outer)


def to_frame(tile, row, frame):
    q = None
    for k in range(3):
        term = frame[:, k : k + 1] * (tile[row + k : row + k + 1, :] - frame[:, 3 + k : 4 + k])
        q = term if q is None else q + term
    return q


def boxes(tile):
    return jnp.min(tile, axis=1, keepdims=True), jnp.max(tile, axis=1, keepdims=True)


def correlate(halo, fields, frame, target_tiles, q_ref, v_ref, tcol, pair, mask_v, mask_s, sem, acc):
    nt = len(target_tiles)
    per = halo[0].shape[2] // BLK
    nf = len(fields)
    lane = lax.broadcasted_iota(jnp.int32, (8, BLK), 1)
    low = jnp.full((8, BLK), 1e6, F32)
    high = jnp.full((8, BLK), 1e6, F32)
    for c in range(3):
        for a in range(3):
            r = c * 3 + a
            q = to_frame(halo[c][a], 3, frame)
            for b in range(per):
                tile = q[:, b * BLK : (b + 1) * BLK]
                q_ref[r * per + b] = tile
                lo, hi = boxes(tile)
                low = jnp.where(lane == r * per + b, lo, low)
                high = jnp.where(lane == r * per + b, hi, high)
            for f in range(nf):
                for b in range(per):
                    v = split3(fields[f][c][a, :, b * BLK : (b + 1) * BLK])
                    v = jnp.concatenate([v, jnp.zeros((8, BLK), BF16)], axis=0)
                    v_ref[r * per + b, 32 * f : 32 * f + 32, 0:BLK] = v
                    v_ref[r * per + b, 32 * f : 32 * f + 32, BLK : 2 * BLK] = v
    bits = jnp.zeros((1, BLK), jnp.int32)
    for t in range(nt):
        tile = target_tiles[t]
        lo, hi = boxes(tile)
        gap = jnp.maximum(jnp.maximum(lo - high, low - hi), 0.0)
        gap2 = jnp.sum(gap * gap, axis=0, keepdims=True)
        far = jnp.sum(lo * lo, axis=0, keepdims=True)
        bits = bits + jnp.where((gap2 < 4.001) & (far < 1e6), 1 << t, 0)
        turned = jnp.transpose(tile)
        for k in range(3):
            tcol[t, k] = jnp.broadcast_to(turned[:, k : k + 1], (BLK, BLK))
        acc[t] = jnp.zeros(acc.shape[1:], F32)
    mask_v[...] = jnp.broadcast_to(bits, (8, BLK))
    copy = pltpu.make_async_copy(mask_v, mask_s, sem)
    copy.start()
    copy.wait()

    def source(n, _):
        word = mask_s[0, n]

        @pl.when(word != 0)
        def _():
            def target(t, _):
                @pl.when(((word >> t) & 1) != 0)
                def _():
                    q = q_ref[n]
                    sx, sy, sz = q[0:1], q[1:2], q[2:3]
                    for i in range(0, BLK, 32):
                        rho = rho_of([tcol[t, k, i : i + 32] for k in range(3)], sx, sy, sz)
                        hi = rho.astype(BF16)
                        pair[i : i + 32, 0:BLK] = hi
                        pair[i : i + 32, BLK : 2 * BLK] = (rho - hi.astype(F32)).astype(BF16)
                    out = lax.dot_general(v_ref[n], pair[...], NT, preferred_element_type=F32)
                    for f in range(nf):
                        o = out[32 * f : 32 * f + 32]
                        acc[t, f] += o[0:8] + o[8:16] + o[16:24]

                return 0

            lax.fori_loop(0, nt, target, 0)

        return 0

    lax.fori_loop(0, 9 * per, source, 0)


def mix(corr, acc):
    return jnp.concatenate(
        [
            corr[c, 0] * acc[0:1] + corr[c, 1] * acc[1:2] + corr[c, 2] * acc[2:3]
            for c in range(3)
        ],
        axis=0,
    )


def operate(refs, acc, own, corr, field):
    total = jnp.concatenate([acc[t, 0] for t in range(acc.shape[0])], axis=1)
    dev, var = own[3:6], own[9:12]
    return dev * mix(corr, total) + var * field


def apply_kernel(corr, frame, hm, hw, he, um, uw, ue, own, field, u_out, img_out, nxt_out, *scratch):
    q_ref, v_ref, tcol, pair, mask_v, mask_s, sem, acc = scratch
    frame = frame[...]
    per = hm.shape[2] // BLK
    q = to_frame(hm[1], 3, frame)
    targets = [q[:, t * BLK : (t + 1) * BLK] for t in range(per)]
    correlate((hm, hw, he), [(um, uw, ue)], frame, targets, *scratch)
    mine = own[...]
    image = operate(None, acc, mine, corr, field[...])
    nxt = image - SHIFT * field[...]
    img_out[...] = image
    nxt_out[...] = nxt
    u_out[...] = jnp.concatenate([mine[3:6] * nxt, jnp.zeros((5, nxt.shape[1]), F32)], axis=0)


def gram_kernel(b0, b1, b2, a0, a1, a2, out):
    pairs = [(b0, a0), (b0, a1), (b0, a2), (b1, a1), (b1, a2), (b2, a2), (b0, b0), (b1, b0), (b2, b0)]
    lane = lax.broadcasted_iota(jnp.int32, (1, BLK), 1)
    row = jnp.zeros((1, BLK), F32)
    for k, (x, y) in enumerate(pairs):
        prod = x[...] * y[...]
        total = jnp.sum(jnp.sum(prod, axis=0, keepdims=True), axis=1, keepdims=True)
        row = jnp.where(lane == k, total, row)
    out[...] = row


def grid_kernel(corr, frame, gpos, hm, hw, he, um, uw, ue, xm, xw, xe, bgg, rank, b1, b2, g_out, w_out, *scratch):
    acc = scratch[-1]
    frame = frame[...]
    nt = gpos.shape[1] // BLK
    q = to_frame(gpos[...], 0, frame)
    targets = [q[:, t * BLK : (t + 1) * BLK] for t in range(nt)]
    correlate(
        (hm, hw, he), [(hm, hw, he), (um, uw, ue), (xm, xw, xe)], frame, targets, *scratch
    )
    for f in range(3):
        total = jnp.concatenate([acc[t, f] for t in range(nt)], axis=1)
        g_out[f] = bgg[0, 0] * mix(corr, total)
    slots = rank.shape[1]
    vals = jnp.concatenate([b1[...], b2[...], jnp.zeros((10, slots), F32)], axis=0)
    back = lax.dot_general(split3(vals), onehot_of(rank[...], slots), NN, preferred_element_type=F32)
    back = back[0:16] + back[16:32] + back[32:48]
    w_out[0] = back[0:3]
    w_out[1] = back[3:6]


def final_kernel(count, parts, innov, w, g, w_out, g_out):
    sums = jnp.sum(parts[...], axis=0, keepdims=True)
    lane = lax.broadcasted_iota(jnp.int32, sums.shape, 1)
    m00, m01, m02, m11, m12, m22, g0, g1, g2 = [
        jnp.sum(jnp.where(lane == k, sums, 0.0), axis=1, keepdims=True) for k in range(9)
    ]
    l10, l20 = m01 / m00, m02 / m00
    d1 = m11 - l10 * m01
    e12 = m12 - l10 * m02
    ok1 = d1 > 1e-6 * m11
    safe1 = jnp.where(ok1, d1, 1.0)
    l21 = jnp.where(ok1, e12 / safe1, 0.0)
    d2 = m22 - l20 * m02 - l21 * e12
    ok2 = ok1 & (d2 > 1e-6 * m22)
    y1 = g1 - l10 * g0
    y2 = g2 - l20 * g0 - l21 * y1
    c2 = jnp.where(ok2, y2 / jnp.where(ok2, d2, 1.0), 0.0)
    c1 = jnp.where(ok1, y1 / safe1, 0.0) - l21 * c2
    c0 = g0 / m00 - l10 * c1 - l20 * c2
    slots = innov.shape[3]
    live = lax.broadcasted_iota(jnp.int32, (1, slots), 1) < count[0, 0] * OBS_TILE
    w_out[0, 0] = c0 * jnp.where(live, innov[0, 0], 0.0) + c1 * w[0] + c2 * w[1]
    g_out[0, 0] = c0 * g[0] + c1 * g[1] + c2 * g[2]


def spread_halo(block):
    nl, nn = lax.axis_size("lat"), lax.axis_size("lon")

    def ring(x, axis, count, step):
        return lax.ppermute(x, axis, [(i, (i + step) % count) for i in range(count)])

    mid = jnp.stack([ring(block, "lat", nl, 1), block, ring(block, "lat", nl, -1)])
    return mid, ring(mid, "lon", nn, 1), ring(mid, "lon", nn, -1)


def frames(bands, sectors):
    table = np.zeros((bands, sectors, 8, 8), np.float64)
    half = 0.3 / bands
    for i in range(bands):
        s = -0.9 + 1.8 * (i + 0.5) / bands
        c = math.sqrt(1.0 - s * s)
        for j in range(sectors):
            lam = 2.0 * math.pi * (j + 0.5) / sectors
            cl, sl = math.cos(lam), math.sin(lam)
            table[i, j, :3, :3] = np.array([[-sl, cl, 0.0], [-s * cl, -s * sl, c], [c * cl, c * sl, s]]) / half
            table[i, j, :, 3:6] = [c * cl, c * sl, s]
    return table.astype(np.float32)


def scratch_for(nt, nf, sources):
    return [
        pltpu.VMEM((sources, 8, BLK), F32),
        pltpu.VMEM((sources, 32 * nf, 2 * BLK), BF16),
        pltpu.VMEM((nt, 3, BLK, BLK), F32),
        pltpu.VMEM((BLK, 2 * BLK), BF16),
        pltpu.VMEM((8, BLK), jnp.int32),
        pltpu.SMEM((8, BLK), jnp.int32),
        pltpu.SemaphoreType.DMA,
        pltpu.VMEM((nt, nf, 8, BLK), F32),
    ]


VM = pl.BlockSpec(memory_space=pltpu.VMEM)
SM = pl.BlockSpec(memory_space=pltpu.SMEM)


def call(kernel, name, ins, outs, scratch, flops):
    return pl.pallas_call(
        kernel,
        out_shape=[jax.ShapeDtypeStruct(s, F32) for s in outs],
        in_specs=ins,
        out_specs=[VM] * len(outs),
        scratch_shapes=scratch,
        name=name,
        compiler_params=pltpu.CompilerParams(vmem_limit_bytes=VLIM),
        cost_estimate=pl.CostEstimate(flops=flops, bytes_accessed=1 << 20, transcendentals=0),
    )


def per_device(tile_counts, obs_pos, innovation, bg_std_obs, obs_std, channel_corr, bg_std_grid):
    bands, sectors = lax.axis_size("lat"), lax.axis_size("lon")
    band, sector = lax.axis_index("lat"), lax.axis_index("lon")
    slots = obs_pos.shape[3]
    cells = bg_std_grid.shape[3]
    sources = 9 * slots // BLK
    frame = lax.dynamic_slice(
        jnp.asarray(frames(bands, sectors)), (band, sector, 0, 0), (1, 1, 8, 8)
    ).reshape(8, 8)

    hb, own, rank = call(
        sort_kernel, "sort", [SM] + [VM] * 5, [(8, slots), (16, slots), (1, slots)], [], 10**8
    )(tile_counts, frame, obs_pos, innovation, bg_std_obs, obs_std)
    near = spread_halo(hb)
    apply = call(
        apply_kernel,
        "apply",
        [SM] + [VM] * 9,
        [(8, slots), (3, slots), (3, slots)],
        scratch_for(slots // BLK, 1, sources),
        10**9,
    )
    b0 = own[6:9]
    u1, a0, b1 = apply(channel_corr, frame, *near, *near, own, b0)
    near1 = spread_halo(u1)
    u2, a1, b2 = apply(channel_corr, frame, *near, *near1, own, b1)
    near2 = spread_halo(u2)
    _, a2, _ = apply(channel_corr, frame, *near, *near2, own, b2)
    (sums,) = call(gram_kernel, "gram", [VM] * 6, [(1, BLK)], [], 10**6)(b0, b1, b2, a0, a1, a2)
    copies = jnp.broadcast_to(sums[:, :16], (bands * sectors, 16))
    parts = lax.all_to_all(copies, ("lat", "lon"), 0, 0, tiled=True)

    columns = cells // GRID_ROWS
    cell = jnp.arange(cells, dtype=jnp.int32)
    frac_lat = ((cell // columns).astype(F32) + 0.5) / GRID_ROWS
    frac_lon = ((cell % columns).astype(F32) + 0.5) / columns
    sinlat = -0.9 + 1.8 * (band.astype(F32) + frac_lat) / bands
    longitude = 2.0 * math.pi * (sector.astype(F32) + frac_lon) / sectors
    coslat = jnp.sqrt(1.0 - sinlat * sinlat)
    grid_pos = jnp.stack([coslat * jnp.cos(longitude), coslat * jnp.sin(longitude), sinlat], axis=0)
    parts_g, parts_w = call(
        grid_kernel,
        "grid",
        [SM] + [VM] * 15,
        [(3, 3, cells), (2, 3, slots)],
        scratch_for(cells // BLK, 3, sources),
        10**9,
    )(channel_corr, frame, grid_pos, *near, *near1, *near2, bg_std_grid, rank, b1, b2)
    return tuple(
        call(
            final_kernel,
            "final",
            [SM] + [VM] * 4,
            [(1, 1, 3, slots), (1, 1, 3, cells)],
            [],
            10**6,
        )(tile_counts, parts, innovation, parts_w, parts_g)
    )


def solution(mesh):
    spec = P("lat", "lon", None, None)
    return jax.shard_map(
        per_device,
        mesh=mesh,
        in_specs=(P("lat", "lon"), spec, spec, spec, spec, P(), spec),
        out_specs=(spec, spec),
        check_vma=False,
    )
```

```python
import functools
import math

import jax
import jax.numpy as jnp
import numpy as np
from jax import lax
from jax.experimental import pallas as pl
from jax.experimental.pallas import tpu as pltpu
from jax.sharding import PartitionSpec as P

OBS_TILE = 512
GRID_ROWS = 16
BLK = 128
SHIFT = 0.5
FAR = 64.0
NT = (((1,), (1,)), ((), ()))
NN = (((1,), (0,)), ((), ()))
F32 = jnp.float32
BF16 = jnp.bfloat16
VLIM = 8 * 1024 * 1024
UNROLL = 8
ROWS = 32
GROUP = 4
KEPT = 96
CELLS = 512


def split3(x):
    hi = x.astype(BF16)
    rest = x - hi.astype(F32)
    mid = rest.astype(BF16)
    low = (rest - mid.astype(F32)).astype(BF16)
    return jnp.concatenate([hi, mid, low], axis=0)


def col_of(row):
    return jnp.transpose(jnp.broadcast_to(row, (8, row.shape[1])))[:, 0:1]


def rank_of(key, slots):
    col = col_of(key)
    parts = []
    for j in range(slots // BLK):
        kj = key[:, j * BLK : (j + 1) * BLK]
        total = jnp.zeros((8, BLK), F32)
        for i in range(slots // BLK):
            ki = jnp.broadcast_to(col[i * BLK : (i + 1) * BLK, :], (BLK, BLK))
            if i < j:
                before = ki <= kj
            elif i > j:
                before = ki < kj
            else:
                first = lax.broadcasted_iota(jnp.int32, (BLK, BLK), 0) < lax.broadcasted_iota(
                    jnp.int32, (BLK, BLK), 1
                )
                before = (ki < kj) | ((ki == kj) & first)
            ones = jnp.where(before, 1.0, 0.0).astype(F32)
            total = total + jnp.sum(ones.reshape(BLK // 8, 8, BLK), axis=0)
        parts.append(jnp.sum(total, axis=0, keepdims=True))
    return jnp.concatenate(parts, axis=1)


def onehot_of(rank, slots):
    place = lax.broadcasted_iota(jnp.int32, (slots, slots), 0).astype(F32)
    return jnp.where(place == rank, 1.0, 0.0).astype(BF16)


def angle_of(x):
    x2 = x * x
    return x * (1.0 + x2 * (1.0 / 6.0 + x2 * (3.0 / 40.0 + x2 * (15.0 / 336.0))))


def sort_kernel(
    count, table, pos_in, innov_in, bg_in, std_in,
    hb_out, dev_out, var_out, b0_out, rank_out, frame_out, bounds_out,
    pos, innov, bg, std, sems,
):
    bands, sectors = lax.axis_size("lat"), lax.axis_size("lon")
    band, sector = lax.axis_index("lat"), lax.axis_index("lon")
    pairs = [
        (table.at[band, sector], frame_out),
        (pos_in, pos),
        (innov_in, innov),
        (bg_in, bg),
        (std_in, std),
    ]
    copies = [pltpu.make_async_copy(x, y, sems.at[k]) for k, (x, y) in enumerate(pairs)]
    for copy in copies:
        copy.start()
    for copy in copies:
        copy.wait()

    def rows(ref):
        return jnp.concatenate([ref[0], ref[1], ref[2]], axis=0)

    slots = pos.shape[2]
    per = slots // BLK
    frame = frame_out[...]
    live_n = count[0, 0] * OBS_TILE
    lane = lax.broadcasted_iota(jnp.int32, (1, slots), 1)
    live = lane < live_n
    px, py, pz = pos[0], pos[1], pos[2]
    key = jnp.where(live, pz, 10.0)
    first = rank_of(key, slots)
    strip = jnp.where(first * 2.0 >= live_n.astype(F32), 8.0, 0.0)
    east = frame[2:3, 6:7] * px + frame[3:4, 6:7] * py
    sine = east * lax.rsqrt(jnp.maximum(px * px + py * py, 1e-6))
    rank = rank_of(jnp.where(live, strip + sine, 100.0), slots)
    rank_out[...] = rank
    maskf = jnp.where(live, 1.0, 0.0).astype(F32)
    where3 = jnp.where(live, rows(pos), FAR)
    dev = rows(bg) * maskf
    start = rows(innov) * maskf
    var = rows(std)
    var = var * var * maskf
    sine = jnp.where(live, sine, 0.0)
    vals = jnp.concatenate([where3, dev, start, var, sine, jnp.zeros((3, slots), F32)], axis=0)
    got = lax.dot_general(split3(vals), onehot_of(rank, slots), NT, preferred_element_type=F32)
    got = got[0:16] + got[16:32] + got[32:48]
    dev, start = got[3:6], got[6:9]
    dev_out[...] = dev
    b0_out[...] = start
    var_out[...] = got[9:12]

    z = jnp.concatenate(blocks(got[2:3]), axis=0)
    angle = angle_of(jnp.concatenate(blocks(got[12:13]), axis=0))
    bounds = [
        jnp.min(z, axis=1, keepdims=True),
        jnp.max(z, axis=1, keepdims=True),
        jnp.min(angle, axis=1, keepdims=True),
        jnp.max(angle, axis=1, keepdims=True),
    ]
    sub = lax.broadcasted_iota(jnp.int32, (per, BLK), 0)
    col = lax.broadcasted_iota(jnp.int32, (per, BLK), 1)

    def spread(x, index):
        return jnp.sum(jnp.where(sub == index, x, 0.0), axis=0, keepdims=True)

    as_source = [spread(x, col & 7) for x in bounds]
    pad = jnp.zeros((1, slots - 4 * BLK), F32)
    hb_out[...] = jnp.concatenate(
        [dev * start, got[0:3], jnp.concatenate(as_source + [pad], axis=1), jnp.zeros((1, slots), F32)],
        axis=0,
    )
    as_target = [spread(x, col >> 3) for x in bounds]
    lane = lax.broadcasted_iota(jnp.int32, (1, BLK), 1)
    t = ((lane - 64) >> 3).astype(F32)
    tall = 1.0 * BLK * GRID_ROWS / CELLS
    floor = -0.9 + 1.8 * band.astype(F32) / bands
    step = 1.8 / bands / GRID_ROWS
    half_width = math.pi / sectors
    grid = [
        floor + step * (t * tall + 0.25),
        floor + step * (t * tall + tall - 0.25),
        jnp.full((1, BLK), -half_width, F32),
        jnp.full((1, BLK), half_width, F32),
    ]
    grid_end = 64 + 8 * (CELLS // BLK)
    rows = [
        jnp.where(lane < 64, x, jnp.where(lane < grid_end, g, 100.0)) for x, g in zip(as_target, grid)
    ]
    bounds_out[...] = jnp.concatenate(rows + [jnp.zeros((4, BLK), F32)], axis=0)


def blocks(wide):
    return [wide[:, b * BLK : (b + 1) * BLK] for b in range(wide.shape[1] // BLK)]


def active_words(source, target, bands):
    slo, shi, wlo, whi = source
    tlo, thi, vlo, vhi = target

    def radius(z):
        return jnp.sqrt(jnp.maximum(1.0 - z * z, 0.0))

    below, above = jnp.minimum(shi, thi), jnp.maximum(slo, tlo)
    fall = radius(below) - radius(above)
    apart = above - below
    lat = jnp.where(apart > 0.0, apart * apart + fall * fall, 0.0)
    gap = jnp.maximum(jnp.maximum(wlo, vlo) - jnp.minimum(whi, vhi), 0.0)
    gap2 = gap * gap
    small = radius(jnp.maximum(jnp.abs(slo), jnp.abs(shi))) * radius(
        jnp.maximum(jnp.abs(tlo), jnp.abs(thi))
    )
    bound = lat + gap2 * (1.0 - gap2 * (1.0 / 12.0)) * small
    reach = (0.6 / bands) ** 2
    lane = lax.broadcasted_iota(jnp.int32, bound.shape, 1)
    active = (bound < reach * 1.002 + 1e-6) & (tlo < 50.0)
    word = jnp.where(active, jnp.left_shift(jnp.full(lane.shape, 1, jnp.int32), (lane >> 3) & 7), 0)
    for shift in (8, 16, 32):
        word = word + pltpu.roll(word, BLK - shift, 1)
    return word


def source_bounds(tiles, shifts):
    rows = []
    for k in range(4):
        parts = []
        for tile, shift in zip(tiles, shifts):
            row = tile[6:7, k * BLK : (k + 1) * BLK]
            parts.append(row + shift if k >= 2 else row)
        rows.append(jnp.concatenate(parts, axis=0))
    return rows


def to_smem(words, mask_v, mask_s, sem):
    mask_v[0 : words.shape[0], :] = words
    copy = pltpu.make_async_copy(mask_v, mask_s, sem)
    copy.start()
    copy.wait()


def list_pairs(mask_s, column, regions, first, pairs, count, below=False):
    def source(i, count):
        r, b = i >> 3, i & 7

        def take(state):
            word, k = state
            bit = word & -word
            pairs[0, k] = (first * 8 + i) * 8 + (31 - lax.clz(bit))
            return word ^ bit, k + 1

        word = mask_s[r, column + b]
        if below:
            word = word & (jnp.left_shift(1, b) - 1)
        return lax.while_loop(lambda state: state[0] != 0, take, (word, count))[1]

    return lax.fori_loop(0, 8 * regions, source, count)


def close_list(pairs, count):
    for k in range(UNROLL):
        pairs[0, count + k] = 0
    pairs[0, pairs.shape[1] - 1] = count


def rho_of(tcol, sx, sy, sz):
    dx, dy, dz = tcol[0] - sx, tcol[1] - sy, tcol[2] - sz
    s = dx * dx + dy * dy + dz * dz
    r = lax.rsqrt(jnp.maximum(s, 1e-30))
    z = s * r
    inner = s * (((-0.25 * z + 0.5) * z + 0.625) * z - 5.0 / 3.0) + 1.0
    t = jnp.maximum(2.0 - z, 0.0)
    t = t * t
    u = z + 1.0
    outer = (t * t) * (u * u * (1.0 / 12.0) - 0.125) * r
    return jnp.where(s <= 1.0, inner, outer)


def to_frame(tile, row, frame):
    q = None
    for k in range(3):
        term = frame[:, k : k + 1] * (tile[row + k : row + k + 1, :] - frame[:, 3 + k : 4 + k])
        q = term if q is None else q + term
    return q


def set_columns(targets, tcol):
    for t, tile in enumerate(targets):
        turned = jnp.transpose(tile)
        for k in range(3):
            tcol[t, k] = jnp.broadcast_to(turned[:, k : k + 1], (BLK, BLK))


def fill_rows(q, tcol, t, out):
    sx, sy, sz = q[0:1], q[1:2], q[2:3]
    for i in range(0, BLK, ROWS):
        rho = rho_of([tcol[t, k, i : i + ROWS] for k in range(3)], sx, sy, sz)
        hi = rho.astype(BF16)
        out[i : i + ROWS, 0:BLK] = hi
        out[i : i + ROWS, BLK : 2 * BLK] = (rho - hi.astype(F32)).astype(BF16)


def fill_pair(entry, q_ref, tcol, out):
    fill_rows(q_ref[entry >> 3], tcol, entry & 7, out)


def fill_cache(count, pairs, q_ref, tcol, cache, first):
    room = cache.shape[0] - UNROLL - first
    kept = jnp.minimum(count, room)

    def fill(p, _):
        fill_pair(pairs[0, p], q_ref, tcol, cache.at[first + p])
        return 0

    lax.fori_loop(0, kept, fill, 0)
    for k in range(UNROLL):
        cache[first + kept + k] = jnp.zeros(cache.shape[1:], BF16)


def parts_of(tile):
    hi = tile.astype(BF16).astype(F32)
    rest = tile - hi
    mid = rest.astype(BF16).astype(F32)
    return [hi, mid, rest - mid]


def set_values(tile, v_ref, first):
    v = jnp.concatenate(parts_of(tile) + [jnp.zeros(tile.shape, F32)], axis=0).astype(BF16)
    for b, part in enumerate(blocks(v)):
        v_ref[first + b, :, 0:BLK] = part
        v_ref[first + b, :, BLK : 2 * BLK] = part


def add_parts(out):
    return out[0:8] + out[8:16] + out[16:24]


def own_fill_kernel(frame, hb, bounds, q_out, tcol_out, pairs_out, cache_out, mask_v, mask_s, sem):
    tile = hb[...]
    tiles = blocks(to_frame(tile, 3, frame[...]))
    per = len(tiles)
    for b, part in enumerate(tiles):
        q_out[b] = part
    words = active_words(
        source_bounds([tile], [0.0]), [bounds[k : k + 1, :] for k in range(4)], lax.axis_size("lat")
    )
    mask_v[0:1, :] = words
    copy = pltpu.make_async_copy(mask_v, mask_s, sem)
    copy.start()
    set_columns(tiles, tcol_out)
    copy.wait()
    count = list_pairs(mask_s, 0, 1, 0, pairs_out, 0, below=True)
    close_list(pairs_out, count)

    def diagonal(b, _):
        fill_pair(b * 9, q_out, tcol_out, cache_out.at[b])
        return 0

    lax.fori_loop(0, per, diagonal, 0)
    fill_cache(count, pairs_out, q_out, tcol_out, cache_out, per)


def own_times_kernel(pairs, cache, u, acc, v_ref):
    set_values(u[...], v_ref, 0)
    per = acc.shape[0]
    for b in range(per):
        acc[b] = add_parts(lax.dot_general(v_ref[b], cache[b], NT, preferred_element_type=F32))
    count = pairs[0, pairs.shape[1] - 1]

    def group(i, _):
        outs = []
        for k in range(UNROLL // 2):
            p = i * (UNROLL // 2) + k
            n, t = pairs[0, p] >> 3, pairs[0, p] & 7
            rho = cache[per + p]
            ahead = lax.dot_general(v_ref[n], rho, NT, preferred_element_type=F32)
            back = lax.dot_general(v_ref[t, :, 0:BLK], rho, NN, preferred_element_type=F32)
            outs.append((ahead, back[:, 0:BLK] + back[:, BLK : 2 * BLK]))
        for k in range(UNROLL // 2):
            p = i * (UNROLL // 2) + k
            n, t = pairs[0, p] >> 3, pairs[0, p] & 7
            acc[t] += add_parts(outs[k][0])
            acc[n] += add_parts(outs[k][1])
        return 0

    half = UNROLL // 2
    lax.fori_loop(0, (count + half - 1) // half, group, 0)


OTHERS = [(0, 0), (0, 2), (1, 0), (1, 1), (1, 2), (2, 0), (2, 1), (2, 2)]


def near_fill_kernel(
    frame, bounds, tcol, hm, hw, he, q_out, pairs_out, cells_out, cache_out, mask_v, mask_s, sem
):
    halo = (hm, hw, he)
    per = hm.shape[2] // BLK
    turn = 2.0 * math.pi / lax.axis_size("lon")
    where = [(0, 1)] + OTHERS
    tiles = [halo[c][a] for c, a in where]
    words = active_words(
        source_bounds(tiles, [(0.0, -turn, turn)[c] for c, a in where]),
        [bounds[k : k + 1, :] for k in range(4)],
        lax.axis_size("lat"),
    )
    mask_v[0 : len(where), :] = words
    copy = pltpu.make_async_copy(mask_v, mask_s, sem)
    copy.start()
    turned = frame[...]
    for r in range(1, len(where)):
        for b, part in enumerate(blocks(to_frame(tiles[r], 3, turned))):
            q_out[(r - 1) * per + b] = part
    copy.wait()
    count = list_pairs(mask_s.at[1 : len(where)], 0, len(where) - 1, 0, pairs_out, 0)
    close_list(pairs_out, count)
    fill_cache(count, pairs_out, q_out, tcol, cache_out, 0)
    close_list(cells_out, list_pairs(mask_s, 64, len(where), 0, cells_out, 0))


def mix(corr, total):
    out = None
    for c in range(3):
        term = corr[:, c : c + 1] * total[c : c + 1, :]
        out = term if out is None else out + term
    return out


def near_times_kernel(
    pairs, corr, cache, q_ref, tcol, acc_own, um, uw, ue, dev, var, field,
    u_out, img_out, nxt_out, v_ref, acc, pair,
):
    halo = (um, uw, ue)
    per = acc.shape[0]
    for k, (c, a) in enumerate(OTHERS):
        set_values(halo[c][a], v_ref, k * per)
    acc[...] = acc_own[...]
    count = pairs[0, pairs.shape[1] - 1]
    kept = jnp.minimum(count, cache.shape[0] - UNROLL)

    def group(i, _):
        outs = []
        for k in range(UNROLL):
            p = i * UNROLL + k
            n = pairs[0, p] >> 3
            outs.append(lax.dot_general(v_ref[n], cache[p], NT, preferred_element_type=F32))
        for k in range(UNROLL):
            acc[pairs[0, i * UNROLL + k] & 7] += add_parts(outs[k])
        return 0

    lax.fori_loop(0, (kept + UNROLL - 1) // UNROLL, group, 0)

    def extra(p, _):
        entry = pairs[0, p]
        fill_pair(entry, q_ref, tcol, pair)
        out = lax.dot_general(v_ref[entry >> 3], pair[...], NT, preferred_element_type=F32)
        acc[entry & 7] += add_parts(out)
        return 0

    lax.fori_loop(kept, count, extra, 0)
    total = jnp.concatenate([acc[t] for t in range(per)], axis=1)
    field = field[...]
    dev = dev[...]
    image = dev * mix(corr, total) + var[...] * field
    nxt = image - SHIFT * field
    img_out[...] = image
    nxt_out[...] = nxt
    u_out[...] = jnp.concatenate([dev * nxt, jnp.zeros((5, nxt.shape[1]), F32)], axis=0)


def gram_kernel(b0, b1, b2, a0, a1, a2, out):
    pairs = [(b0, a0), (b0, a1), (b0, a2), (b1, a1), (b1, a2), (b2, a2), (b0, b0), (b1, b0), (b2, b0)]
    rows = []
    for x, y in pairs:
        prod = blocks(x[...] * y[...])
        while len(prod) > 1:
            prod = [prod[k] + prod[k + 1] for k in range(0, len(prod), 2)]
        rows.append(jnp.sum(prod[0], axis=0, keepdims=True))
    rows.append(jnp.zeros((16 - len(rows), BLK), F32))
    totals = jnp.sum(jnp.concatenate(rows, axis=0), axis=1, keepdims=True)
    sub = lax.broadcasted_iota(jnp.int32, (16, 16), 0)
    col = lax.broadcasted_iota(jnp.int32, (16, 16), 1)
    row = jnp.sum(jnp.where(sub == col, totals, 0.0), axis=0, keepdims=True)
    out[...] = jnp.broadcast_to(row[None], out.shape)


def pack_kernel(q_own, q_near, u0, u1, u2, *refs):
    out = refs[-1]
    fields = [refs[3 * f : 3 * f + 3] for f in range(3)]
    per = q_own.shape[0]
    for f, u in enumerate((u0, u1, u2)):
        for r, (c, a) in enumerate([(0, 1)] + OTHERS):
            tile = u[...] if r == 0 else fields[f][c][a]
            for b, part in enumerate(blocks(tile)):
                out[r * per + b, 3 * f : 3 * f + 3, :] = part[0:3]
    for b in range(per):
        out[b, 9:12, :] = q_own[b, 0:3, :]
    for n in range(q_near.shape[0]):
        out[per + n, 9:12, :] = q_near[n, 0:3, :]
    for n in range(out.shape[0]):
        out[n, 12:16, :] = jnp.zeros((4, BLK), F32)


def grid_kernel(pairs, corr, frame, packed, bgg, g_out, tcol, rho, acc):
    cells = g_out.shape[2]
    columns = cells // GRID_ROWS
    bands, sectors = lax.axis_size("lat"), lax.axis_size("lon")
    cell = lax.broadcasted_iota(jnp.int32, (8, cells), 1)
    row = lax.broadcasted_iota(jnp.int32, (8, cells), 0)
    frac_lat = ((cell // columns).astype(F32) + 0.5) / GRID_ROWS
    frac_lon = ((cell % columns).astype(F32) + 0.5) / columns
    band, sector = frame[0:1, 6:7], frame[1:2, 6:7]
    sinlat = -0.9 + 1.8 * (band + frac_lat) / bands
    longitude = 2.0 * math.pi * (sector + frac_lon) / sectors
    coslat = jnp.sqrt(1.0 - sinlat * sinlat)
    point = jnp.where(row == 0, coslat * jnp.cos(longitude), coslat * jnp.sin(longitude))
    point = jnp.where(row == 2, sinlat, point)
    set_columns(blocks(to_frame(point, 0, frame[...])), tcol)
    acc[...] = jnp.zeros(acc.shape, F32)
    count = pairs[0, pairs.shape[1] - 1]

    def group(i, _):
        outs = []
        for k in range(GROUP):
            p = i * GROUP + k
            entry = pairs[0, p]
            near = packed[entry >> 3]
            fill_rows(near[9:12], tcol, entry & 7, rho.at[k])
            near = near * jnp.where(p < count, 1.0, 0.0).astype(F32)
            v = jnp.concatenate(parts_of(near), axis=0).astype(BF16)
            v = jnp.concatenate([v, v], axis=1)
            outs.append(lax.dot_general(v, rho[k], NT, preferred_element_type=F32))
        for k in range(GROUP):
            out = outs[k]
            acc[pairs[0, i * GROUP + k] & 7] += out[0:16] + out[16:32] + out[32:48]
        return 0

    lax.fori_loop(0, (count + GROUP - 1) // GROUP, group, 0)
    total = jnp.concatenate([acc[t] for t in range(acc.shape[0])], axis=1)
    dev = jnp.concatenate([bgg[0], bgg[1], bgg[2]], axis=0)
    for f in range(3):
        g_out[f] = dev * mix(corr, total[3 * f : 3 * f + 3])


def unsort_kernel(rank, b1, b2, w_out):
    slots = rank.shape[1]
    vals = jnp.concatenate([b1[...], b2[...], jnp.zeros((10, slots), F32)], axis=0)
    back = lax.dot_general(split3(vals), onehot_of(rank[...], slots), NN, preferred_element_type=F32)
    back = back[0:16] + back[16:32] + back[32:48]
    w_out[0] = back[0:3]
    w_out[1] = back[3:6]


def final_kernel(count, parts, innov, w, g, w_out, g_out, w_buf, g_buf, sems):
    sums = parts[...]
    while sums.shape[0] > 1:
        half = sums.shape[0] // 2
        sums = sums[:half] + sums[half:]
    sums = sums[0]
    lane = lax.broadcasted_iota(jnp.int32, sums.shape, 1)
    m00, m01, m02, m11, m12, m22, g0, g1, g2 = [
        jnp.sum(jnp.where(lane == k, sums, 0.0), axis=1, keepdims=True) for k in range(9)
    ]
    l10, l20 = m01 / m00, m02 / m00
    d1 = m11 - l10 * m01
    e12 = m12 - l10 * m02
    ok1 = d1 > 1e-6 * m11
    safe1 = jnp.where(ok1, d1, 1.0)
    l21 = jnp.where(ok1, e12 / safe1, 0.0)
    d2 = m22 - l20 * m02 - l21 * e12
    ok2 = ok1 & (d2 > 1e-6 * m22)
    y1 = g1 - l10 * g0
    y2 = g2 - l20 * g0 - l21 * y1
    c2 = jnp.where(ok2, y2 / jnp.where(ok2, d2, 1.0), 0.0)
    c1 = jnp.where(ok1, y1 / safe1, 0.0) - l21 * c2
    c0 = g0 / m00 - l10 * c1 - l20 * c2
    slots = innov.shape[2]
    live = lax.broadcasted_iota(jnp.int32, (1, slots), 1) < count[0, 0] * OBS_TILE
    for k in range(3):
        first = jnp.where(live, innov[k], 0.0)
        w_buf[k] = c0 * first + c1 * w[0, k : k + 1] + c2 * w[1, k : k + 1]
        g_buf[k] = c0 * g[0, k : k + 1] + c1 * g[1, k : k + 1] + c2 * g[2, k : k + 1]
    copies = [
        pltpu.make_async_copy(w_buf, w_out, sems.at[0]),
        pltpu.make_async_copy(g_buf, g_out, sems.at[1]),
    ]
    for copy in copies:
        copy.start()
    for copy in copies:
        copy.wait()


def ring(x, axis, step):
    count = lax.axis_size(axis)
    return lax.ppermute(x, axis, [(i, (i + step) % count) for i in range(count)])


def frames(bands, sectors):
    table = np.zeros((bands, sectors, 8, 8), np.float64)
    half = 0.3 / bands
    for i in range(bands):
        s = -0.9 + 1.8 * (i + 0.5) / bands
        c = math.sqrt(1.0 - s * s)
        for j in range(sectors):
            lam = 2.0 * math.pi * (j + 0.5) / sectors
            cl, sl = math.cos(lam), math.sin(lam)
            table[i, j, :3, :3] = np.array([[-sl, cl, 0.0], [-s * cl, -s * sl, c], [c * cl, c * sl, s]]) / half
            table[i, j, :, 3:6] = [c * cl, c * sl, s]
            table[i, j, :4, 6] = [i, j, -sl, cl]
    return table.astype(np.float32)


VM = pl.BlockSpec(memory_space=pltpu.VMEM)
SM = pl.BlockSpec(memory_space=pltpu.SMEM)
HB = pl.BlockSpec(memory_space=pltpu.HBM)
MASKS = [pltpu.VMEM((16, BLK), jnp.int32), pltpu.SMEM((16, BLK), jnp.int32), pltpu.SemaphoreType.DMA]
PAIR = pltpu.VMEM((BLK, 2 * BLK), BF16)


def arr(*shape, dtype=F32):
    return jax.ShapeDtypeStruct(shape, dtype)


def call(kernel, name, ins, outs, scratch, flops, out_specs=None, vmem=VLIM):
    return pl.pallas_call(
        kernel,
        out_shape=outs,
        in_specs=ins,
        out_specs=[VM] * len(outs) if out_specs is None else out_specs,
        scratch_shapes=scratch,
        name=name,
        compiler_params=pltpu.CompilerParams(vmem_limit_bytes=vmem),
        cost_estimate=pl.CostEstimate(flops=flops, bytes_accessed=1 << 20, transcendentals=0),
    )


def tie(first, *rest):
    return lax.optimization_barrier((first, *rest))[0]


def per_device(tile_counts, obs_pos, innovation, bg_std_obs, obs_std, channel_corr, bg_std_grid):
    bands, sectors = lax.axis_size("lat"), lax.axis_size("lon")
    slots = obs_pos.shape[3]
    cells = bg_std_grid.shape[3]
    per = slots // BLK
    grids = cells // BLK
    table = jnp.asarray(frames(bands, sectors))

    def flat(x):
        return x.reshape(3, 1, x.shape[3])

    obs_in = pltpu.VMEM((3, 1, slots), F32)
    three = arr(3, slots)
    hb, dev, var, b0, rank, frame, bounds = call(
        sort_kernel,
        "sort",
        [SM] + [HB] * 5,
        [arr(8, slots), three, three, three, arr(1, slots), arr(8, 8), arr(8, BLK)],
        [obs_in] * 4 + [pltpu.SemaphoreType.DMA((5,))],
        10**8,
        vmem=60 * 1024 * 1024,
    )(tile_counts, table, flat(obs_pos), flat(innovation), flat(bg_std_obs), flat(obs_std))

    def exchange(block, beside, after):
        south, north = ring(block, "lat", 1), ring(block, "lat", -1)
        first = beside()
        mid = tie(jnp.stack([south, block, north]), first)
        west, east = ring(mid, "lon", 1), ring(mid, "lon", -1)
        second = after(first)
        west, east, second = lax.optimization_barrier((west, east, second))
        return (mid, west, east), first, second

    off = per * (per - 1) // 2

    def own_fill():
        return call(
            own_fill_kernel,
            "own_fill",
            [VM] * 3,
            [
                arr(per, 8, BLK),
                arr(per, 3, BLK, BLK),
                arr(1, off + BLK, dtype=jnp.int32),
                arr(per + off + UNROLL, BLK, 2 * BLK, dtype=BF16),
            ],
            MASKS,
            10**9,
            [VM, VM, SM, VM],
        )(frame, hb, bounds)

    def own_times(filled, u):
        return call(
            own_times_kernel,
            "own_times",
            [SM] + [VM] * 2,
            [arr(per, 8, BLK)],
            [pltpu.VMEM((per, 32, 2 * BLK), BF16)],
            10**8,
        )(*filled[2:], u)[0]

    near0, filled, acc = exchange(hb, own_fill, lambda filled: own_times(filled, hb))
    q_own, tcol = filled[:2]
    full = 8 * per * per
    q_near, pairs_near, pairs_cells, cache_near = call(
        near_fill_kernel,
        "near_fill",
        [VM] * 6,
        [
            arr(8 * per, 8, BLK),
            arr(1, full + BLK, dtype=jnp.int32),
            arr(1, 9 * per * (cells // BLK) + BLK, dtype=jnp.int32),
            arr(min(full, KEPT) + UNROLL, BLK, 2 * BLK, dtype=BF16),
        ],
        MASKS,
        10**9,
        [VM, SM, SM, VM],
    )(frame, bounds, tcol, *near0)

    def near_times(halo, acc, field):
        return call(
            near_times_kernel,
            "near_times",
            [SM] + [VM] * 11,
            [arr(8, slots), three, three],
            [pltpu.VMEM((8 * per, 32, 2 * BLK), BF16), pltpu.VMEM((per, 8, BLK), F32), PAIR],
            10**8,
        )(pairs_near, channel_corr, cache_near, q_near, tcol, acc, *halo, dev, var, field)

    u1, a0, b1 = near_times(near0, acc, b0)
    near1, acc, _ = exchange(u1, lambda: own_times(filled, u1), lambda acc: acc)
    u2, a1, b2 = near_times(near1, acc, b1)
    near2, acc, _ = exchange(u2, lambda: own_times(filled, u2), lambda acc: acc)
    _, a2, _ = near_times(near2, acc, b2)
    (packed,) = call(
        pack_kernel, "pack", [VM] * 14, [arr(9 * per, 16, BLK)], [], 10**7
    )(q_own, q_near, hb, u1, u2, *near0, *near1, *near2)
    (copies,) = call(gram_kernel, "gram", [VM] * 6, [arr(bands * sectors, 1, 16)], [], 10**6)(
        b0, b1, b2, a0, a1, a2
    )
    copies, packed = lax.optimization_barrier((copies, packed))
    parts = lax.all_to_all(copies, ("lat", "lon"), 0, 0, tiled=True)
    (parts_g,) = call(
        grid_kernel,
        "grid",
        [SM] + [VM] * 4,
        [arr(3, 3, cells)],
        [
            pltpu.VMEM((cells // BLK, 3, BLK, BLK), F32),
            pltpu.VMEM((GROUP, BLK, 2 * BLK), BF16),
            pltpu.VMEM((cells // BLK, 16, BLK), F32),
        ],
        10**9,
    )(pairs_cells, channel_corr, frame, packed, flat(bg_std_grid))
    (parts_w,) = call(unsort_kernel, "unsort", [VM] * 3, [arr(2, 3, slots)], [], 10**8)(rank, b1, b2)
    weights, increment = call(
        final_kernel,
        "final",
        [SM] + [VM] * 4,
        [arr(3, 1, slots), arr(3, 1, cells)],
        [obs_in, pltpu.VMEM((3, 1, cells), F32), pltpu.SemaphoreType.DMA((2,))],
        10**6,
        [HB, HB],
    )(tile_counts, parts, flat(innovation), parts_w, parts_g)
    return weights.reshape(1, 1, 3, slots), increment.reshape(1, 1, 3, cells)


def solution(mesh):
    spec = P("lat", "lon", None, None)
    return jax.shard_map(
        per_device,
        mesh=mesh,
        in_specs=(P("lat", "lon"), spec, spec, spec, spec, P(), spec),
        out_specs=(spec, spec),
        check_vma=False,
    )
```

```python
import functools
import math

import jax
import jax.numpy as jnp
import numpy as np
from jax import lax
from jax.experimental import pallas as pl
from jax.experimental.pallas import tpu as pltpu
from jax.sharding import PartitionSpec as P

OBS_TILE = 512
GRID_ROWS = 16
BLK = 128
SHIFT = 0.5
FAR = 64.0
NT = (((1,), (1,)), ((), ()))
NN = (((1,), (0,)), ((), ()))
F32 = jnp.float32
BF16 = jnp.bfloat16
VLIM = 8 * 1024 * 1024
UNROLL = 8
ROWS = 32
GROUP = 4
KEPT = 96
CELLS = 512


def split3(x):
    hi = x.astype(BF16)
    rest = x - hi.astype(F32)
    mid = rest.astype(BF16)
    low = (rest - mid.astype(F32)).astype(BF16)
    return jnp.concatenate([hi, mid, low], axis=0)


def col_of(row):
    return jnp.transpose(jnp.broadcast_to(row, (8, row.shape[1])))[:, 0:1]


def rank_of(key, slots):
    col = col_of(key)
    parts = []
    for j in range(slots // BLK):
        kj = key[:, j * BLK : (j + 1) * BLK]
        total = jnp.zeros((8, BLK), F32)
        for i in range(slots // BLK):
            ki = jnp.broadcast_to(col[i * BLK : (i + 1) * BLK, :], (BLK, BLK))
            if i < j:
                before = ki <= kj
            elif i > j:
                before = ki < kj
            else:
                first = lax.broadcasted_iota(jnp.int32, (BLK, BLK), 0) < lax.broadcasted_iota(
                    jnp.int32, (BLK, BLK), 1
                )
                before = (ki < kj) | ((ki == kj) & first)
            ones = jnp.where(before, 1.0, 0.0).astype(F32)
            total = total + jnp.sum(ones.reshape(BLK // 8, 8, BLK), axis=0)
        parts.append(jnp.sum(total, axis=0, keepdims=True))
    return jnp.concatenate(parts, axis=1)


def onehot_of(rank, slots):
    place = lax.broadcasted_iota(jnp.int32, (slots, slots), 0).astype(F32)
    return jnp.where(place == rank, 1.0, 0.0).astype(BF16)


def angle_of(x):
    x2 = x * x
    return x * (1.0 + x2 * (1.0 / 6.0 + x2 * (3.0 / 40.0 + x2 * (15.0 / 336.0))))


def sort_kernel(
    count, table, pos_in, innov_in, bg_in, std_in, bgg_in, corr_in,
    hb_out, dev_out, var_out, b0_out, rank_out, frame_out, bounds_out, innov_out, bgg_out, corr_out,
    pos, innov, bg, std, sems,
):
    bands, sectors = lax.axis_size("lat"), lax.axis_size("lon")
    band, sector = lax.axis_index("lat"), lax.axis_index("lon")
    pairs = [
        (table.at[band, sector], frame_out),
        (pos_in, pos),
        (innov_in, innov),
        (bg_in, bg),
        (std_in, std),
        (bgg_in, bgg_out),
        (corr_in, corr_out),
    ]
    copies = [pltpu.make_async_copy(x, y, sems.at[k]) for k, (x, y) in enumerate(pairs)]
    for copy in copies:
        copy.start()
    copies[0].wait()
    copies[1].wait()

    def rows(ref):
        return jnp.concatenate([ref[0], ref[1], ref[2]], axis=0)

    slots = pos.shape[2]
    per = slots // BLK
    frame = frame_out[...]
    live_n = count[0, 0] * OBS_TILE
    lane = lax.broadcasted_iota(jnp.int32, (1, slots), 1)
    live = lane < live_n
    px, py, pz = pos[0], pos[1], pos[2]
    key = jnp.where(live, pz, 10.0)
    first = rank_of(key, slots)
    strip = jnp.where(first * 2.0 >= live_n.astype(F32), 8.0, 0.0)
    east = frame[2:3, 6:7] * px + frame[3:4, 6:7] * py
    sine = east * lax.rsqrt(jnp.maximum(px * px + py * py, 1e-6))
    rank = rank_of(jnp.where(live, strip + sine, 100.0), slots)
    rank_out[...] = rank
    for copy in copies[2:]:
        copy.wait()
    maskf = jnp.where(live, 1.0, 0.0).astype(F32)
    where3 = jnp.where(live, rows(pos), FAR)
    dev = rows(bg) * maskf
    start = rows(innov) * maskf
    innov_out[...] = start
    var = rows(std)
    var = var * var * maskf
    sine = jnp.where(live, sine, 0.0)
    vals = jnp.concatenate([where3, dev, start, var, sine, jnp.zeros((3, slots), F32)], axis=0)
    got = lax.dot_general(split3(vals), onehot_of(rank, slots), NT, preferred_element_type=F32)
    got = got[0:16] + got[16:32] + got[32:48]
    dev, start = got[3:6], got[6:9]
    dev_out[...] = dev
    b0_out[...] = start
    var_out[...] = got[9:12]

    z = jnp.concatenate(blocks(got[2:3]), axis=0)
    angle = angle_of(jnp.concatenate(blocks(got[12:13]), axis=0))
    bounds = [
        jnp.min(z, axis=1, keepdims=True),
        jnp.max(z, axis=1, keepdims=True),
        jnp.min(angle, axis=1, keepdims=True),
        jnp.max(angle, axis=1, keepdims=True),
    ]
    sub = lax.broadcasted_iota(jnp.int32, (per, BLK), 0)
    col = lax.broadcasted_iota(jnp.int32, (per, BLK), 1)

    def spread(x, index):
        return jnp.sum(jnp.where(sub == index, x, 0.0), axis=0, keepdims=True)

    as_source = [spread(x, col & 7) for x in bounds]
    pad = jnp.zeros((1, slots - 4 * BLK), F32)
    hb_out[...] = jnp.concatenate(
        [dev * start, got[0:3], jnp.concatenate(as_source + [pad], axis=1), jnp.zeros((1, slots), F32)],
        axis=0,
    )
    as_target = [spread(x, col >> 3) for x in bounds]
    lane = lax.broadcasted_iota(jnp.int32, (1, BLK), 1)
    t = ((lane - 64) >> 3).astype(F32)
    tall = 1.0 * BLK * GRID_ROWS / CELLS
    floor = -0.9 + 1.8 * band.astype(F32) / bands
    step = 1.8 / bands / GRID_ROWS
    half_width = math.pi / sectors
    grid = [
        floor + step * (t * tall + 0.25),
        floor + step * (t * tall + tall - 0.25),
        jnp.full((1, BLK), -half_width, F32),
        jnp.full((1, BLK), half_width, F32),
    ]
    grid_end = 64 + 8 * (CELLS // BLK)
    rows = [
        jnp.where(lane < 64, x, jnp.where(lane < grid_end, g, 100.0)) for x, g in zip(as_target, grid)
    ]
    bounds_out[...] = jnp.concatenate(rows + [jnp.zeros((4, BLK), F32)], axis=0)


def blocks(wide):
    return [wide[:, b * BLK : (b + 1) * BLK] for b in range(wide.shape[1] // BLK)]


def active_blocks(source, target, bands):
    slo, shi, wlo, whi = source
    tlo, thi, vlo, vhi = target

    def radius(z):
        return jnp.sqrt(jnp.maximum(1.0 - z * z, 0.0))

    below, above = jnp.minimum(shi, thi), jnp.maximum(slo, tlo)
    fall = radius(below) - radius(above)
    apart = above - below
    lat = jnp.where(apart > 0.0, apart * apart + fall * fall, 0.0)
    gap = jnp.maximum(jnp.maximum(wlo, vlo) - jnp.minimum(whi, vhi), 0.0)
    gap2 = gap * gap
    small = radius(jnp.maximum(jnp.abs(slo), jnp.abs(shi))) * radius(
        jnp.maximum(jnp.abs(tlo), jnp.abs(thi))
    )
    bound = lat + gap2 * (1.0 - gap2 * (1.0 / 12.0)) * small
    reach = (0.6 / bands) ** 2
    return (bound < reach * 1.002 + 1e-6) & (tlo < 50.0) & (slo < 50.0)


def source_bounds(tiles, shifts, height):
    rows = []
    for k in range(4):
        parts = []
        for tile, shift in zip(tiles, shifts):
            row = tile[6:7, k * BLK : (k + 1) * BLK]
            parts.append(row + shift if k >= 2 else row)
        parts.append(jnp.full((height - len(tiles), BLK), 100.0, F32))
        rows.append(jnp.concatenate(parts, axis=0))
    return rows


def two_lists(active, source, target, regions):
    height = active.shape[0]

    def exact(x, y, dims):
        return lax.dot_general(x.astype(BF16), y.astype(BF16), dims, preferred_element_type=F32)

    def ones(mask):
        return jnp.where(mask, 1.0, 0.0).astype(F32)

    def iota(shape, dim):
        return lax.broadcasted_iota(jnp.int32, shape, dim)

    act = ones(active)
    i, j = iota((BLK, BLK), 0), iota((BLK, BLK), 1)
    same = ones((i >> 6) == (j >> 6))
    ahead = ones(((i >> 6) == (j >> 6)) & (i < j))
    above = ones(iota((height, height), 1) < iota((height, height), 0))
    place = exact(act, ahead, NN) + exact(exact(above, act, NN), same, NN)
    counts = exact(exact(jnp.ones((8, height), F32), act, NN), same, NN)[0:1]
    lane = iota(active.shape, 1)
    slot = jnp.where(active & (place < BLK), place + jnp.where(lane < 64, 0.0, 1.0 * BLK), -1.0)
    index = iota((2 * BLK, BLK), 0).astype(F32)
    picks = jnp.concatenate([ones(index == slot[r : r + 1]) for r in range(regions)], axis=1)
    names = [
        jnp.concatenate([x[r : r + 1].astype(F32) for r in range(regions)], axis=1)
        for x in (source, target)
    ]
    names = jnp.concatenate(names + [jnp.zeros((6, regions * BLK), F32)], axis=0)
    found = exact(names, picks, NT)
    entries = found[0:1] * 8.0 + found[1:2]
    return jnp.concatenate(
        [entries[:, 0:BLK], entries[:, BLK : 2 * BLK], counts, jnp.zeros((5, BLK), F32)], axis=0
    ).astype(jnp.int32)


def rho_of(tcol, sx, sy, sz):
    dx, dy, dz = tcol[0] - sx, tcol[1] - sy, tcol[2] - sz
    s = dx * dx + dy * dy + dz * dz
    r = lax.rsqrt(jnp.maximum(s, 1e-30))
    z = s * r
    inner = s * (((-0.25 * z + 0.5) * z + 0.625) * z - 5.0 / 3.0) + 1.0
    t = jnp.maximum(2.0 - z, 0.0)
    t = t * t
    u = z + 1.0
    outer = (t * t) * (u * u * (1.0 / 12.0) - 0.125) * r
    return jnp.where(s <= 1.0, inner, outer)


def to_frame(tile, row, frame):
    q = None
    for k in range(3):
        term = frame[:, k : k + 1] * (tile[row + k : row + k + 1, :] - frame[:, 3 + k : 4 + k])
        q = term if q is None else q + term
    return q


def set_columns(targets, tcol):
    for t, tile in enumerate(targets):
        turned = jnp.transpose(tile)
        for k in range(3):
            tcol[t, k] = jnp.broadcast_to(turned[:, k : k + 1], (BLK, BLK))


def fill_rows(q, tcol, t, out):
    sx, sy, sz = q[0:1], q[1:2], q[2:3]
    for i in range(0, BLK, ROWS):
        rho = rho_of([tcol[t, k, i : i + ROWS] for k in range(3)], sx, sy, sz)
        hi = rho.astype(BF16)
        out[i : i + ROWS, 0:BLK] = hi
        out[i : i + ROWS, BLK : 2 * BLK] = (rho - hi.astype(F32)).astype(BF16)


def fill_pair(entry, q_ref, tcol, out):
    fill_rows(q_ref[entry >> 3], tcol, entry & 7, out)


def fill_cache(count, lists, q_ref, tcol, cache, first):
    room = cache.shape[0] - UNROLL - first
    kept = jnp.minimum(count, room)

    def fill(p, _):
        fill_pair(lists[0, p], q_ref, tcol, cache.at[first + p])
        return 0

    lax.fori_loop(0, kept, fill, 0)
    for k in range(UNROLL):
        cache[first + kept + k] = jnp.zeros(cache.shape[1:], BF16)


def parts_of(tile):
    hi = tile.astype(BF16).astype(F32)
    rest = tile - hi
    mid = rest.astype(BF16).astype(F32)
    return [hi, mid, rest - mid]


def set_values(rows, v_ref, first):
    v = jnp.concatenate(parts_of(rows) + [jnp.zeros(rows.shape, F32)], axis=0).astype(BF16)
    for b, part in enumerate(blocks(v)):
        v_ref[first + b, :, 0:BLK] = part
        v_ref[first + b, :, BLK : 2 * BLK] = part


def add_parts(out):
    return out[0:8] + out[8:16]


def total_of(acc):
    wide = jnp.concatenate([acc[t] for t in range(acc.shape[0])], axis=1)
    return wide[0:4] + wide[4:8]


def own_fill_kernel(frame, hb, bounds, q_out, tcol_out, lists_out, cache_out, lists_v, sem):
    tile = hb[...]
    tiles = blocks(to_frame(tile, 3, frame[...]))
    per = len(tiles)
    active = active_blocks(
        source_bounds([tile], [0.0], 8), [bounds[k : k + 1, :] for k in range(4)], lax.axis_size("lat")
    )
    lane = lax.broadcasted_iota(jnp.int32, active.shape, 1)
    source, target = lane & 7, (lane >> 3) & 7
    lists_v[...] = two_lists(active & (lane < 64) & (target < source), source, target, 1)
    copy = pltpu.make_async_copy(lists_v, lists_out, sem)
    copy.start()
    for b, part in enumerate(tiles):
        q_out[b] = part
    set_columns(tiles, tcol_out)

    def diagonal(b, _):
        fill_pair(b * 9, q_out, tcol_out, cache_out.at[b])
        return 0

    lax.fori_loop(0, per, diagonal, 0)
    copy.wait()
    fill_cache(lists_out[2, 0], lists_out, q_out, tcol_out, cache_out, per)


def own_times_kernel(pairs, cache, u, acc, v_ref):
    set_values(u[0:4, :], v_ref, 0)
    per = acc.shape[0]
    for b in range(per):
        acc[b] = add_parts(lax.dot_general(v_ref[b], cache[b], NT, preferred_element_type=F32))
    count = pairs[2, 0]

    def group(i, _):
        outs = []
        for k in range(UNROLL // 2):
            p = i * (UNROLL // 2) + k
            n, t = pairs[0, p] >> 3, pairs[0, p] & 7
            rho = cache[per + p]
            ahead = lax.dot_general(v_ref[n], rho, NT, preferred_element_type=F32)
            back = lax.dot_general(v_ref[t, :, 0:BLK], rho, NN, preferred_element_type=F32)
            outs.append((ahead, back[:, 0:BLK] + back[:, BLK : 2 * BLK]))
        for k in range(UNROLL // 2):
            p = i * (UNROLL // 2) + k
            n, t = pairs[0, p] >> 3, pairs[0, p] & 7
            acc[t] += add_parts(outs[k][0])
            acc[n] += add_parts(outs[k][1])
        return 0

    half = UNROLL // 2
    lax.fori_loop(0, (count + half - 1) // half, group, 0)


OTHERS = [(0, 0), (0, 2), (1, 0), (1, 1), (1, 2), (2, 0), (2, 1), (2, 2)]


def near_fill_kernel(
    frame, bounds, tcol, mid, south, north,
    q_out, lists_out, long_out, cache_out, lists_v, mask_v, mask_s, sem, sem_long,
):
    halo = (mid, south, north)
    per = mid.shape[2] // BLK
    turn = 2.0 * math.pi / lax.axis_size("lon") * frame[4:5, 6:7]
    where = [(0, 1)] + OTHERS
    regions = len(where)
    tiles = [halo[c][a] for c, a in where]
    active = active_blocks(
        source_bounds(tiles, [(a - 1) * turn for c, a in where], 16),
        [bounds[k : k + 1, :] for k in range(4)],
        lax.axis_size("lat"),
    )
    lane = lax.broadcasted_iota(jnp.int32, active.shape, 1)
    region = lax.broadcasted_iota(jnp.int32, active.shape, 0)
    active = active & ((lane >= 64) | (region > 0))
    source = (lane & 7) + 8 * jnp.where(lane < 64, region - 1, region)
    target = (lane >> 3) & 7
    lists_v[...] = two_lists(active, source, target, regions)
    copy = pltpu.make_async_copy(lists_v, lists_out, sem)
    copy.start()
    turned = frame[...]
    for r in range(1, regions):
        for b, part in enumerate(blocks(to_frame(tiles[r], 3, turned))):
            q_out[(r - 1) * per + b] = part
    mask_v[...] = jnp.where(active, source * 8 + target + 1, 0)
    copy.wait()
    count, count_cells = lists_out[2, 0], lists_out[2, 64]

    @pl.when((count > KEPT) | (count_cells > KEPT))
    def _():
        again = pltpu.make_async_copy(mask_v, mask_s, sem_long)
        again.start()
        again.wait()
        for half in range(2):

            def step(i, k, half=half):
                entry = mask_s[i >> 6, 64 * half + (i & 63)]
                long_out[half, k] = entry - 1
                return k + jnp.where(entry > 0, 1, 0)

            lax.fori_loop(0, 64 * regions, step, 0)

    fill_cache(count, lists_out, q_out, tcol, cache_out, 0)


def mix(corr, total):
    out = None
    for c in range(3):
        term = corr[:, c : c + 1] * total[c : c + 1, :]
        out = term if out is None else out + term
    return out


def near_times_kernel(
    last, lists, long, corr, cache, q_ref, tcol, acc_own, um, us, un, dev, var, field, *refs
):
    outs, (v_ref, acc, pair) = refs[:-3], refs[-3:]
    halo = (um, us, un)
    per = acc.shape[0]
    for k, (c, a) in enumerate(OTHERS):
        set_values(halo[c][a, 0:4, :], v_ref, k * per)
    acc[...] = acc_own[...]
    count = lists[2, 0]
    kept = jnp.minimum(count, cache.shape[0] - UNROLL)

    def group(i, _):
        found = []
        for k in range(UNROLL):
            p = i * UNROLL + k
            n = lists[0, p] >> 3
            found.append(lax.dot_general(v_ref[n], cache[p], NT, preferred_element_type=F32))
        for k in range(UNROLL):
            acc[lists[0, i * UNROLL + k] & 7] += add_parts(found[k])
        return 0

    lax.fori_loop(0, (kept + UNROLL - 1) // UNROLL, group, 0)

    def extra(p, _):
        entry = long[0, p]
        fill_pair(entry, q_ref, tcol, pair)
        out = lax.dot_general(v_ref[entry >> 3], pair[...], NT, preferred_element_type=F32)
        acc[entry & 7] += add_parts(out)
        return 0

    lax.fori_loop(kept, count, extra, 0)
    field = field[...]
    dev = dev[...]
    image = dev * mix(corr, total_of(acc)) + var[...] * field
    outs[0][...] = image
    if not last:
        nxt = image - SHIFT * field
        outs[1][...] = nxt
        outs[2][...] = jnp.concatenate([dev * nxt, jnp.zeros((1, nxt.shape[1]), F32)], axis=0)


def gram_kernel(b0, b1, b2, a0, a1, a2, out):
    pairs = [(b0, a0), (b0, a1), (b0, a2), (b1, a1), (b1, a2), (b2, a2), (b0, b0), (b1, b0), (b2, b0)]
    rows = []
    for x, y in pairs:
        prod = blocks(x[...] * y[...])
        while len(prod) > 1:
            prod = [prod[k] + prod[k + 1] for k in range(0, len(prod), 2)]
        rows.append(jnp.sum(prod[0], axis=0, keepdims=True))
    rows.append(jnp.zeros((16 - len(rows), BLK), F32))
    totals = jnp.sum(jnp.concatenate(rows, axis=0), axis=1, keepdims=True)
    sub = lax.broadcasted_iota(jnp.int32, (16, 16), 0)
    col = lax.broadcasted_iota(jnp.int32, (16, 16), 1)
    row = jnp.sum(jnp.where(sub == col, totals, 0.0), axis=0, keepdims=True)
    out[...] = jnp.broadcast_to(row[None], out.shape)


def pack_kernel(q_own, q_near, *refs):
    out = refs[-1]
    fields = [refs[3 * f : 3 * f + 3] for f in range(3)]
    per = q_own.shape[0]
    for f in range(3):
        for r, (c, a) in enumerate([(0, 1)] + OTHERS):
            tile = fields[f][c][a, 0:4, :]
            for b, part in enumerate(blocks(tile)):
                out[r * per + b, 3 * f : 3 * f + 3, :] = part[0:3]
    for b in range(per):
        out[b, 9:12, :] = q_own[b, 0:3, :]
    for n in range(q_near.shape[0]):
        out[per + n, 9:12, :] = q_near[n, 0:3, :]
    for n in range(out.shape[0]):
        out[n, 12:16, :] = jnp.zeros((4, BLK), F32)


def grid_kernel(lists, long, corr, frame, packed, bgg, g_out, tcol, rho, acc):
    cells = g_out.shape[2]
    columns = cells // GRID_ROWS
    bands, sectors = lax.axis_size("lat"), lax.axis_size("lon")
    cell = lax.broadcasted_iota(jnp.int32, (8, cells), 1)
    row = lax.broadcasted_iota(jnp.int32, (8, cells), 0)
    frac_lat = ((cell // columns).astype(F32) + 0.5) / GRID_ROWS
    frac_lon = ((cell % columns).astype(F32) + 0.5) / columns
    band, sector = frame[0:1, 6:7], frame[1:2, 6:7]
    sinlat = -0.9 + 1.8 * (band + frac_lat) / bands
    longitude = 2.0 * math.pi * (sector + frac_lon) / sectors
    coslat = jnp.sqrt(1.0 - sinlat * sinlat)
    point = jnp.where(row == 0, coslat * jnp.cos(longitude), coslat * jnp.sin(longitude))
    point = jnp.where(row == 2, sinlat, point)
    set_columns(blocks(to_frame(point, 0, frame[...])), tcol)
    acc[...] = jnp.zeros(acc.shape, F32)
    count = lists[2, 64]
    short = jnp.minimum(count, KEPT)

    def one(entry, weight, out):
        near = packed[entry >> 3]
        fill_rows(near[9:12], tcol, entry & 7, out)
        v = jnp.concatenate(parts_of(near * weight), axis=0).astype(BF16)
        v = jnp.concatenate([v, v], axis=1)
        got = lax.dot_general(v, out[...], NT, preferred_element_type=F32)
        return got[0:16] + got[16:32] + got[32:48]

    def group(i, _):
        found = []
        for k in range(GROUP):
            p = i * GROUP + k
            weight = jnp.where(p < short, 1.0, 0.0).astype(F32)
            found.append(one(lists[1, p], weight, rho.at[k]))
        for k in range(GROUP):
            acc[lists[1, i * GROUP + k] & 7] += found[k]
        return 0

    lax.fori_loop(0, (short + GROUP - 1) // GROUP, group, 0)

    def extra(p, _):
        entry = long[1, p]
        acc[entry & 7] += one(entry, 1.0, rho.at[0])
        return 0

    lax.fori_loop(short, count, extra, 0)
    total = jnp.concatenate([acc[t] for t in range(acc.shape[0])], axis=1)
    dev = jnp.concatenate([bgg[0], bgg[1], bgg[2]], axis=0)
    for f in range(3):
        g_out[f] = dev * mix(corr, total[3 * f : 3 * f + 3])


def unsort_kernel(rank, b1, b2, w_out):
    slots = rank.shape[1]
    vals = jnp.concatenate([b1[...], b2[...], jnp.zeros((10, slots), F32)], axis=0)
    back = lax.dot_general(split3(vals), onehot_of(rank[...], slots), NN, preferred_element_type=F32)
    back = back[0:16] + back[16:32] + back[32:48]
    w_out[0] = back[0:3]
    w_out[1] = back[3:6]


def final_kernel(parts, innov, w, g, w_out, g_out, w_buf, g_buf, sems):
    sums = parts[...]
    while sums.shape[0] > 1:
        half = sums.shape[0] // 2
        sums = sums[:half] + sums[half:]
    sums = sums[0]
    lane = lax.broadcasted_iota(jnp.int32, sums.shape, 1)
    m00, m01, m02, m11, m12, m22, g0, g1, g2 = [
        jnp.sum(jnp.where(lane == k, sums, 0.0), axis=1, keepdims=True) for k in range(9)
    ]
    l10, l20 = m01 / m00, m02 / m00
    d1 = m11 - l10 * m01
    e12 = m12 - l10 * m02
    ok1 = d1 > 1e-6 * m11
    safe1 = jnp.where(ok1, d1, 1.0)
    l21 = jnp.where(ok1, e12 / safe1, 0.0)
    d2 = m22 - l20 * m02 - l21 * e12
    ok2 = ok1 & (d2 > 1e-6 * m22)
    y1 = g1 - l10 * g0
    y2 = g2 - l20 * g0 - l21 * y1
    c2 = jnp.where(ok2, y2 / jnp.where(ok2, d2, 1.0), 0.0)
    c1 = jnp.where(ok1, y1 / safe1, 0.0) - l21 * c2
    c0 = g0 / m00 - l10 * c1 - l20 * c2
    for k in range(3):
        w_buf[k] = c0 * innov[k : k + 1, :] + c1 * w[0, k : k + 1] + c2 * w[1, k : k + 1]
        g_buf[k] = c0 * g[0, k : k + 1] + c1 * g[1, k : k + 1] + c2 * g[2, k : k + 1]
    copies = [
        pltpu.make_async_copy(w_buf, w_out, sems.at[0]),
        pltpu.make_async_copy(g_buf, g_out, sems.at[1]),
    ]
    for copy in copies:
        copy.start()
    for copy in copies:
        copy.wait()


def ring(x, axis, step):
    count = lax.axis_size(axis)
    return lax.ppermute(x, axis, [(i, (i + step) % count) for i in range(count)])


def swap(x, axis, first, wrap):
    count = lax.axis_size(axis)
    pairs = []
    for i in range(first, count, 2):
        if i + 1 < count or wrap:
            pairs += [(i, (i + 1) % count), ((i + 1) % count, i)]
    return lax.ppermute(x, axis, pairs)


def frames(bands, sectors):
    table = np.zeros((bands, sectors, 8, 8), np.float64)
    half = 0.3 / bands
    for i in range(bands):
        s = -0.9 + 1.8 * (i + 0.5) / bands
        c = math.sqrt(1.0 - s * s)
        for j in range(sectors):
            lam = 2.0 * math.pi * (j + 0.5) / sectors
            cl, sl = math.cos(lam), math.sin(lam)
            table[i, j, :3, :3] = np.array([[-sl, cl, 0.0], [-s * cl, -s * sl, c], [c * cl, c * sl, s]]) / half
            table[i, j, :, 3:6] = [c * cl, c * sl, s]
            table[i, j, :5, 6] = [i, j, -sl, cl, 2 * (j % 2) - 1]
    return table.astype(np.float32)


VM = pl.BlockSpec(memory_space=pltpu.VMEM)
SM = pl.BlockSpec(memory_space=pltpu.SMEM)
HB = pl.BlockSpec(memory_space=pltpu.HBM)
LISTS = pltpu.VMEM((8, BLK), jnp.int32)
PAIR = pltpu.VMEM((BLK, 2 * BLK), BF16)


def arr(*shape, dtype=F32):
    return jax.ShapeDtypeStruct(shape, dtype)


def call(kernel, name, ins, outs, scratch, flops, out_specs=None, vmem=VLIM):
    return pl.pallas_call(
        kernel,
        out_shape=outs,
        in_specs=ins,
        out_specs=[VM] * len(outs) if out_specs is None else out_specs,
        scratch_shapes=scratch,
        name=name,
        compiler_params=pltpu.CompilerParams(vmem_limit_bytes=vmem),
        cost_estimate=pl.CostEstimate(flops=flops, bytes_accessed=1 << 20, transcendentals=0),
    )


def tie(first, *rest):
    return lax.optimization_barrier((first, *rest))[0]


def per_device(tile_counts, obs_pos, innovation, bg_std_obs, obs_std, channel_corr, bg_std_grid):
    bands, sectors = lax.axis_size("lat"), lax.axis_size("lon")
    slots = obs_pos.shape[3]
    cells = bg_std_grid.shape[3]
    per = slots // BLK
    grids = cells // BLK
    table = pltpu.with_memory_space_constraint(jnp.asarray(frames(bands, sectors)), pltpu.HBM)

    def flat(x):
        return pltpu.with_memory_space_constraint(x.reshape(3, 1, x.shape[3]), pltpu.HBM)

    obs_in = pltpu.VMEM((3, 1, slots), F32)
    three = arr(3, slots)
    hb, dev, var, b0, rank, frame, bounds, innov, bgg, corr = call(
        sort_kernel,
        "sort",
        [SM] + [HB] * 7,
        [arr(8, slots), three, three, three, arr(1, slots), arr(8, 8), arr(8, BLK), three]
        + [arr(3, 1, cells), arr(3, 3)],
        [obs_in] * 4 + [pltpu.SemaphoreType.DMA((7,))],
        10**8,
    )(
        tile_counts, table, flat(obs_pos), flat(innovation), flat(bg_std_obs), flat(obs_std),
        flat(bg_std_grid), pltpu.with_memory_space_constraint(channel_corr, pltpu.HBM),
    )

    def exchange(block, beside, after):
        one, two = swap(block, "lon", 0, True), swap(block, "lon", 1, True)
        first = beside()
        mid = tie(jnp.stack([one, block, two]), first)
        three, four = ring(mid, "lat", 1), ring(mid, "lat", -1)
        second = after(first)
        three, four, second = lax.optimization_barrier((three, four, second))
        return (mid, three, four), first, second

    off = per * (per - 1) // 2

    def own_fill():
        return call(
            own_fill_kernel,
            "own_fill",
            [VM] * 3,
            [
                arr(per, 8, BLK),
                arr(per, 3, BLK, BLK),
                arr(8, BLK, dtype=jnp.int32),
                arr(per + off + UNROLL, BLK, 2 * BLK, dtype=BF16),
            ],
            [LISTS, pltpu.SemaphoreType.DMA],
            10**9,
            [VM, VM, SM, VM],
        )(frame, hb, bounds)

    def own_times(filled, u):
        return call(
            own_times_kernel,
            "own_times",
            [SM] + [VM] * 2,
            [arr(per, 8, BLK)],
            [pltpu.VMEM((per, 16, 2 * BLK), BF16)],
            10**8,
        )(*filled[2:], u)[0]

    near0, filled, acc = exchange(hb, own_fill, lambda filled: own_times(filled, hb))
    q_own, tcol = filled[:2]
    full = 8 * per * per
    q_near, lists, long, cache_near = call(
        near_fill_kernel,
        "near_fill",
        [VM] * 6,
        [
            arr(8 * per, 8, BLK),
            arr(8, BLK, dtype=jnp.int32),
            arr(2, 9 * per * per + BLK, dtype=jnp.int32),
            arr(min(full, KEPT) + UNROLL, BLK, 2 * BLK, dtype=BF16),
        ],
        [LISTS, pltpu.VMEM((16, BLK), jnp.int32), pltpu.SMEM((16, BLK), jnp.int32)]
        + [pltpu.SemaphoreType.DMA] * 2,
        10**9,
        [VM, SM, SM, VM],
    )(frame, bounds, tcol, *near0)

    def near_times(halo, acc, field, last=False):
        return call(
            functools.partial(near_times_kernel, last),
            "near_times",
            [SM] * 2 + [VM] * 11,
            [three] if last else [three, three, arr(4, slots)],
            [pltpu.VMEM((8 * per, 16, 2 * BLK), BF16), pltpu.VMEM((per, 8, BLK), F32), PAIR],
            10**8,
        )(lists, long, corr, cache_near, q_near, tcol, acc, *halo, dev, var, field)

    a0, b1, u1 = near_times(near0, acc, b0)
    near1, acc, _ = exchange(u1, lambda: own_times(filled, u1), lambda acc: acc)
    a1, b2, u2 = near_times(near1, acc, b1)
    near2, acc, _ = exchange(u2, lambda: own_times(filled, u2), lambda acc: acc)
    (a2,) = near_times(near2, acc, b2, last=True)
    (packed,) = call(
        pack_kernel, "pack", [VM] * 11, [arr(9 * per, 16, BLK)], [], 10**7
    )(q_own, q_near, *near0, *near1, *near2)
    (copies,) = call(gram_kernel, "gram", [VM] * 6, [arr(bands * sectors, 1, 16)], [], 10**6)(
        b0, b1, b2, a0, a1, a2
    )
    copies, packed = lax.optimization_barrier((copies, packed))
    parts = lax.all_to_all(copies, ("lat", "lon"), 0, 0, tiled=True)
    (parts_g,) = call(
        grid_kernel,
        "grid",
        [SM] * 2 + [VM] * 4,
        [arr(3, 3, cells)],
        [
            pltpu.VMEM((cells // BLK, 3, BLK, BLK), F32),
            pltpu.VMEM((GROUP, BLK, 2 * BLK), BF16),
            pltpu.VMEM((cells // BLK, 16, BLK), F32),
        ],
        10**9,
    )(lists, long, corr, frame, packed, bgg)
    (parts_w,) = call(unsort_kernel, "unsort", [VM] * 3, [arr(2, 3, slots)], [], 10**8)(rank, b1, b2)
    weights, increment = call(
        final_kernel,
        "final",
        [VM] * 4,
        [arr(3, 1, slots), arr(3, 1, cells)],
        [obs_in, pltpu.VMEM((3, 1, cells), F32), pltpu.SemaphoreType.DMA((2,))],
        10**6,
        [HB, HB],
    )(parts, innov, parts_w, parts_g)
    return weights.reshape(1, 1, 3, slots), increment.reshape(1, 1, 3, cells)


def solution(mesh):
    spec = P("lat", "lon", None, None)
    return jax.shard_map(
        per_device,
        mesh=mesh,
        in_specs=(P("lat", "lon"), spec, spec, spec, spec, P(), spec),
        out_specs=(spec, spec),
        check_vma=False,
    )
```

```python
import functools
import math

import jax
import jax.numpy as jnp
import numpy as np
from jax import lax
from jax.experimental import pallas as pl
from jax.experimental.pallas import tpu as pltpu
from jax.sharding import PartitionSpec as P

OBS_TILE = 512
GRID_ROWS = 16
BLK = 128
SHIFT = 0.5
FAR = 64.0
NT = (((1,), (1,)), ((), ()))
NN = (((1,), (0,)), ((), ()))
F32 = jnp.float32
BF16 = jnp.bfloat16
VLIM = 8 * 1024 * 1024
UNROLL = 8
ROWS = 32
GROUP = 4
KEPT = 96
CELLS = 512


def split3(x):
    hi = x.astype(BF16)
    rest = x - hi.astype(F32)
    mid = rest.astype(BF16)
    low = (rest - mid.astype(F32)).astype(BF16)
    return jnp.concatenate([hi, mid, low], axis=0)


def col_of(row):
    return jnp.transpose(jnp.broadcast_to(row, (8, row.shape[1])))[:, 0:1]


def rank_of(key, slots):
    col = col_of(key)
    parts = []
    for j in range(slots // BLK):
        kj = key[:, j * BLK : (j + 1) * BLK]
        total = jnp.zeros((8, BLK), F32)
        for i in range(slots // BLK):
            ki = jnp.broadcast_to(col[i * BLK : (i + 1) * BLK, :], (BLK, BLK))
            if i < j:
                before = ki <= kj
            elif i > j:
                before = ki < kj
            else:
                first = lax.broadcasted_iota(jnp.int32, (BLK, BLK), 0) < lax.broadcasted_iota(
                    jnp.int32, (BLK, BLK), 1
                )
                before = (ki < kj) | ((ki == kj) & first)
            ones = jnp.where(before, 1.0, 0.0).astype(F32)
            total = total + jnp.sum(ones.reshape(BLK // 8, 8, BLK), axis=0)
        parts.append(jnp.sum(total, axis=0, keepdims=True))
    return jnp.concatenate(parts, axis=1)


def onehot_of(rank, slots):
    place = lax.broadcasted_iota(jnp.int32, (slots, slots), 0).astype(F32)
    return jnp.where(place == rank, 1.0, 0.0).astype(BF16)


def angle_of(x):
    x2 = x * x
    return x * (1.0 + x2 * (1.0 / 6.0 + x2 * (3.0 / 40.0 + x2 * (15.0 / 336.0))))


def sort_kernel(
    count, table, pos_in, innov_in, bg_in, std_in, bgg_in, corr_in,
    hb_out, dev_out, var_out, b0_out, rank_out, frame_out, bounds_out, innov_out, bgg_out, corr_out,
    pos, innov, bg, std, sems,
):
    bands, sectors = lax.axis_size("lat"), lax.axis_size("lon")
    band, sector = lax.axis_index("lat"), lax.axis_index("lon")
    pairs = [
        (table.at[band, sector], frame_out),
        (pos_in, pos),
        (innov_in, innov),
        (bg_in, bg),
        (std_in, std),
        (bgg_in, bgg_out),
        (corr_in, corr_out),
    ]
    copies = [pltpu.make_async_copy(x, y, sems.at[k]) for k, (x, y) in enumerate(pairs)]
    for copy in copies:
        copy.start()
    copies[0].wait()
    copies[1].wait()

    def rows(ref):
        return jnp.concatenate([ref[0], ref[1], ref[2]], axis=0)

    slots = pos.shape[2]
    per = slots // BLK
    frame = frame_out[...]
    live_n = count[0, 0] * OBS_TILE
    lane = lax.broadcasted_iota(jnp.int32, (1, slots), 1)
    live = lane < live_n
    px, py, pz = pos[0], pos[1], pos[2]
    key = jnp.where(live, pz, 10.0)
    first = rank_of(key, slots)
    strip = jnp.where(first * 2.0 >= live_n.astype(F32), 8.0, 0.0)
    east = frame[2:3, 6:7] * px + frame[3:4, 6:7] * py
    sine = east * lax.rsqrt(jnp.maximum(px * px + py * py, 1e-6))
    rank = rank_of(jnp.where(live, strip + sine, 100.0), slots)
    rank_out[...] = rank
    for copy in copies[2:]:
        copy.wait()
    maskf = jnp.where(live, 1.0, 0.0).astype(F32)
    where3 = jnp.where(live, rows(pos), FAR)
    dev = rows(bg) * maskf
    start = rows(innov) * maskf
    innov_out[...] = start
    var = rows(std)
    var = var * var * maskf
    sine = jnp.where(live, sine, 0.0)
    vals = jnp.concatenate([where3, dev, start, var, sine, jnp.zeros((3, slots), F32)], axis=0)
    got = lax.dot_general(split3(vals), onehot_of(rank, slots), NT, preferred_element_type=F32)
    got = got[0:16] + got[16:32] + got[32:48]
    dev, start = got[3:6], got[6:9]
    dev_out[...] = dev
    b0_out[...] = start
    var_out[...] = got[9:12]

    z = jnp.concatenate(blocks(got[2:3]), axis=0)
    angle = angle_of(jnp.concatenate(blocks(got[12:13]), axis=0))
    bounds = [
        jnp.min(z, axis=1, keepdims=True),
        jnp.max(z, axis=1, keepdims=True),
        jnp.min(angle, axis=1, keepdims=True),
        jnp.max(angle, axis=1, keepdims=True),
    ]
    sub = lax.broadcasted_iota(jnp.int32, (per, BLK), 0)
    col = lax.broadcasted_iota(jnp.int32, (per, BLK), 1)

    def spread(x, index):
        return jnp.sum(jnp.where(sub == index, x, 0.0), axis=0, keepdims=True)

    as_source = [spread(x, col & 7) for x in bounds]
    pad = jnp.zeros((1, slots - 4 * BLK), F32)
    hb_out[...] = jnp.concatenate(
        [dev * start, got[0:3], jnp.concatenate(as_source + [pad], axis=1), jnp.zeros((1, slots), F32)],
        axis=0,
    )
    as_target = [spread(x, col >> 3) for x in bounds]
    lane = lax.broadcasted_iota(jnp.int32, (1, BLK), 1)
    t = ((lane - 64) >> 3).astype(F32)
    tall = 1.0 * BLK * GRID_ROWS / CELLS
    floor = -0.9 + 1.8 * band.astype(F32) / bands
    step = 1.8 / bands / GRID_ROWS
    half_width = math.pi / sectors
    grid = [
        floor + step * (t * tall + 0.25),
        floor + step * (t * tall + tall - 0.25),
        jnp.full((1, BLK), -half_width, F32),
        jnp.full((1, BLK), half_width, F32),
    ]
    grid_end = 64 + 8 * (CELLS // BLK)
    rows = [
        jnp.where(lane < 64, x, jnp.where(lane < grid_end, g, 100.0)) for x, g in zip(as_target, grid)
    ]
    bounds_out[...] = jnp.concatenate(rows + [jnp.zeros((4, BLK), F32)], axis=0)


def blocks(wide):
    return [wide[:, b * BLK : (b + 1) * BLK] for b in range(wide.shape[1] // BLK)]


def active_blocks(source, target, bands):
    slo, shi, wlo, whi = source
    tlo, thi, vlo, vhi = target

    def radius(z):
        return jnp.sqrt(jnp.maximum(1.0 - z * z, 0.0))

    below, above = jnp.minimum(shi, thi), jnp.maximum(slo, tlo)
    fall = radius(below) - radius(above)
    apart = above - below
    lat = jnp.where(apart > 0.0, apart * apart + fall * fall, 0.0)
    gap = jnp.maximum(jnp.maximum(wlo, vlo) - jnp.minimum(whi, vhi), 0.0)
    gap2 = gap * gap
    small = radius(jnp.maximum(jnp.abs(slo), jnp.abs(shi))) * radius(
        jnp.maximum(jnp.abs(tlo), jnp.abs(thi))
    )
    bound = lat + gap2 * (1.0 - gap2 * (1.0 / 12.0)) * small
    reach = (0.6 / bands) ** 2
    return (bound < reach * 1.002 + 1e-6) & (tlo < 50.0) & (slo < 50.0)


def source_bounds(tiles, shifts, height):
    rows = []
    for k in range(4):
        parts = []
        for tile, shift in zip(tiles, shifts):
            row = tile[6:7, k * BLK : (k + 1) * BLK]
            parts.append(row + shift if k >= 2 else row)
        parts.append(jnp.full((height - len(tiles), BLK), 100.0, F32))
        rows.append(jnp.concatenate(parts, axis=0))
    return rows


def list_of(active, source, target, regions):
    height = active.shape[0]

    def exact(x, y, dims):
        return lax.dot_general(x.astype(BF16), y.astype(BF16), dims, preferred_element_type=F32)

    def ones(mask):
        return jnp.where(mask, 1.0, 0.0).astype(F32)

    def iota(shape, dim):
        return lax.broadcasted_iota(jnp.int32, shape, dim)

    act = ones(active)
    ahead = ones(iota((BLK, BLK), 0) < iota((BLK, BLK), 1))
    above = ones(iota((height, height), 1) < iota((height, height), 0))
    rows = jnp.sum(act, axis=1, keepdims=True)
    place = exact(act, ahead, NN) + exact(above, jnp.broadcast_to(rows, act.shape), NN)
    count = jnp.broadcast_to(jnp.sum(rows, axis=0, keepdims=True), (1, BLK))
    slot = jnp.where(active & (place < BLK), place, -1.0)
    index = iota((BLK, BLK), 0).astype(F32)
    picks = jnp.concatenate([ones(index == slot[r : r + 1]) for r in range(regions)], axis=1)
    names = [
        jnp.concatenate([x[r : r + 1].astype(F32) for r in range(regions)], axis=1)
        for x in (source, target)
    ]
    names = jnp.concatenate(names + [jnp.zeros((6, regions * BLK), F32)], axis=0)
    found = exact(names, picks, NT)
    entries = found[0:1] * 8.0 + found[1:2]
    return jnp.concatenate([entries, count, jnp.zeros((6, BLK), F32)], axis=0).astype(jnp.int32)


def near_active(tiles, where, frame, bounds):
    turn = 2.0 * math.pi / lax.axis_size("lon") * frame[4:5, 6:7]
    active = active_blocks(
        source_bounds(tiles, [(a - 1) * turn for c, a in where], 16),
        [bounds[k : k + 1, :] for k in range(4)],
        lax.axis_size("lat"),
    )
    lane = lax.broadcasted_iota(jnp.int32, active.shape, 1)
    region = lax.broadcasted_iota(jnp.int32, active.shape, 0)
    return active, lane, (lane & 7) + 8 * region, (lane >> 3) & 7


def long_list(active, source, target, regions, out, mask_v, mask_s, sem):
    mask_v[...] = jnp.where(active, source * 8 + target + 1, 0)
    copy = pltpu.make_async_copy(mask_v, mask_s, sem)
    copy.start()
    copy.wait()

    def step(i, k):
        entry = mask_s[i >> 7, i & 127]
        out[0, k] = entry - 1
        return k + jnp.where(entry > 0, 1, 0)

    lax.fori_loop(0, BLK * regions, step, 0)


def rho_of(tcol, sx, sy, sz):
    dx, dy, dz = tcol[0] - sx, tcol[1] - sy, tcol[2] - sz
    s = dx * dx + dy * dy + dz * dz
    r = lax.rsqrt(jnp.maximum(s, 1e-30))
    z = s * r
    inner = s * (((-0.25 * z + 0.5) * z + 0.625) * z - 5.0 / 3.0) + 1.0
    t = jnp.maximum(2.0 - z, 0.0)
    t = t * t
    u = z + 1.0
    outer = (t * t) * (u * u * (1.0 / 12.0) - 0.125) * r
    return jnp.where(s <= 1.0, inner, outer)


def to_frame(tile, row, frame):
    q = None
    for k in range(3):
        term = frame[:, k : k + 1] * (tile[row + k : row + k + 1, :] - frame[:, 3 + k : 4 + k])
        q = term if q is None else q + term
    return q


def set_columns(targets, tcol):
    part = lax.broadcasted_iota(jnp.int32, (24, 3 * BLK), 0)
    lane = lax.broadcasted_iota(jnp.int32, (24, 3 * BLK), 1)
    pick = jnp.where((part & 7) == lane // BLK, 1.0, 0.0).astype(BF16)
    for t, tile in enumerate(targets):
        turned = jnp.transpose(jnp.concatenate(parts_of(tile), axis=0)).astype(BF16)
        wide = lax.dot_general(turned, pick, NN, preferred_element_type=F32)
        for k in range(3):
            tcol[t, k] = wide[:, k * BLK : (k + 1) * BLK]


def fill_rows(q, tcol, t, out):
    sx, sy, sz = q[0:1], q[1:2], q[2:3]
    for i in range(0, BLK, ROWS):
        rho = rho_of([tcol[t, k, i : i + ROWS] for k in range(3)], sx, sy, sz)
        hi = rho.astype(BF16)
        out[i : i + ROWS, 0:BLK] = hi
        out[i : i + ROWS, BLK : 2 * BLK] = (rho - hi.astype(F32)).astype(BF16)


def fill_pair(entry, q_ref, tcol, out):
    fill_rows(q_ref[entry >> 3], tcol, entry & 7, out)


def parts_of(tile):
    hi = tile.astype(BF16).astype(F32)
    rest = tile - hi
    mid = rest.astype(BF16).astype(F32)
    return [hi, mid, rest - mid]


def set_values(rows, v_ref, first):
    v = jnp.concatenate(parts_of(rows) + [jnp.zeros(rows.shape, F32)], axis=0).astype(BF16)
    for b, part in enumerate(blocks(v)):
        v_ref[first + b, :, 0:BLK] = part
        v_ref[first + b, :, BLK : 2 * BLK] = part


def add_parts(out):
    return out[0:8] + out[8:16]


def total_of(acc):
    wide = jnp.concatenate([acc[t] for t in range(acc.shape[0])], axis=1)
    return wide[0:4] + wide[4:8]


def both_ways(lists, p, slot, cache, v_ref):
    n, t = lists[0, p] >> 3, lists[0, p] & 7
    rho = cache[slot]
    ahead = lax.dot_general(v_ref[n], rho, NT, preferred_element_type=F32)
    back = lax.dot_general(v_ref[t, :, 0:BLK], rho, NN, preferred_element_type=F32)
    return t, add_parts(ahead), n, add_parts(back[:, 0:BLK] + back[:, BLK : 2 * BLK])


def add_both(acc, found):
    for t, ahead, n, back in found:
        acc[t] += ahead
        acc[n] += back


def own_first_kernel(
    frame, hb, bounds, q_out, tcol_out, lists_out, cache_out, acc, v_ref, lists_v, sem
):
    tile = hb[...]
    tiles = blocks(to_frame(tile, 3, frame[...]))
    per = len(tiles)
    active = active_blocks(
        source_bounds([tile], [0.0], 8), [bounds[k : k + 1, :] for k in range(4)], lax.axis_size("lat")
    )
    lane = lax.broadcasted_iota(jnp.int32, active.shape, 1)
    source, target = lane & 7, (lane >> 3) & 7
    lists_v[...] = list_of(active & (lane < 64) & (target < source), source, target, 1)
    copy = pltpu.make_async_copy(lists_v, lists_out, sem)
    copy.start()
    set_values(tile[0:4], v_ref, 0)
    for b, part in enumerate(tiles):
        q_out[b] = part
    set_columns(tiles, tcol_out)

    def fill_own(b):
        fill_pair(b * 9, q_out, tcol_out, cache_out.at[b])

    def multiply_own(b):
        acc[b] = add_parts(lax.dot_general(v_ref[b], cache_out[b], NT, preferred_element_type=F32))

    def step_own(b, _):
        multiply_own(b - 1)
        fill_own(b)
        return 0

    fill_own(0)
    lax.fori_loop(1, per, step_own, 0)
    multiply_own(per - 1)
    copy.wait()
    count = lists_out[1, 0]
    steps = jnp.maximum((count + 1) // 2, 1)

    def fill(i):
        for p in (2 * i, 2 * i + 1):
            fill_pair(lists_out[0, p], q_out, tcol_out, cache_out.at[per + p])

    def multiply(i):
        add_both(acc, [both_ways(lists_out, p, per + p, cache_out, v_ref) for p in (2 * i, 2 * i + 1)])

    def step(i, _):
        multiply(i - 1)
        fill(i)
        return 0

    fill(0)
    lax.fori_loop(1, steps, step, 0)
    for k in range(UNROLL):
        cache_out[per + count + k] = jnp.zeros(cache_out.shape[1:], BF16)
    multiply(steps - 1)


def own_times_kernel(lists, cache, u, acc, v_ref):
    set_values(u[0:4, :], v_ref, 0)
    per = acc.shape[0]
    for b in range(per):
        acc[b] = add_parts(lax.dot_general(v_ref[b], cache[b], NT, preferred_element_type=F32))
    half = UNROLL // 2

    def group(i, _):
        places = [i * half + k for k in range(half)]
        add_both(acc, [both_ways(lists, p, per + p, cache, v_ref) for p in places])
        return 0

    lax.fori_loop(0, (lists[1, 0] + half - 1) // half, group, 0)


OTHERS = [(0, 0), (0, 2), (1, 0), (1, 1), (1, 2), (2, 0), (2, 1), (2, 2)]


def near_first_kernel(
    frame, bounds, corr, tcol, mid, three, four, acc_own, dev, var, field,
    q_out, lists_out, long_out, cache_out, img_out, nxt_out, u_out,
    v_ref, acc, pair, lists_v, mask_v, mask_s, sem, sem_long,
):
    halo = (mid, three, four)
    per = mid.shape[2] // BLK
    turned = frame[...]
    tiles = [halo[c][a] for c, a in OTHERS]
    regions = len(tiles)
    active, lane, source, target = near_active(tiles, OTHERS, turned, bounds)
    active = active & (lane < 64)
    lists_v[...] = list_of(active, source, target, regions)
    copy = pltpu.make_async_copy(lists_v, lists_out, sem)
    copy.start()
    for r in range(regions):
        for b, part in enumerate(blocks(to_frame(tiles[r], 3, turned))):
            q_out[r * per + b] = part
        set_values(tiles[r][0:4], v_ref, r * per)
    acc[...] = acc_own[...]
    copy.wait()
    count = lists_out[1, 0]

    @pl.when(count > KEPT)
    def _():
        long_list(active, source, target, regions, long_out, mask_v, mask_s, sem_long)

    kept = jnp.minimum(count, cache_out.shape[0] - UNROLL)
    steps = jnp.maximum((kept + 1) // 2, 1)

    def fill(i):
        for p in (2 * i, 2 * i + 1):
            fill_pair(lists_out[0, p], q_out, tcol, cache_out.at[p])

    def multiply(i):
        found = []
        for p in (2 * i, 2 * i + 1):
            n = lists_out[0, p] >> 3
            found.append(lax.dot_general(v_ref[n], cache_out[p], NT, preferred_element_type=F32))
        for k in range(2):
            acc[lists_out[0, 2 * i + k] & 7] += add_parts(found[k])

    def step(i, _):
        multiply(i - 1)
        fill(i)
        return 0

    fill(0)
    lax.fori_loop(1, steps, step, 0)
    for k in range(UNROLL):
        cache_out[kept + k] = jnp.zeros(cache_out.shape[1:], BF16)
    multiply(steps - 1)
    extra_pairs(kept, count, long_out, q_out, tcol, v_ref, acc, pair)
    field = field[...]
    dev = dev[...]
    image = dev * mix(corr, total_of(acc)) + var[...] * field
    give_next(image, field, dev, img_out, nxt_out, u_out)


def cells_list_kernel(
    frame, bounds, mid, three, four, lists_out, long_out, lists_v, mask_v, mask_s, sem, sem_long
):
    halo = (mid, three, four)
    where = [(0, 1)] + OTHERS
    tiles = [halo[c][a] for c, a in where]
    active, lane, source, target = near_active(tiles, where, frame[...], bounds)
    active = active & (lane >= 64)
    lists_v[...] = list_of(active, source, target, len(where))
    copy = pltpu.make_async_copy(lists_v, lists_out, sem)
    copy.start()
    copy.wait()

    @pl.when(lists_out[1, 0] > KEPT)
    def _():
        long_list(active, source, target, len(where), long_out, mask_v, mask_s, sem_long)


def mix(corr, total):
    out = None
    for c in range(3):
        term = corr[:, c : c + 1] * total[c : c + 1, :]
        out = term if out is None else out + term
    return out


def extra_pairs(kept, count, long, q_ref, tcol, v_ref, acc, pair):
    def extra(p, _):
        entry = long[0, p]
        fill_pair(entry, q_ref, tcol, pair)
        out = lax.dot_general(v_ref[entry >> 3], pair[...], NT, preferred_element_type=F32)
        acc[entry & 7] += add_parts(out)
        return 0

    lax.fori_loop(kept, count, extra, 0)


def give_next(image, field, dev, img_out, nxt_out, u_out):
    nxt = image - SHIFT * field
    img_out[...] = image
    nxt_out[...] = nxt
    u_out[...] = jnp.concatenate([dev * nxt, jnp.zeros((1, nxt.shape[1]), F32)], axis=0)


def near_times_kernel(
    last, lists, long, corr, cache, q_ref, tcol, acc_own, um, us, un, dev, var, field, *refs
):
    refs, (v_ref, acc, pair) = refs[:-3], refs[-3:]
    outs = refs[-1:] if last else refs
    halo = (um, us, un)
    per = acc.shape[0]
    for k, (c, a) in enumerate(OTHERS):
        set_values(halo[c][a, 0:4, :], v_ref, k * per)
    acc[...] = acc_own[...]
    count = lists[1, 0]
    kept = jnp.minimum(count, cache.shape[0] - UNROLL)

    def group(i, _):
        found = []
        for k in range(UNROLL):
            p = i * UNROLL + k
            n = lists[0, p] >> 3
            found.append(lax.dot_general(v_ref[n], cache[p], NT, preferred_element_type=F32))
        for k in range(UNROLL):
            acc[lists[0, i * UNROLL + k] & 7] += add_parts(found[k])
        return 0

    lax.fori_loop(0, (kept + UNROLL - 1) // UNROLL, group, 0)

    extra_pairs(kept, count, long, q_ref, tcol, v_ref, acc, pair)
    field = field[...]
    dev = dev[...]
    image = dev * mix(corr, total_of(acc)) + var[...] * field
    if last:
        b0, b1, a0, a1 = [ref[...] for ref in refs[:4]]
        sums_out(b0, b1, field, a0, a1, image, outs[0])
    else:
        give_next(image, field, dev, *outs)


def sums_out(b0, b1, b2, a0, a1, a2, out):
    pairs = [(b0, a0), (b0, a1), (b0, a2), (b1, a1), (b1, a2), (b2, a2), (b0, b0), (b1, b0), (b2, b0)]
    rows = []
    for x, y in pairs:
        prod = blocks(x * y)
        while len(prod) > 1:
            prod = [prod[k] + prod[k + 1] for k in range(0, len(prod), 2)]
        rows.append(jnp.sum(prod[0], axis=0, keepdims=True))
    rows.append(jnp.zeros((16 - len(rows), BLK), F32))
    totals = jnp.sum(jnp.concatenate(rows, axis=0), axis=1, keepdims=True)
    sub = lax.broadcasted_iota(jnp.int32, (16, 16), 0)
    col = lax.broadcasted_iota(jnp.int32, (16, 16), 1)
    row = jnp.sum(jnp.where(sub == col, totals, 0.0), axis=0, keepdims=True)
    out[...] = jnp.broadcast_to(row[None], out.shape)


def pack_kernel(q_own, q_near, *refs):
    out = refs[-1]
    fields = [refs[3 * f : 3 * f + 3] for f in range(3)]
    per = q_own.shape[0]
    for f in range(3):
        for r, (c, a) in enumerate([(0, 1)] + OTHERS):
            tile = fields[f][c][a, 0:4, :]
            for b, part in enumerate(blocks(tile)):
                out[r * per + b, 3 * f : 3 * f + 3, :] = part[0:3]
    for b in range(per):
        out[b, 9:12, :] = q_own[b, 0:3, :]
    for n in range(q_near.shape[0]):
        out[per + n, 9:12, :] = q_near[n, 0:3, :]
    for n in range(out.shape[0]):
        out[n, 12:16, :] = jnp.zeros((4, BLK), F32)


def grid_kernel(lists, long, corr, frame, packed, bgg, g_out, tcol, rho, acc):
    cells = g_out.shape[2]
    columns = cells // GRID_ROWS
    bands, sectors = lax.axis_size("lat"), lax.axis_size("lon")
    cell = lax.broadcasted_iota(jnp.int32, (8, cells), 1)
    row = lax.broadcasted_iota(jnp.int32, (8, cells), 0)
    frac_lat = ((cell // columns).astype(F32) + 0.5) / GRID_ROWS
    frac_lon = ((cell % columns).astype(F32) + 0.5) / columns
    band, sector = frame[0:1, 6:7], frame[1:2, 6:7]
    sinlat = -0.9 + 1.8 * (band + frac_lat) / bands
    longitude = 2.0 * math.pi * (sector + frac_lon) / sectors
    coslat = jnp.sqrt(1.0 - sinlat * sinlat)
    point = jnp.where(row == 0, coslat * jnp.cos(longitude), coslat * jnp.sin(longitude))
    point = jnp.where(row == 2, sinlat, point)
    set_columns(blocks(to_frame(point, 0, frame[...])), tcol)
    acc[...] = jnp.zeros(acc.shape, F32)
    count = lists[1, 0]
    short = jnp.minimum(count, KEPT)

    def one(entry, weight, out):
        near = packed[entry >> 3]
        fill_rows(near[9:12], tcol, entry & 7, out)
        v = jnp.concatenate(parts_of(near * weight), axis=0).astype(BF16)
        v = jnp.concatenate([v, v], axis=1)
        got = lax.dot_general(v, out[...], NT, preferred_element_type=F32)
        return got[0:16] + got[16:32] + got[32:48]

    def group(i, _):
        found = []
        for k in range(GROUP):
            p = i * GROUP + k
            weight = jnp.where(p < short, 1.0, 0.0).astype(F32)
            found.append(one(lists[0, p], weight, rho.at[k]))
        for k in range(GROUP):
            acc[lists[0, i * GROUP + k] & 7] += found[k]
        return 0

    lax.fori_loop(0, (short + GROUP - 1) // GROUP, group, 0)

    def extra(p, _):
        entry = long[0, p]
        acc[entry & 7] += one(entry, 1.0, rho.at[0])
        return 0

    lax.fori_loop(short, count, extra, 0)
    total = jnp.concatenate([acc[t] for t in range(acc.shape[0])], axis=1)
    dev = jnp.concatenate([bgg[0], bgg[1], bgg[2]], axis=0)
    for f in range(3):
        g_out[f] = dev * mix(corr, total[3 * f : 3 * f + 3])


def unsort_kernel(rank, b1, b2, w_out):
    slots = rank.shape[1]
    vals = jnp.concatenate([b1[...], b2[...], jnp.zeros((10, slots), F32)], axis=0)
    back = lax.dot_general(split3(vals), onehot_of(rank[...], slots), NN, preferred_element_type=F32)
    back = back[0:16] + back[16:32] + back[32:48]
    w_out[0] = back[0:3]
    w_out[1] = back[3:6]


def final_kernel(parts, innov, w, g, w_out, g_out, w_buf, g_buf, sems):
    sums = parts[...]
    while sums.shape[0] > 1:
        half = sums.shape[0] // 2
        sums = sums[:half] + sums[half:]
    sums = sums[0]
    lane = lax.broadcasted_iota(jnp.int32, sums.shape, 1)
    m00, m01, m02, m11, m12, m22, g0, g1, g2 = [
        jnp.sum(jnp.where(lane == k, sums, 0.0), axis=1, keepdims=True) for k in range(9)
    ]
    l10, l20 = m01 / m00, m02 / m00
    d1 = m11 - l10 * m01
    e12 = m12 - l10 * m02
    ok1 = d1 > 1e-6 * m11
    safe1 = jnp.where(ok1, d1, 1.0)
    l21 = jnp.where(ok1, e12 / safe1, 0.0)
    d2 = m22 - l20 * m02 - l21 * e12
    ok2 = ok1 & (d2 > 1e-6 * m22)
    y1 = g1 - l10 * g0
    y2 = g2 - l20 * g0 - l21 * y1
    c2 = jnp.where(ok2, y2 / jnp.where(ok2, d2, 1.0), 0.0)
    c1 = jnp.where(ok1, y1 / safe1, 0.0) - l21 * c2
    c0 = g0 / m00 - l10 * c1 - l20 * c2
    for k in range(3):
        w_buf[k] = c0 * innov[k : k + 1, :] + c1 * w[0, k : k + 1] + c2 * w[1, k : k + 1]
        g_buf[k] = c0 * g[0, k : k + 1] + c1 * g[1, k : k + 1] + c2 * g[2, k : k + 1]
    copies = [
        pltpu.make_async_copy(w_buf, w_out, sems.at[0]),
        pltpu.make_async_copy(g_buf, g_out, sems.at[1]),
    ]
    for copy in copies:
        copy.start()
    for copy in copies:
        copy.wait()


def swap(x, axis, first):
    count = lax.axis_size(axis)
    pairs = []
    for i in range(first, count, 2):
        pairs += [(i, (i + 1) % count), ((i + 1) % count, i)]
    return lax.ppermute(x, axis, pairs)


def frames(bands, sectors):
    table = np.zeros((bands, sectors, 8, 8), np.float64)
    half = 0.3 / bands
    for i in range(bands):
        s = -0.9 + 1.8 * (i + 0.5) / bands
        c = math.sqrt(1.0 - s * s)
        for j in range(sectors):
            lam = 2.0 * math.pi * (j + 0.5) / sectors
            cl, sl = math.cos(lam), math.sin(lam)
            table[i, j, :3, :3] = np.array([[-sl, cl, 0.0], [-s * cl, -s * sl, c], [c * cl, c * sl, s]]) / half
            table[i, j, :, 3:6] = [c * cl, c * sl, s]
            table[i, j, :5, 6] = [i, j, -sl, cl, 2 * (j % 2) - 1]
    return table.astype(np.float32)


VM = pl.BlockSpec(memory_space=pltpu.VMEM)
SM = pl.BlockSpec(memory_space=pltpu.SMEM)
HB = pl.BlockSpec(memory_space=pltpu.HBM)
LISTS = pltpu.VMEM((8, BLK), jnp.int32)
PAIR = pltpu.VMEM((BLK, 2 * BLK), BF16)


def arr(*shape, dtype=F32):
    return jax.ShapeDtypeStruct(shape, dtype)


def call(kernel, name, ins, outs, scratch, flops, out_specs=None, vmem=VLIM):
    return pl.pallas_call(
        kernel,
        out_shape=outs,
        in_specs=ins,
        out_specs=[VM] * len(outs) if out_specs is None else out_specs,
        scratch_shapes=scratch,
        name=name,
        compiler_params=pltpu.CompilerParams(vmem_limit_bytes=vmem),
        cost_estimate=pl.CostEstimate(flops=flops, bytes_accessed=1 << 20, transcendentals=0),
    )


def tie(first, *rest):
    return lax.optimization_barrier((first, *rest))[0]


def per_device(tile_counts, obs_pos, innovation, bg_std_obs, obs_std, channel_corr, bg_std_grid):
    bands, sectors = lax.axis_size("lat"), lax.axis_size("lon")
    slots = obs_pos.shape[3]
    cells = bg_std_grid.shape[3]
    per = slots // BLK
    grids = cells // BLK
    table = pltpu.with_memory_space_constraint(jnp.asarray(frames(bands, sectors)), pltpu.HBM)

    def flat(x):
        return pltpu.with_memory_space_constraint(x.reshape(3, 1, x.shape[3]), pltpu.HBM)

    obs_in = pltpu.VMEM((3, 1, slots), F32)
    three = arr(3, slots)
    hb, dev, var, b0, rank, frame, bounds, innov, bgg, corr = call(
        sort_kernel,
        "sort",
        [SM] + [HB] * 7,
        [arr(8, slots), three, three, three, arr(1, slots), arr(8, 8), arr(8, BLK), three]
        + [arr(3, 1, cells), arr(3, 3)],
        [obs_in] * 4 + [pltpu.SemaphoreType.DMA((7,))],
        10**8,
    )(
        tile_counts, table, flat(obs_pos), flat(innovation), flat(bg_std_obs), flat(obs_std),
        flat(bg_std_grid), pltpu.with_memory_space_constraint(channel_corr, pltpu.HBM),
    )

    def exchange(block, beside, after):
        one, two = swap(block, "lon", 0), swap(block, "lon", 1)
        first = beside()
        mid = tie(jnp.stack([one, block, two]), first)
        three, four = swap(mid, "lat", 0), swap(mid, "lat", 1)
        second = after(first)
        three, four, second = lax.optimization_barrier((three, four, second))
        return (mid, three, four), first, second

    off = per * (per - 1) // 2

    def own_first():
        return call(
            own_first_kernel,
            "own_first",
            [VM] * 3,
            [
                arr(per, 8, BLK),
                arr(per, 3, BLK, BLK),
                arr(8, BLK, dtype=jnp.int32),
                arr(per + off + UNROLL, BLK, 2 * BLK, dtype=BF16),
                arr(per, 8, BLK),
            ],
            [pltpu.VMEM((per, 16, 2 * BLK), BF16), LISTS, pltpu.SemaphoreType.DMA],
            10**9,
            [VM, VM, SM, VM, VM],
        )(frame, hb, bounds)

    def own_times(filled, u):
        return call(
            own_times_kernel,
            "own_times",
            [SM] + [VM] * 2,
            [arr(per, 8, BLK)],
            [pltpu.VMEM((per, 16, 2 * BLK), BF16)],
            10**8,
        )(*filled[2:4], u)[0]

    near0, filled, _ = exchange(hb, own_first, lambda filled: filled[4])
    q_own, tcol = filled[:2]
    full = 8 * per * per
    long_scratch = [LISTS, pltpu.VMEM((16, BLK), jnp.int32), pltpu.SMEM((16, BLK), jnp.int32)]
    long_scratch += [pltpu.SemaphoreType.DMA] * 2
    near_scratch = [
        pltpu.VMEM((8 * per, 16, 2 * BLK), BF16),
        pltpu.VMEM((per, 8, BLK), F32),
        PAIR,
    ]
    next_outs = [three, three, arr(4, slots)]
    q_near, lists, long, cache_near, a0, b1, u1 = call(
        near_first_kernel,
        "near_first",
        [VM] * 11,
        [
            arr(8 * per, 8, BLK),
            arr(8, BLK, dtype=jnp.int32),
            arr(1, 10 * BLK, dtype=jnp.int32),
            arr(min(full, KEPT) + UNROLL, BLK, 2 * BLK, dtype=BF16),
        ]
        + next_outs,
        near_scratch + long_scratch,
        10**9,
        [VM, SM, SM, VM, VM, VM, VM],
    )(frame, bounds, corr, tcol, *near0, filled[4], dev, var, b0)

    def near_times(halo, acc, field, *earlier):
        last = len(earlier) > 0
        outs = [arr(bands * sectors, 1, 16)] if last else next_outs
        return call(
            functools.partial(near_times_kernel, last),
            "near_times",
            [SM] * 2 + [VM] * (11 + len(earlier)),
            outs,
            near_scratch,
            10**8,
        )(lists, long, corr, cache_near, q_near, tcol, acc, *halo, dev, var, field, *earlier)

    def list_cells(_):
        return call(
            cells_list_kernel,
            "cells_list",
            [VM] * 5,
            [arr(8, BLK, dtype=jnp.int32), arr(1, 10 * BLK, dtype=jnp.int32)],
            long_scratch,
            10**8,
            [SM, SM],
        )(frame, bounds, *near0)

    near1, acc, cells_lists = exchange(u1, lambda: own_times(filled, u1), list_cells)
    a1, b2, u2 = near_times(near1, acc, b1)
    near2, acc, _ = exchange(u2, lambda: own_times(filled, u2), lambda acc: acc)
    (copies,) = near_times(near2, acc, b2, b0, b1, a0, a1)
    (packed,) = call(
        pack_kernel, "pack", [VM] * 11, [arr(9 * per, 16, BLK)], [], 10**7
    )(q_own, q_near, *near0, *near1, *near2)
    copies, packed = lax.optimization_barrier((copies, packed))
    parts = lax.all_to_all(copies, ("lat", "lon"), 0, 0, tiled=True)
    (parts_g,) = call(
        grid_kernel,
        "grid",
        [SM] * 2 + [VM] * 4,
        [arr(3, 3, cells)],
        [
            pltpu.VMEM((cells // BLK, 3, BLK, BLK), F32),
            pltpu.VMEM((GROUP, BLK, 2 * BLK), BF16),
            pltpu.VMEM((cells // BLK, 16, BLK), F32),
        ],
        10**9,
    )(*cells_lists, corr, frame, packed, bgg)
    (parts_w,) = call(unsort_kernel, "unsort", [VM] * 3, [arr(2, 3, slots)], [], 10**8)(rank, b1, b2)
    weights, increment = call(
        final_kernel,
        "final",
        [VM] * 4,
        [arr(3, 1, slots), arr(3, 1, cells)],
        [obs_in, pltpu.VMEM((3, 1, cells), F32), pltpu.SemaphoreType.DMA((2,))],
        10**6,
        [HB, HB],
    )(parts, innov, parts_w, parts_g)
    return weights.reshape(1, 1, 3, slots), increment.reshape(1, 1, 3, cells)


def solution(mesh):
    spec = P("lat", "lon", None, None)
    return jax.shard_map(
        per_device,
        mesh=mesh,
        in_specs=(P("lat", "lon"), spec, spec, spec, spec, P(), spec),
        out_specs=(spec, spec),
        check_vma=False,
    )
```

```python
import functools
import math

import jax
import jax.numpy as jnp
import numpy as np
from jax import lax
from jax.experimental import pallas as pl
from jax.experimental.pallas import tpu as pltpu
from jax.sharding import PartitionSpec as P

OBS_TILE = 512
GRID_ROWS = 16
BLK = 128
SHIFT = 0.5
FAR = 64.0
NT = (((1,), (1,)), ((), ()))
NN = (((1,), (0,)), ((), ()))
F32 = jnp.float32
BF16 = jnp.bfloat16
VLIM = 8 * 1024 * 1024
UNROLL = 8
ROWS = 32
GROUP = 4
KEPT = 96
EARLY = 14
CELLS = 512


def split3(x):
    hi = x.astype(BF16)
    rest = x - hi.astype(F32)
    mid = rest.astype(BF16)
    low = (rest - mid.astype(F32)).astype(BF16)
    return jnp.concatenate([hi, mid, low], axis=0)


def col_of(row):
    return jnp.transpose(jnp.broadcast_to(row, (8, row.shape[1])))[:, 0:1]


def rank_of(key, slots):
    col = col_of(key)
    parts = []
    for j in range(slots // BLK):
        kj = key[:, j * BLK : (j + 1) * BLK]
        total = jnp.zeros((8, BLK), F32)
        for i in range(slots // BLK):
            ki = jnp.broadcast_to(col[i * BLK : (i + 1) * BLK, :], (BLK, BLK))
            if i < j:
                before = ki <= kj
            elif i > j:
                before = ki < kj
            else:
                first = lax.broadcasted_iota(jnp.int32, (BLK, BLK), 0) < lax.broadcasted_iota(
                    jnp.int32, (BLK, BLK), 1
                )
                before = (ki < kj) | ((ki == kj) & first)
            ones = jnp.where(before, 1.0, 0.0).astype(F32)
            total = total + jnp.sum(ones.reshape(BLK // 8, 8, BLK), axis=0)
        parts.append(jnp.sum(total, axis=0, keepdims=True))
    return jnp.concatenate(parts, axis=1)


def onehot_of(rank, slots):
    place = lax.broadcasted_iota(jnp.int32, (slots, slots), 0).astype(F32)
    return jnp.where(place == rank, 1.0, 0.0).astype(BF16)


def angle_of(x):
    x2 = x * x
    return x * (1.0 + x2 * (1.0 / 6.0 + x2 * (3.0 / 40.0 + x2 * (15.0 / 336.0))))


def sort_kernel(
    count, table, pos_in, innov_in, bg_in, std_in, bgg_in, corr_in,
    hb_out, dev_out, var_out, b0_out, rank_out, frame_out, bounds_out, innov_out, bgg_out, corr_out,
    pos, innov, bg, std, sems,
):
    bands, sectors = lax.axis_size("lat"), lax.axis_size("lon")
    band, sector = lax.axis_index("lat"), lax.axis_index("lon")
    pairs = [
        (table.at[band, sector], frame_out),
        (pos_in, pos),
        (innov_in, innov),
        (bg_in, bg),
        (std_in, std),
        (bgg_in, bgg_out),
        (corr_in, corr_out),
    ]
    copies = [pltpu.make_async_copy(x, y, sems.at[k]) for k, (x, y) in enumerate(pairs)]
    for copy in copies:
        copy.start()
    copies[0].wait()
    copies[1].wait()

    def rows(ref):
        return jnp.concatenate([ref[0], ref[1], ref[2]], axis=0)

    slots = pos.shape[2]
    per = slots // BLK
    frame = frame_out[...]
    live_n = count[0, 0] * OBS_TILE
    lane = lax.broadcasted_iota(jnp.int32, (1, slots), 1)
    live = lane < live_n
    px, py, pz = pos[0], pos[1], pos[2]
    key = jnp.where(live, pz, 10.0)
    first = rank_of(key, slots)
    strip = jnp.where(first * 2.0 >= live_n.astype(F32), 8.0, 0.0)
    east = frame[2:3, 6:7] * px + frame[3:4, 6:7] * py
    sine = east * lax.rsqrt(jnp.maximum(px * px + py * py, 1e-6))
    rank = rank_of(jnp.where(live, strip + sine, 100.0), slots)
    rank_out[...] = rank
    for copy in copies[2:]:
        copy.wait()
    maskf = jnp.where(live, 1.0, 0.0).astype(F32)
    where3 = jnp.where(live, rows(pos), FAR)
    dev = rows(bg) * maskf
    start = rows(innov) * maskf
    innov_out[...] = start
    var = rows(std)
    var = var * var * maskf
    sine = jnp.where(live, sine, 0.0)
    vals = jnp.concatenate([where3, dev, start, var, sine, jnp.zeros((3, slots), F32)], axis=0)
    got = lax.dot_general(split3(vals), onehot_of(rank, slots), NT, preferred_element_type=F32)
    got = got[0:16] + got[16:32] + got[32:48]
    dev, start = got[3:6], got[6:9]
    dev_out[...] = dev
    b0_out[...] = start
    var_out[...] = got[9:12]

    z = jnp.concatenate(blocks(got[2:3]), axis=0)
    angle = angle_of(jnp.concatenate(blocks(got[12:13]), axis=0))
    bounds = [
        jnp.min(z, axis=1, keepdims=True),
        jnp.max(z, axis=1, keepdims=True),
        jnp.min(angle, axis=1, keepdims=True),
        jnp.max(angle, axis=1, keepdims=True),
    ]
    sub = lax.broadcasted_iota(jnp.int32, (per, BLK), 0)
    col = lax.broadcasted_iota(jnp.int32, (per, BLK), 1)

    def spread(x, index):
        return jnp.sum(jnp.where(sub == index, x, 0.0), axis=0, keepdims=True)

    as_source = [spread(x, col & 7) for x in bounds]
    pad = jnp.zeros((1, slots - 4 * BLK), F32)
    hb_out[...] = jnp.concatenate(
        [dev * start, got[0:3], jnp.concatenate(as_source + [pad], axis=1), jnp.zeros((1, slots), F32)],
        axis=0,
    )
    as_target = [spread(x, col >> 3) for x in bounds]
    lane = lax.broadcasted_iota(jnp.int32, (1, BLK), 1)
    t = ((lane - 64) >> 3).astype(F32)
    tall = 1.0 * BLK * GRID_ROWS / CELLS
    floor = -0.9 + 1.8 * band.astype(F32) / bands
    step = 1.8 / bands / GRID_ROWS
    half_width = math.pi / sectors
    grid = [
        floor + step * (t * tall + 0.25),
        floor + step * (t * tall + tall - 0.25),
        jnp.full((1, BLK), -half_width, F32),
        jnp.full((1, BLK), half_width, F32),
    ]
    grid_end = 64 + 8 * (CELLS // BLK)
    rows = [
        jnp.where(lane < 64, x, jnp.where(lane < grid_end, g, 100.0)) for x, g in zip(as_target, grid)
    ]
    bounds_out[...] = jnp.concatenate(rows + [jnp.zeros((4, BLK), F32)], axis=0)


def blocks(wide):
    return [wide[:, b * BLK : (b + 1) * BLK] for b in range(wide.shape[1] // BLK)]


def active_blocks(source, target, bands):
    slo, shi, wlo, whi = source
    tlo, thi, vlo, vhi = target

    def radius(z):
        return jnp.sqrt(jnp.maximum(1.0 - z * z, 0.0))

    below, above = jnp.minimum(shi, thi), jnp.maximum(slo, tlo)
    fall = radius(below) - radius(above)
    apart = above - below
    lat = jnp.where(apart > 0.0, apart * apart + fall * fall, 0.0)
    gap = jnp.maximum(jnp.maximum(wlo, vlo) - jnp.minimum(whi, vhi), 0.0)
    gap2 = gap * gap
    small = radius(jnp.maximum(jnp.abs(slo), jnp.abs(shi))) * radius(
        jnp.maximum(jnp.abs(tlo), jnp.abs(thi))
    )
    bound = lat + gap2 * (1.0 - gap2 * (1.0 / 12.0)) * small
    reach = (0.6 / bands) ** 2
    return (bound < reach * 1.002 + 1e-6) & (tlo < 50.0) & (slo < 50.0)


def source_bounds(tiles, shifts, height):
    rows = []
    for k in range(4):
        parts = []
        for tile, shift in zip(tiles, shifts):
            row = tile[6:7, k * BLK : (k + 1) * BLK]
            parts.append(row + shift if k >= 2 else row)
        parts.append(jnp.full((height - len(tiles), BLK), 100.0, F32))
        rows.append(jnp.concatenate(parts, axis=0))
    return rows


def list_of(active, source, target, regions):
    height = active.shape[0]

    def exact(x, y, dims):
        return lax.dot_general(x.astype(BF16), y.astype(BF16), dims, preferred_element_type=F32)

    def ones(mask):
        return jnp.where(mask, 1.0, 0.0).astype(F32)

    def iota(shape, dim):
        return lax.broadcasted_iota(jnp.int32, shape, dim)

    act = ones(active)
    ahead = ones(iota((BLK, BLK), 0) < iota((BLK, BLK), 1))
    above = ones(iota((height, height), 1) < iota((height, height), 0))
    rows = jnp.sum(act, axis=1, keepdims=True)
    place = exact(act, ahead, NN) + exact(above, jnp.broadcast_to(rows, act.shape), NN)
    count = jnp.broadcast_to(jnp.sum(rows, axis=0, keepdims=True), (1, BLK))
    slot = jnp.where(active & (place < BLK), place, -1.0)
    index = iota((BLK, BLK), 0).astype(F32)
    picks = jnp.concatenate([ones(index == slot[r : r + 1]) for r in range(regions)], axis=1)
    names = [
        jnp.concatenate([x[r : r + 1].astype(F32) for r in range(regions)], axis=1)
        for x in (source, target)
    ]
    names = jnp.concatenate(names + [jnp.zeros((6, regions * BLK), F32)], axis=0)
    found = exact(names, picks, NT)
    entries = found[0:1] * 8.0 + found[1:2]
    return jnp.concatenate([entries, count, jnp.zeros((6, BLK), F32)], axis=0).astype(jnp.int32)


def near_active(tiles, where, frame, bounds):
    turn = 2.0 * math.pi / lax.axis_size("lon") * frame[4:5, 6:7]
    active = active_blocks(
        source_bounds(tiles, [(a - 1) * turn for c, a in where], 16),
        [bounds[k : k + 1, :] for k in range(4)],
        lax.axis_size("lat"),
    )
    lane = lax.broadcasted_iota(jnp.int32, active.shape, 1)
    region = lax.broadcasted_iota(jnp.int32, active.shape, 0)
    return active, lane, (lane & 7) + 8 * region, (lane >> 3) & 7


def long_list(active, source, target, regions, out, mask_v, mask_s, sem):
    mask_v[...] = jnp.where(active, source * 8 + target + 1, 0)
    copy = pltpu.make_async_copy(mask_v, mask_s, sem)
    copy.start()
    copy.wait()

    def step(i, k):
        entry = mask_s[i >> 7, i & 127]
        out[0, k] = entry - 1
        return k + jnp.where(entry > 0, 1, 0)

    lax.fori_loop(0, BLK * regions, step, 0)


def rho_of(tcol, sx, sy, sz):
    dx, dy, dz = tcol[0] - sx, tcol[1] - sy, tcol[2] - sz
    s = dx * dx + dy * dy + dz * dz
    r = lax.rsqrt(jnp.maximum(s, 1e-30))
    z = s * r
    inner = s * (((-0.25 * z + 0.5) * z + 0.625) * z - 5.0 / 3.0) + 1.0
    t = jnp.maximum(2.0 - z, 0.0)
    t = t * t
    u = z + 1.0
    outer = (t * t) * (u * u * (1.0 / 12.0) - 0.125) * r
    return jnp.where(s <= 1.0, inner, outer)


def to_frame(tile, row, frame):
    q = None
    for k in range(3):
        term = frame[:, k : k + 1] * (tile[row + k : row + k + 1, :] - frame[:, 3 + k : 4 + k])
        q = term if q is None else q + term
    return q


def set_columns(targets, tcol):
    part = lax.broadcasted_iota(jnp.int32, (24, 3 * BLK), 0)
    lane = lax.broadcasted_iota(jnp.int32, (24, 3 * BLK), 1)
    pick = jnp.where((part & 7) == lane // BLK, 1.0, 0.0).astype(BF16)
    for t, tile in enumerate(targets):
        turned = jnp.transpose(jnp.concatenate(parts_of(tile), axis=0)).astype(BF16)
        wide = lax.dot_general(turned, pick, NN, preferred_element_type=F32)
        for k in range(3):
            tcol[t, k] = wide[:, k * BLK : (k + 1) * BLK]


def fill_rows(q, tcol, t, out):
    sx, sy, sz = q[0:1], q[1:2], q[2:3]
    for i in range(0, BLK, ROWS):
        rho = rho_of([tcol[t, k, i : i + ROWS] for k in range(3)], sx, sy, sz)
        hi = rho.astype(BF16)
        out[i : i + ROWS, 0:BLK] = hi
        out[i : i + ROWS, BLK : 2 * BLK] = (rho - hi.astype(F32)).astype(BF16)


def fill_pair(entry, q_ref, tcol, out):
    fill_rows(q_ref[entry >> 3], tcol, entry & 7, out)


def parts_of(tile):
    hi = tile.astype(BF16).astype(F32)
    rest = tile - hi
    mid = rest.astype(BF16).astype(F32)
    return [hi, mid, rest - mid]


def set_values(rows, v_ref, first):
    v = jnp.concatenate(parts_of(rows) + [jnp.zeros(rows.shape, F32)], axis=0).astype(BF16)
    for b, part in enumerate(blocks(v)):
        v_ref[first + b, :, 0:BLK] = part
        v_ref[first + b, :, BLK : 2 * BLK] = part


def add_parts(out):
    return out[0:8] + out[8:16]


def total_of(acc):
    wide = jnp.concatenate([acc[t] for t in range(acc.shape[0])], axis=1)
    return wide[0:4] + wide[4:8]


def both_ways(lists, p, slot, cache, v_ref):
    n, t = lists[0, p] >> 3, lists[0, p] & 7
    rho = cache[slot]
    ahead = lax.dot_general(v_ref[n], rho, NT, preferred_element_type=F32)
    back = lax.dot_general(v_ref[t, :, 0:BLK], rho, NN, preferred_element_type=F32)
    return t, add_parts(ahead), n, add_parts(back[:, 0:BLK] + back[:, BLK : 2 * BLK])


def add_both(acc, found):
    for t, ahead, n, back in found:
        acc[t] += ahead
        acc[n] += back


def own_pairs(lists, first, count, slot, q, tcol, cache, v_ref, acc):
    steps = jnp.maximum((count + 1) // 2, 1)

    def fill(i):
        for p in (2 * i, 2 * i + 1):
            fill_pair(lists[0, first + p], q, tcol, cache.at[slot + p])

    def multiply(i):
        add_both(
            acc, [both_ways(lists, first + p, slot + p, cache, v_ref) for p in (2 * i, 2 * i + 1)]
        )

    def step(i, _):
        multiply(i - 1)
        fill(i)
        return 0

    fill(0)
    lax.fori_loop(1, steps, step, 0)
    for k in range(UNROLL):
        cache[slot + count + k] = jnp.zeros(cache.shape[1:], BF16)
    multiply(steps - 1)


def own_first_kernel(
    frame, hb, bounds, q_out, tcol_out, lists_out, cache_out, v_ref, acc, lists_v, sem
):
    tile = hb[...]
    tiles = blocks(to_frame(tile, 3, frame[...]))
    per = len(tiles)
    active = active_blocks(
        source_bounds([tile], [0.0], 8), [bounds[k : k + 1, :] for k in range(4)], lax.axis_size("lat")
    )
    lane = lax.broadcasted_iota(jnp.int32, active.shape, 1)
    source, target = lane & 7, (lane >> 3) & 7
    lists_v[...] = list_of(active & (lane < 64) & (target < source), source, target, 1)
    copy = pltpu.make_async_copy(lists_v, lists_out, sem)
    copy.start()
    set_values(tile[0:4], v_ref, 0)
    for b, part in enumerate(tiles):
        q_out[b] = part
    set_columns(tiles, tcol_out)

    def fill_own(b):
        fill_pair(b * 9, q_out, tcol_out, cache_out.at[b])

    def multiply_own(b):
        acc[b] = add_parts(lax.dot_general(v_ref[b], cache_out[b], NT, preferred_element_type=F32))

    def step_own(b, _):
        multiply_own(b - 1)
        fill_own(b)
        return 0

    fill_own(0)
    lax.fori_loop(1, per, step_own, 0)
    multiply_own(per - 1)
    copy.wait()
    count = jnp.minimum(lists_out[1, 0], EARLY)
    own_pairs(lists_out, 0, count, per, q_out, tcol_out, cache_out, v_ref, acc)


def own_second_kernel(lists, q, tcol, v_ref, acc_in, cache_out, acc):
    acc[...] = acc_in[...]
    count = jnp.maximum(lists[1, 0] - EARLY, 0)
    own_pairs(lists, EARLY, count, 0, q, tcol, cache_out, v_ref, acc)


def own_times_kernel(lists, cache, cache_late, u, acc, v_ref):
    set_values(u[0:4, :], v_ref, 0)
    per = acc.shape[0]
    for b in range(per):
        acc[b] = add_parts(lax.dot_general(v_ref[b], cache[b], NT, preferred_element_type=F32))
    half = UNROLL // 2

    def apply(ref, first, count, slot):
        def group(i, _):
            places = [i * half + k for k in range(half)]
            add_both(acc, [both_ways(lists, first + p, slot + p, ref, v_ref) for p in places])
            return 0

        lax.fori_loop(0, (count + half - 1) // half, group, 0)

    count = lists[1, 0]
    apply(cache, 0, jnp.minimum(count, EARLY), per)
    apply(cache_late, EARLY, jnp.maximum(count - EARLY, 0), 0)


OTHERS = [(0, 0), (0, 2), (1, 0), (1, 1), (1, 2), (2, 0), (2, 1), (2, 2)]


def near_first_kernel(
    frame, bounds, corr, tcol, mid, three, four, acc_own, dev, var, field,
    q_out, lists_out, long_out, cache_out, img_out, nxt_out, u_out,
    v_ref, acc, pair, lists_v, mask_v, mask_s, sem, sem_long,
):
    halo = (mid, three, four)
    per = mid.shape[2] // BLK
    turned = frame[...]
    tiles = [halo[c][a] for c, a in OTHERS]
    regions = len(tiles)
    active, lane, source, target = near_active(tiles, OTHERS, turned, bounds)
    active = active & (lane < 64)
    lists_v[...] = list_of(active, source, target, regions)
    copy = pltpu.make_async_copy(lists_v, lists_out, sem)
    copy.start()
    for r in range(regions):
        for b, part in enumerate(blocks(to_frame(tiles[r], 3, turned))):
            q_out[r * per + b] = part
        set_values(tiles[r][0:4], v_ref, r * per)
    acc[...] = acc_own[...]
    copy.wait()
    count = lists_out[1, 0]

    @pl.when(count > KEPT)
    def _():
        long_list(active, source, target, regions, long_out, mask_v, mask_s, sem_long)

    kept = jnp.minimum(count, cache_out.shape[0] - UNROLL)
    steps = jnp.maximum((kept + 1) // 2, 1)

    def fill(i):
        for p in (2 * i, 2 * i + 1):
            fill_pair(lists_out[0, p], q_out, tcol, cache_out.at[p])

    def multiply(i):
        found = []
        for p in (2 * i, 2 * i + 1):
            n = lists_out[0, p] >> 3
            found.append(lax.dot_general(v_ref[n], cache_out[p], NT, preferred_element_type=F32))
        for k in range(2):
            acc[lists_out[0, 2 * i + k] & 7] += add_parts(found[k])

    def step(i, _):
        multiply(i - 1)
        fill(i)
        return 0

    fill(0)
    lax.fori_loop(1, steps, step, 0)
    for k in range(UNROLL):
        cache_out[kept + k] = jnp.zeros(cache_out.shape[1:], BF16)
    multiply(steps - 1)
    extra_pairs(kept, count, long_out, q_out, tcol, v_ref, acc, pair)
    field = field[...]
    dev = dev[...]
    image = dev * mix(corr, total_of(acc)) + var[...] * field
    give_next(image, field, dev, img_out, nxt_out, u_out)


def cells_list_kernel(
    frame, bounds, mid, three, four, lists_out, long_out, lists_v, mask_v, mask_s, sem, sem_long
):
    halo = (mid, three, four)
    where = [(0, 1)] + OTHERS
    tiles = [halo[c][a] for c, a in where]
    active, lane, source, target = near_active(tiles, where, frame[...], bounds)
    active = active & (lane >= 64)
    lists_v[...] = list_of(active, source, target, len(where))
    copy = pltpu.make_async_copy(lists_v, lists_out, sem)
    copy.start()
    copy.wait()

    @pl.when(lists_out[1, 0] > KEPT)
    def _():
        long_list(active, source, target, len(where), long_out, mask_v, mask_s, sem_long)


def mix(corr, total):
    out = None
    for c in range(3):
        term = corr[:, c : c + 1] * total[c : c + 1, :]
        out = term if out is None else out + term
    return out


def extra_pairs(kept, count, long, q_ref, tcol, v_ref, acc, pair):
    def extra(p, _):
        entry = long[0, p]
        fill_pair(entry, q_ref, tcol, pair)
        out = lax.dot_general(v_ref[entry >> 3], pair[...], NT, preferred_element_type=F32)
        acc[entry & 7] += add_parts(out)
        return 0

    lax.fori_loop(kept, count, extra, 0)


def give_next(image, field, dev, img_out, nxt_out, u_out):
    nxt = image - SHIFT * field
    img_out[...] = image
    nxt_out[...] = nxt
    u_out[...] = jnp.concatenate([dev * nxt, jnp.zeros((1, nxt.shape[1]), F32)], axis=0)


def near_times_kernel(
    last, lists, long, corr, cache, q_ref, tcol, acc_own, um, us, un, dev, var, field, *refs
):
    refs, (v_ref, acc, pair) = refs[:-3], refs[-3:]
    outs = refs[-1:] if last else refs
    halo = (um, us, un)
    per = acc.shape[0]
    for k, (c, a) in enumerate(OTHERS):
        set_values(halo[c][a, 0:4, :], v_ref, k * per)
    acc[...] = acc_own[...]
    count = lists[1, 0]
    kept = jnp.minimum(count, cache.shape[0] - UNROLL)

    def group(i, _):
        found = []
        for k in range(UNROLL):
            p = i * UNROLL + k
            n = lists[0, p] >> 3
            found.append(lax.dot_general(v_ref[n], cache[p], NT, preferred_element_type=F32))
        for k in range(UNROLL):
            acc[lists[0, i * UNROLL + k] & 7] += add_parts(found[k])
        return 0

    lax.fori_loop(0, (kept + UNROLL - 1) // UNROLL, group, 0)

    extra_pairs(kept, count, long, q_ref, tcol, v_ref, acc, pair)
    field = field[...]
    dev = dev[...]
    image = dev * mix(corr, total_of(acc)) + var[...] * field
    if last:
        b0, b1, a0, a1 = [ref[...] for ref in refs[:4]]
        sums_out(b0, b1, field, a0, a1, image, outs[0])
    else:
        give_next(image, field, dev, *outs)


def sums_out(b0, b1, b2, a0, a1, a2, out):
    pairs = [(b0, a0), (b0, a1), (b0, a2), (b1, a1), (b1, a2), (b2, a2), (b0, b0), (b1, b0), (b2, b0)]
    rows = []
    for x, y in pairs:
        prod = blocks(x * y)
        while len(prod) > 1:
            prod = [prod[k] + prod[k + 1] for k in range(0, len(prod), 2)]
        rows.append(jnp.sum(prod[0], axis=0, keepdims=True))
    rows.append(jnp.zeros((16 - len(rows), BLK), F32))
    totals = jnp.sum(jnp.concatenate(rows, axis=0), axis=1, keepdims=True)
    sub = lax.broadcasted_iota(jnp.int32, (16, 16), 0)
    col = lax.broadcasted_iota(jnp.int32, (16, 16), 1)
    row = jnp.sum(jnp.where(sub == col, totals, 0.0), axis=0, keepdims=True)
    out[...] = jnp.broadcast_to(row[None], out.shape)


def pack_kernel(q_own, q_near, *refs):
    out = refs[-1]
    fields = [refs[3 * f : 3 * f + 3] for f in range(3)]
    per = q_own.shape[0]
    for f in range(3):
        for r, (c, a) in enumerate([(0, 1)] + OTHERS):
            tile = fields[f][c][a, 0:4, :]
            for b, part in enumerate(blocks(tile)):
                out[r * per + b, 3 * f : 3 * f + 3, :] = part[0:3]
    for b in range(per):
        out[b, 9:12, :] = q_own[b, 0:3, :]
    for n in range(q_near.shape[0]):
        out[per + n, 9:12, :] = q_near[n, 0:3, :]
    for n in range(out.shape[0]):
        out[n, 12:16, :] = jnp.zeros((4, BLK), F32)


def grid_kernel(lists, long, corr, frame, packed, bgg, g_out, tcol, rho, acc):
    cells = g_out.shape[2]
    columns = cells // GRID_ROWS
    bands, sectors = lax.axis_size("lat"), lax.axis_size("lon")
    cell = lax.broadcasted_iota(jnp.int32, (8, cells), 1)
    row = lax.broadcasted_iota(jnp.int32, (8, cells), 0)
    frac_lat = ((cell // columns).astype(F32) + 0.5) / GRID_ROWS
    frac_lon = ((cell % columns).astype(F32) + 0.5) / columns
    band, sector = frame[0:1, 6:7], frame[1:2, 6:7]
    sinlat = -0.9 + 1.8 * (band + frac_lat) / bands
    longitude = 2.0 * math.pi * (sector + frac_lon) / sectors
    coslat = jnp.sqrt(1.0 - sinlat * sinlat)
    point = jnp.where(row == 0, coslat * jnp.cos(longitude), coslat * jnp.sin(longitude))
    point = jnp.where(row == 2, sinlat, point)
    set_columns(blocks(to_frame(point, 0, frame[...])), tcol)
    acc[...] = jnp.zeros(acc.shape, F32)
    count = lists[1, 0]
    short = jnp.minimum(count, KEPT)

    def one(entry, weight, out):
        near = packed[entry >> 3]
        fill_rows(near[9:12], tcol, entry & 7, out)
        v = jnp.concatenate(parts_of(near * weight), axis=0).astype(BF16)
        v = jnp.concatenate([v, v], axis=1)
        got = lax.dot_general(v, out[...], NT, preferred_element_type=F32)
        return got[0:16] + got[16:32] + got[32:48]

    def group(i, _):
        found = []
        for k in range(GROUP):
            p = i * GROUP + k
            weight = jnp.where(p < short, 1.0, 0.0).astype(F32)
            found.append(one(lists[0, p], weight, rho.at[k]))
        for k in range(GROUP):
            acc[lists[0, i * GROUP + k] & 7] += found[k]
        return 0

    lax.fori_loop(0, (short + GROUP - 1) // GROUP, group, 0)

    def extra(p, _):
        entry = long[0, p]
        acc[entry & 7] += one(entry, 1.0, rho.at[0])
        return 0

    lax.fori_loop(short, count, extra, 0)
    total = jnp.concatenate([acc[t] for t in range(acc.shape[0])], axis=1)
    dev = jnp.concatenate([bgg[0], bgg[1], bgg[2]], axis=0)
    for f in range(3):
        g_out[f] = dev * mix(corr, total[3 * f : 3 * f + 3])


def unsort_kernel(rank, b1, b2, w_out):
    slots = rank.shape[1]
    vals = jnp.concatenate([b1[...], b2[...], jnp.zeros((10, slots), F32)], axis=0)
    back = lax.dot_general(split3(vals), onehot_of(rank[...], slots), NN, preferred_element_type=F32)
    back = back[0:16] + back[16:32] + back[32:48]
    w_out[0] = back[0:3]
    w_out[1] = back[3:6]


def final_kernel(parts, innov, w, g, w_out, g_out, w_buf, g_buf, sems):
    sums = parts[...]
    while sums.shape[0] > 1:
        half = sums.shape[0] // 2
        sums = sums[:half] + sums[half:]
    sums = sums[0]
    lane = lax.broadcasted_iota(jnp.int32, sums.shape, 1)
    m00, m01, m02, m11, m12, m22, g0, g1, g2 = [
        jnp.sum(jnp.where(lane == k, sums, 0.0), axis=1, keepdims=True) for k in range(9)
    ]
    l10, l20 = m01 / m00, m02 / m00
    d1 = m11 - l10 * m01
    e12 = m12 - l10 * m02
    ok1 = d1 > 1e-6 * m11
    safe1 = jnp.where(ok1, d1, 1.0)
    l21 = jnp.where(ok1, e12 / safe1, 0.0)
    d2 = m22 - l20 * m02 - l21 * e12
    ok2 = ok1 & (d2 > 1e-6 * m22)
    y1 = g1 - l10 * g0
    y2 = g2 - l20 * g0 - l21 * y1
    c2 = jnp.where(ok2, y2 / jnp.where(ok2, d2, 1.0), 0.0)
    c1 = jnp.where(ok1, y1 / safe1, 0.0) - l21 * c2
    c0 = g0 / m00 - l10 * c1 - l20 * c2
    for k in range(3):
        w_buf[k] = c0 * innov[k : k + 1, :] + c1 * w[0, k : k + 1] + c2 * w[1, k : k + 1]
        g_buf[k] = c0 * g[0, k : k + 1] + c1 * g[1, k : k + 1] + c2 * g[2, k : k + 1]
    copies = [
        pltpu.make_async_copy(w_buf, w_out, sems.at[0]),
        pltpu.make_async_copy(g_buf, g_out, sems.at[1]),
    ]
    for copy in copies:
        copy.start()
    for copy in copies:
        copy.wait()


def swap(x, axis, first):
    count = lax.axis_size(axis)
    pairs = []
    for i in range(first, count, 2):
        pairs += [(i, (i + 1) % count), ((i + 1) % count, i)]
    return lax.ppermute(x, axis, pairs)


def frames(bands, sectors):
    table = np.zeros((bands, sectors, 8, 8), np.float64)
    half = 0.3 / bands
    for i in range(bands):
        s = -0.9 + 1.8 * (i + 0.5) / bands
        c = math.sqrt(1.0 - s * s)
        for j in range(sectors):
            lam = 2.0 * math.pi * (j + 0.5) / sectors
            cl, sl = math.cos(lam), math.sin(lam)
            table[i, j, :3, :3] = np.array([[-sl, cl, 0.0], [-s * cl, -s * sl, c], [c * cl, c * sl, s]]) / half
            table[i, j, :, 3:6] = [c * cl, c * sl, s]
            table[i, j, :5, 6] = [i, j, -sl, cl, 2 * (j % 2) - 1]
    return table.astype(np.float32)


VM = pl.BlockSpec(memory_space=pltpu.VMEM)
SM = pl.BlockSpec(memory_space=pltpu.SMEM)
HB = pl.BlockSpec(memory_space=pltpu.HBM)
LISTS = pltpu.VMEM((8, BLK), jnp.int32)
PAIR = pltpu.VMEM((BLK, 2 * BLK), BF16)


def arr(*shape, dtype=F32):
    return jax.ShapeDtypeStruct(shape, dtype)


def call(kernel, name, ins, outs, scratch, flops, out_specs=None, vmem=VLIM):
    return pl.pallas_call(
        kernel,
        out_shape=outs,
        in_specs=ins,
        out_specs=[VM] * len(outs) if out_specs is None else out_specs,
        scratch_shapes=scratch,
        name=name,
        compiler_params=pltpu.CompilerParams(vmem_limit_bytes=vmem),
        cost_estimate=pl.CostEstimate(flops=flops, bytes_accessed=1 << 20, transcendentals=0),
    )


def tie(first, *rest):
    return lax.optimization_barrier((first, *rest))[0]


def per_device(tile_counts, obs_pos, innovation, bg_std_obs, obs_std, channel_corr, bg_std_grid):
    bands, sectors = lax.axis_size("lat"), lax.axis_size("lon")
    slots = obs_pos.shape[3]
    cells = bg_std_grid.shape[3]
    per = slots // BLK
    grids = cells // BLK
    table = pltpu.with_memory_space_constraint(jnp.asarray(frames(bands, sectors)), pltpu.HBM)

    def flat(x):
        return pltpu.with_memory_space_constraint(x.reshape(3, 1, x.shape[3]), pltpu.HBM)

    obs_in = pltpu.VMEM((3, 1, slots), F32)
    three = arr(3, slots)
    hb, dev, var, b0, rank, frame, bounds, innov, bgg, corr = call(
        sort_kernel,
        "sort",
        [SM] + [HB] * 7,
        [arr(8, slots), three, three, three, arr(1, slots), arr(8, 8), arr(8, BLK), three]
        + [arr(3, 1, cells), arr(3, 3)],
        [obs_in] * 4 + [pltpu.SemaphoreType.DMA((7,))],
        10**8,
    )(
        tile_counts, table, flat(obs_pos), flat(innovation), flat(bg_std_obs), flat(obs_std),
        flat(bg_std_grid), pltpu.with_memory_space_constraint(channel_corr, pltpu.HBM),
    )

    def exchange(block, beside, after):
        one, two = swap(block, "lon", 0), swap(block, "lon", 1)
        first = beside()
        mid = tie(jnp.stack([one, block, two]), first)
        three, four = swap(mid, "lat", 0), swap(mid, "lat", 1)
        second = after(first)
        three, four, second = lax.optimization_barrier((three, four, second))
        return (mid, three, four), first, second

    off = per * (per - 1) // 2

    def own_first():
        return call(
            own_first_kernel,
            "own_first",
            [VM] * 3,
            [
                arr(per, 8, BLK),
                arr(per, 3, BLK, BLK),
                arr(8, BLK, dtype=jnp.int32),
                arr(per + EARLY + UNROLL, BLK, 2 * BLK, dtype=BF16),
                arr(per, 16, 2 * BLK, dtype=BF16),
                arr(per, 8, BLK),
            ],
            [LISTS, pltpu.SemaphoreType.DMA],
            10**9,
            [VM, VM, SM, VM, VM, VM],
        )(frame, hb, bounds)

    def own_second(filled):
        return call(
            own_second_kernel,
            "own_second",
            [SM] + [VM] * 4,
            [arr(off - EARLY + UNROLL, BLK, 2 * BLK, dtype=BF16), arr(per, 8, BLK)],
            [],
            10**9,
        )(filled[2], filled[0], filled[1], filled[4], filled[5])

    def own_times(u):
        return call(
            own_times_kernel,
            "own_times",
            [SM] + [VM] * 3,
            [arr(per, 8, BLK)],
            [pltpu.VMEM((per, 16, 2 * BLK), BF16)],
            10**8,
        )(*filled[2:4], late[0], u)[0]

    near0, filled, late = exchange(hb, own_first, own_second)
    q_own, tcol = filled[:2]
    full = 8 * per * per
    long_scratch = [LISTS, pltpu.VMEM((16, BLK), jnp.int32), pltpu.SMEM((16, BLK), jnp.int32)]
    long_scratch += [pltpu.SemaphoreType.DMA] * 2
    near_scratch = [
        pltpu.VMEM((8 * per, 16, 2 * BLK), BF16),
        pltpu.VMEM((per, 8, BLK), F32),
        PAIR,
    ]
    next_outs = [three, three, arr(4, slots)]
    q_near, lists, long, cache_near, a0, b1, u1 = call(
        near_first_kernel,
        "near_first",
        [VM] * 11,
        [
            arr(8 * per, 8, BLK),
            arr(8, BLK, dtype=jnp.int32),
            arr(1, 10 * BLK, dtype=jnp.int32),
            arr(min(full, KEPT) + UNROLL, BLK, 2 * BLK, dtype=BF16),
        ]
        + next_outs,
        near_scratch + long_scratch,
        10**9,
        [VM, SM, SM, VM, VM, VM, VM],
    )(frame, bounds, corr, tcol, *near0, late[1], dev, var, b0)

    def near_times(halo, acc, field, *earlier):
        last = len(earlier) > 0
        outs = [arr(bands * sectors, 1, 16)] if last else next_outs
        return call(
            functools.partial(near_times_kernel, last),
            "near_times",
            [SM] * 2 + [VM] * (11 + len(earlier)),
            outs,
            near_scratch,
            10**8,
        )(lists, long, corr, cache_near, q_near, tcol, acc, *halo, dev, var, field, *earlier)

    def list_cells(_):
        return call(
            cells_list_kernel,
            "cells_list",
            [VM] * 5,
            [arr(8, BLK, dtype=jnp.int32), arr(1, 10 * BLK, dtype=jnp.int32)],
            long_scratch,
            10**8,
            [SM, SM],
        )(frame, bounds, *near0)

    near1, acc, cells_lists = exchange(u1, lambda: own_times(u1), list_cells)
    a1, b2, u2 = near_times(near1, acc, b1)
    near2, acc, _ = exchange(u2, lambda: own_times(u2), lambda acc: acc)
    (copies,) = near_times(near2, acc, b2, b0, b1, a0, a1)
    (packed,) = call(
        pack_kernel, "pack", [VM] * 11, [arr(9 * per, 16, BLK)], [], 10**7
    )(q_own, q_near, *near0, *near1, *near2)
    copies, packed = lax.optimization_barrier((copies, packed))
    parts = lax.all_to_all(copies, ("lat", "lon"), 0, 0, tiled=True)
    (parts_g,) = call(
        grid_kernel,
        "grid",
        [SM] * 2 + [VM] * 4,
        [arr(3, 3, cells)],
        [
            pltpu.VMEM((cells // BLK, 3, BLK, BLK), F32),
            pltpu.VMEM((GROUP, BLK, 2 * BLK), BF16),
            pltpu.VMEM((cells // BLK, 16, BLK), F32),
        ],
        10**9,
    )(*cells_lists, corr, frame, packed, bgg)
    (parts_w,) = call(unsort_kernel, "unsort", [VM] * 3, [arr(2, 3, slots)], [], 10**8)(rank, b1, b2)
    weights, increment = call(
        final_kernel,
        "final",
        [VM] * 4,
        [arr(3, 1, slots), arr(3, 1, cells)],
        [obs_in, pltpu.VMEM((3, 1, cells), F32), pltpu.SemaphoreType.DMA((2,))],
        10**6,
        [HB, HB],
    )(parts, innov, parts_w, parts_g)
    return weights.reshape(1, 1, 3, slots), increment.reshape(1, 1, 3, cells)


def solution(mesh):
    spec = P("lat", "lon", None, None)
    return jax.shard_map(
        per_device,
        mesh=mesh,
        in_specs=(P("lat", "lon"), spec, spec, spec, spec, P(), spec),
        out_specs=(spec, spec),
        check_vma=False,
    )
```

```python
import functools
import math

import jax
import jax.numpy as jnp
import numpy as np
from jax import lax
from jax.experimental import pallas as pl
from jax.experimental.pallas import tpu as pltpu
from jax.sharding import PartitionSpec as P

OBS_TILE = 512
GRID_ROWS = 16
BLK = 128
SHIFT = 0.5
FAR = 64.0
NT = (((1,), (1,)), ((), ()))
NN = (((1,), (0,)), ((), ()))
F32 = jnp.float32
BF16 = jnp.bfloat16
VLIM = 8 * 1024 * 1024
UNROLL = 16
ROWS = 32
GROUP = 4
KEPT = 96
EARLY = 14
CELLS = 512


def split3(x):
    hi = x.astype(BF16)
    rest = x - hi.astype(F32)
    mid = rest.astype(BF16)
    low = (rest - mid.astype(F32)).astype(BF16)
    return jnp.concatenate([hi, mid, low], axis=0)


def col_of(row):
    return jnp.transpose(jnp.broadcast_to(row, (8, row.shape[1])))[:, 0:1]


def rank_of(key, slots):
    col = col_of(key)
    parts = []
    for j in range(slots // BLK):
        kj = key[:, j * BLK : (j + 1) * BLK]
        total = jnp.zeros((8, BLK), F32)
        for i in range(slots // BLK):
            ki = jnp.broadcast_to(col[i * BLK : (i + 1) * BLK, :], (BLK, BLK))
            if i < j:
                before = ki <= kj
            elif i > j:
                before = ki < kj
            else:
                first = lax.broadcasted_iota(jnp.int32, (BLK, BLK), 0) < lax.broadcasted_iota(
                    jnp.int32, (BLK, BLK), 1
                )
                before = (ki < kj) | ((ki == kj) & first)
            ones = jnp.where(before, 1.0, 0.0).astype(F32)
            total = total + jnp.sum(ones.reshape(BLK // 8, 8, BLK), axis=0)
        parts.append(jnp.sum(total, axis=0, keepdims=True))
    return jnp.concatenate(parts, axis=1)


def onehot_of(rank, slots):
    place = lax.broadcasted_iota(jnp.int32, (slots, slots), 0).astype(F32)
    return jnp.where(place == rank, 1.0, 0.0).astype(BF16)


def angle_of(x):
    x2 = x * x
    return x * (1.0 + x2 * (1.0 / 6.0 + x2 * (3.0 / 40.0 + x2 * (15.0 / 336.0))))


def sort_kernel(
    count, table, pos_in, innov_in, bg_in, std_in, bgg_in, corr_in,
    hb_out, dev_out, var_out, b0_out, rank_out, frame_out, bounds_out, innov_out, bgg_out, corr_out,
    pos, innov, bg, std, sems,
):
    bands, sectors = lax.axis_size("lat"), lax.axis_size("lon")
    band, sector = lax.axis_index("lat"), lax.axis_index("lon")
    pairs = [
        (table.at[band, sector], frame_out),
        (pos_in, pos),
        (innov_in, innov),
        (bg_in, bg),
        (std_in, std),
        (bgg_in, bgg_out),
        (corr_in, corr_out),
    ]
    copies = [pltpu.make_async_copy(x, y, sems.at[k]) for k, (x, y) in enumerate(pairs)]
    for copy in copies:
        copy.start()
    copies[0].wait()
    copies[1].wait()

    def rows(ref):
        return jnp.concatenate([ref[0], ref[1], ref[2]], axis=0)

    slots = pos.shape[2]
    per = slots // BLK
    frame = frame_out[...]
    live_n = count[0, 0] * OBS_TILE
    lane = lax.broadcasted_iota(jnp.int32, (1, slots), 1)
    live = lane < live_n
    px, py, pz = pos[0], pos[1], pos[2]
    key = jnp.where(live, pz, 10.0)
    first = rank_of(key, slots)
    strip = jnp.where(first * 2.0 >= live_n.astype(F32), 8.0, 0.0)
    east = frame[2:3, 6:7] * px + frame[3:4, 6:7] * py
    sine = east * lax.rsqrt(jnp.maximum(px * px + py * py, 1e-6))
    rank = rank_of(jnp.where(live, strip + sine, 100.0), slots)
    rank_out[...] = rank
    for copy in copies[2:]:
        copy.wait()
    maskf = jnp.where(live, 1.0, 0.0).astype(F32)
    where3 = jnp.where(live, rows(pos), FAR)
    dev = rows(bg) * maskf
    start = rows(innov) * maskf
    innov_out[...] = start
    var = rows(std)
    var = var * var * maskf
    sine = jnp.where(live, sine, 0.0)
    vals = jnp.concatenate([where3, dev, start, var, sine, jnp.zeros((3, slots), F32)], axis=0)
    got = lax.dot_general(split3(vals), onehot_of(rank, slots), NT, preferred_element_type=F32)
    got = got[0:16] + got[16:32] + got[32:48]
    dev, start = got[3:6], got[6:9]
    dev_out[...] = dev
    b0_out[...] = start
    var_out[...] = got[9:12]

    z = jnp.concatenate(blocks(got[2:3]), axis=0)
    angle = angle_of(jnp.concatenate(blocks(got[12:13]), axis=0))
    bounds = [
        jnp.min(z, axis=1, keepdims=True),
        jnp.max(z, axis=1, keepdims=True),
        jnp.min(angle, axis=1, keepdims=True),
        jnp.max(angle, axis=1, keepdims=True),
    ]
    sub = lax.broadcasted_iota(jnp.int32, (per, BLK), 0)
    col = lax.broadcasted_iota(jnp.int32, (per, BLK), 1)

    def spread(x, index):
        return jnp.sum(jnp.where(sub == index, x, 0.0), axis=0, keepdims=True)

    as_source = [spread(x, col & 7) for x in bounds]
    pad = jnp.zeros((1, slots - 4 * BLK), F32)
    hb_out[...] = jnp.concatenate(
        [dev * start, got[0:3], jnp.concatenate(as_source + [pad], axis=1), jnp.zeros((1, slots), F32)],
        axis=0,
    )
    as_target = [spread(x, col >> 3) for x in bounds]
    lane = lax.broadcasted_iota(jnp.int32, (1, BLK), 1)
    t = ((lane - 64) >> 3).astype(F32)
    tall = 1.0 * BLK * GRID_ROWS / CELLS
    floor = -0.9 + 1.8 * band.astype(F32) / bands
    step = 1.8 / bands / GRID_ROWS
    half_width = math.pi / sectors
    grid = [
        floor + step * (t * tall + 0.25),
        floor + step * (t * tall + tall - 0.25),
        jnp.full((1, BLK), -half_width, F32),
        jnp.full((1, BLK), half_width, F32),
    ]
    grid_end = 64 + 8 * (CELLS // BLK)
    rows = [
        jnp.where(lane < 64, x, jnp.where(lane < grid_end, g, 100.0)) for x, g in zip(as_target, grid)
    ]
    bounds_out[...] = jnp.concatenate(rows + [jnp.zeros((4, BLK), F32)], axis=0)


def blocks(wide):
    return [wide[:, b * BLK : (b + 1) * BLK] for b in range(wide.shape[1] // BLK)]


def active_blocks(source, target, bands):
    slo, shi, wlo, whi = source
    tlo, thi, vlo, vhi = target

    def radius(z):
        return jnp.sqrt(jnp.maximum(1.0 - z * z, 0.0))

    below, above = jnp.minimum(shi, thi), jnp.maximum(slo, tlo)
    fall = radius(below) - radius(above)
    apart = above - below
    lat = jnp.where(apart > 0.0, apart * apart + fall * fall, 0.0)
    gap = jnp.maximum(jnp.maximum(wlo, vlo) - jnp.minimum(whi, vhi), 0.0)
    gap2 = gap * gap
    small = radius(jnp.maximum(jnp.abs(slo), jnp.abs(shi))) * radius(
        jnp.maximum(jnp.abs(tlo), jnp.abs(thi))
    )
    bound = lat + gap2 * (1.0 - gap2 * (1.0 / 12.0)) * small
    reach = (0.6 / bands) ** 2
    return (bound < reach * 1.002 + 1e-6) & (tlo < 50.0) & (slo < 50.0)


def source_bounds(tiles, shifts, height):
    rows = []
    for k in range(4):
        parts = []
        for tile, shift in zip(tiles, shifts):
            row = tile[6:7, k * BLK : (k + 1) * BLK]
            parts.append(row + shift if k >= 2 else row)
        parts.append(jnp.full((height - len(tiles), BLK), 100.0, F32))
        rows.append(jnp.concatenate(parts, axis=0))
    return rows


def list_of(active, source, target, regions):
    height = active.shape[0]

    def exact(x, y, dims):
        return lax.dot_general(x.astype(BF16), y.astype(BF16), dims, preferred_element_type=F32)

    def ones(mask):
        return jnp.where(mask, 1.0, 0.0).astype(F32)

    def iota(shape, dim):
        return lax.broadcasted_iota(jnp.int32, shape, dim)

    act = ones(active)
    ahead = ones(iota((BLK, BLK), 0) < iota((BLK, BLK), 1))
    above = ones(iota((height, height), 1) < iota((height, height), 0))
    rows = jnp.sum(act, axis=1, keepdims=True)
    place = exact(act, ahead, NN) + exact(above, jnp.broadcast_to(rows, act.shape), NN)
    count = jnp.broadcast_to(jnp.sum(rows, axis=0, keepdims=True), (1, BLK))
    slot = jnp.where(active & (place < BLK), place, -1.0)
    index = iota((BLK, BLK), 0).astype(F32)
    picks = jnp.concatenate([ones(index == slot[r : r + 1]) for r in range(regions)], axis=1)
    names = [
        jnp.concatenate([x[r : r + 1].astype(F32) for r in range(regions)], axis=1)
        for x in (source, target)
    ]
    names = jnp.concatenate(names + [jnp.zeros((6, regions * BLK), F32)], axis=0)
    found = exact(names, picks, NT)
    entries = found[0:1] * 8.0 + found[1:2]
    return jnp.concatenate([entries, count, jnp.zeros((6, BLK), F32)], axis=0).astype(jnp.int32)


def near_active(tiles, where, frame, bounds):
    turn = 2.0 * math.pi / lax.axis_size("lon") * frame[4:5, 6:7]
    active = active_blocks(
        source_bounds(tiles, [(a - 1) * turn for c, a in where], 16),
        [bounds[k : k + 1, :] for k in range(4)],
        lax.axis_size("lat"),
    )
    lane = lax.broadcasted_iota(jnp.int32, active.shape, 1)
    region = lax.broadcasted_iota(jnp.int32, active.shape, 0)
    return active, lane, (lane & 7) + 8 * region, (lane >> 3) & 7


def entries_of(active, source, target):
    return jnp.where(active, source * 8 + target + 1, 0)


def long_list(mask_v, regions, out, mask_s, sem):
    copy = pltpu.make_async_copy(mask_v, mask_s, sem)
    copy.start()
    copy.wait()

    def step(i, k):
        entry = mask_s[i >> 7, i & 127]
        out[0, k] = entry - 1
        return k + jnp.where(entry > 0, 1, 0)

    lax.fori_loop(0, BLK * regions, step, 0)


def rho_of(tcol, sx, sy, sz):
    dx, dy, dz = tcol[0] - sx, tcol[1] - sy, tcol[2] - sz
    s = dx * dx + dy * dy + dz * dz
    r = lax.rsqrt(jnp.maximum(s, 1e-30))
    z = s * r
    inner = s * (((-0.25 * z + 0.5) * z + 0.625) * z - 5.0 / 3.0) + 1.0
    t = jnp.maximum(2.0 - z, 0.0)
    t = t * t
    u = z + 1.0
    outer = (t * t) * (u * u * (1.0 / 12.0) - 0.125) * r
    return jnp.where(s <= 1.0, inner, outer)


def to_frame(tile, row, frame):
    q = None
    for k in range(3):
        term = frame[:, k : k + 1] * (tile[row + k : row + k + 1, :] - frame[:, 3 + k : 4 + k])
        q = term if q is None else q + term
    return q


def set_columns(targets, tcol):
    part = lax.broadcasted_iota(jnp.int32, (24, 3 * BLK), 0)
    lane = lax.broadcasted_iota(jnp.int32, (24, 3 * BLK), 1)
    pick = jnp.where((part & 7) == lane // BLK, 1.0, 0.0).astype(BF16)
    for t, tile in enumerate(targets):
        turned = jnp.transpose(jnp.concatenate(parts_of(tile), axis=0)).astype(BF16)
        wide = lax.dot_general(turned, pick, NN, preferred_element_type=F32)
        for k in range(3):
            tcol[t, k] = wide[:, k * BLK : (k + 1) * BLK]


def fill_rows(q, tcol, t, out):
    sx, sy, sz = q[0:1], q[1:2], q[2:3]
    for i in range(0, BLK, ROWS):
        rho = rho_of([tcol[t, k, i : i + ROWS] for k in range(3)], sx, sy, sz)
        hi = rho.astype(BF16)
        out[i : i + ROWS, 0:BLK] = hi
        out[i : i + ROWS, BLK : 2 * BLK] = (rho - hi.astype(F32)).astype(BF16)


def fill_pair(entry, q_ref, tcol, out):
    fill_rows(q_ref[entry >> 3], tcol, entry & 7, out)


def parts_of(tile):
    hi = tile.astype(BF16).astype(F32)
    rest = tile - hi
    mid = rest.astype(BF16).astype(F32)
    return [hi, mid, rest - mid]


def set_values(rows, v_ref, first):
    v = jnp.concatenate(parts_of(rows) + [jnp.zeros(rows.shape, F32)], axis=0).astype(BF16)
    for b, part in enumerate(blocks(v)):
        v_ref[first + b, :, 0:BLK] = part
        v_ref[first + b, :, BLK : 2 * BLK] = part


def add_parts(out):
    return out[0:8] + out[8:16]


def total_of(acc):
    wide = jnp.concatenate([acc[t] for t in range(acc.shape[0])], axis=1)
    return wide[0:4] + wide[4:8]


def both_ways(lists, p, slot, cache, v_ref):
    n, t = lists[0, p] >> 3, lists[0, p] & 7
    rho = cache[slot]
    ahead = lax.dot_general(v_ref[n], rho, NT, preferred_element_type=F32)
    back = lax.dot_general(v_ref[t, :, 0:BLK], rho, NN, preferred_element_type=F32)
    return t, add_parts(ahead), n, add_parts(back[:, 0:BLK] + back[:, BLK : 2 * BLK])


def add_both(acc, found):
    for t, ahead, n, back in found:
        acc[t] += ahead
        acc[n] += back


def own_pairs(lists, first, count, slot, q, tcol, cache, v_ref, acc):
    steps = jnp.maximum((count + 1) // 2, 1)

    def fill(i):
        for p in (2 * i, 2 * i + 1):
            fill_pair(lists[0, first + p], q, tcol, cache.at[slot + p])

    def multiply(i):
        add_both(
            acc, [both_ways(lists, first + p, slot + p, cache, v_ref) for p in (2 * i, 2 * i + 1)]
        )

    def step(i, _):
        multiply(i - 1)
        fill(i)
        return 0

    fill(0)
    lax.fori_loop(1, steps, step, 0)
    for k in range(UNROLL):
        cache[slot + count + k] = jnp.zeros(cache.shape[1:], BF16)
    multiply(steps - 1)


def own_first_kernel(
    frame, hb, bounds, q_out, tcol_out, lists_out, cache_out, v_ref, acc, lists_v, sem
):
    tile = hb[...]
    tiles = blocks(to_frame(tile, 3, frame[...]))
    per = len(tiles)
    active = active_blocks(
        source_bounds([tile], [0.0], 8), [bounds[k : k + 1, :] for k in range(4)], lax.axis_size("lat")
    )
    lane = lax.broadcasted_iota(jnp.int32, active.shape, 1)
    source, target = lane & 7, (lane >> 3) & 7
    lists_v[...] = list_of(active & (lane < 64) & (target < source), source, target, 1)
    copy = pltpu.make_async_copy(lists_v, lists_out, sem)
    copy.start()
    set_values(tile[0:4], v_ref, 0)
    for b, part in enumerate(tiles):
        q_out[b] = part
    set_columns(tiles, tcol_out)

    def fill_own(b):
        fill_pair(b * 9, q_out, tcol_out, cache_out.at[b])

    def multiply_own(b):
        acc[b] = add_parts(lax.dot_general(v_ref[b], cache_out[b], NT, preferred_element_type=F32))

    def step_own(b, _):
        multiply_own(b - 1)
        fill_own(b)
        return 0

    fill_own(0)
    lax.fori_loop(1, per, step_own, 0)
    multiply_own(per - 1)
    copy.wait()
    count = jnp.minimum(lists_out[1, 0], EARLY)
    own_pairs(lists_out, 0, count, per, q_out, tcol_out, cache_out, v_ref, acc)


def own_second_kernel(lists, q, tcol, v_ref, acc_in, cache_out, acc):
    acc[...] = acc_in[...]
    count = jnp.maximum(lists[1, 0] - EARLY, 0)
    own_pairs(lists, EARLY, count, 0, q, tcol, cache_out, v_ref, acc)


def own_times_kernel(lists, cache, cache_late, u, acc, v_ref):
    set_values(u[0:4, :], v_ref, 0)
    per = acc.shape[0]
    for b in range(per):
        acc[b] = add_parts(lax.dot_general(v_ref[b], cache[b], NT, preferred_element_type=F32))
    half = UNROLL // 2

    def apply(ref, first, count, slot):
        def group(i, _):
            places = [i * half + k for k in range(half)]
            add_both(acc, [both_ways(lists, first + p, slot + p, ref, v_ref) for p in places])
            return 0

        lax.fori_loop(0, (count + half - 1) // half, group, 0)

    count = lists[1, 0]
    apply(cache, 0, jnp.minimum(count, EARLY), per)
    apply(cache_late, EARLY, jnp.maximum(count - EARLY, 0), 0)


OTHERS = [(0, 0), (0, 2), (1, 0), (1, 1), (1, 2), (2, 0), (2, 1), (2, 2)]


def near_first_kernel(
    frame, bounds, corr, tcol, mid, three, four, acc_own, dev, var, field,
    q_out, lists_out, long_out, cache_out, img_out, nxt_out, u_out,
    v_ref, acc, pair, lists_v, mask_v, mask_s, sem, sem_long,
):
    halo = (mid, three, four)
    per = mid.shape[2] // BLK
    turned = frame[...]
    tiles = [halo[c][a] for c, a in OTHERS]
    regions = len(tiles)
    active, lane, source, target = near_active(tiles, OTHERS, turned, bounds)
    active = active & (lane < 64)
    lists_v[...] = list_of(active, source, target, regions)
    copy = pltpu.make_async_copy(lists_v, lists_out, sem)
    copy.start()
    for r in range(regions):
        for b, part in enumerate(blocks(to_frame(tiles[r], 3, turned))):
            q_out[r * per + b] = part
        set_values(tiles[r][0:4], v_ref, r * per)
    acc[...] = acc_own[...]
    copy.wait()
    count = lists_out[1, 0]

    @pl.when(count > KEPT)
    def _():
        mask_v[...] = entries_of(active, source, target)
        long_list(mask_v, regions, long_out, mask_s, sem_long)

    kept = jnp.minimum(count, cache_out.shape[0] - UNROLL)
    steps = jnp.maximum((kept + 1) // 2, 1)

    def fill(i):
        for p in (2 * i, 2 * i + 1):
            fill_pair(lists_out[0, p], q_out, tcol, cache_out.at[p])

    def multiply(i):
        found = []
        for p in (2 * i, 2 * i + 1):
            n = lists_out[0, p] >> 3
            found.append(lax.dot_general(v_ref[n], cache_out[p], NT, preferred_element_type=F32))
        for k in range(2):
            acc[lists_out[0, 2 * i + k] & 7] += add_parts(found[k])

    def step(i, _):
        multiply(i - 1)
        fill(i)
        return 0

    fill(0)
    lax.fori_loop(1, steps, step, 0)
    for k in range(UNROLL):
        cache_out[kept + k] = jnp.zeros(cache_out.shape[1:], BF16)
    multiply(steps - 1)
    extra_pairs(kept, count, long_out, q_out, tcol, v_ref, acc, pair)
    field = field[...]
    dev = dev[...]
    image = dev * mix(corr, total_of(acc)) + var[...] * field
    give_next(image, field, dev, img_out, nxt_out, u_out)


def cells_list_kernel(frame, bounds, mid, three, four, lists_out, mask_out):
    halo = (mid, three, four)
    where = [(0, 1)] + OTHERS
    tiles = [halo[c][a] for c, a in where]
    active, lane, source, target = near_active(tiles, where, frame[...], bounds)
    active = active & (lane >= 64)
    lists_out[...] = list_of(active, source, target, len(where))
    mask_out[...] = entries_of(active, source, target)


def mix(corr, total):
    out = None
    for c in range(3):
        term = corr[:, c : c + 1] * total[c : c + 1, :]
        out = term if out is None else out + term
    return out


def extra_pairs(kept, count, long, q_ref, tcol, v_ref, acc, pair):
    def extra(p, _):
        entry = long[0, p]
        fill_pair(entry, q_ref, tcol, pair)
        out = lax.dot_general(v_ref[entry >> 3], pair[...], NT, preferred_element_type=F32)
        acc[entry & 7] += add_parts(out)
        return 0

    lax.fori_loop(kept, count, extra, 0)


def give_next(image, field, dev, img_out, nxt_out, u_out):
    nxt = image - SHIFT * field
    img_out[...] = image
    nxt_out[...] = nxt
    u_out[...] = jnp.concatenate([dev * nxt, jnp.zeros((1, nxt.shape[1]), F32)], axis=0)


def near_times_kernel(
    last, lists, long, corr, cache, q_ref, tcol, acc_own, um, us, un, dev, var, field, *refs
):
    refs, (v_ref, acc, pair) = refs[:-3], refs[-3:]
    outs = refs[-1:] if last else refs
    halo = (um, us, un)
    per = acc.shape[0]
    for k, (c, a) in enumerate(OTHERS):
        set_values(halo[c][a, 0:4, :], v_ref, k * per)
    acc[...] = acc_own[...]
    count = lists[1, 0]
    kept = jnp.minimum(count, cache.shape[0] - UNROLL)

    def group(i, _):
        found = []
        for k in range(UNROLL):
            p = i * UNROLL + k
            n = lists[0, p] >> 3
            found.append(lax.dot_general(v_ref[n], cache[p], NT, preferred_element_type=F32))
        for k in range(UNROLL):
            acc[lists[0, i * UNROLL + k] & 7] += add_parts(found[k])
        return 0

    lax.fori_loop(0, (kept + UNROLL - 1) // UNROLL, group, 0)

    extra_pairs(kept, count, long, q_ref, tcol, v_ref, acc, pair)
    field = field[...]
    dev = dev[...]
    image = dev * mix(corr, total_of(acc)) + var[...] * field
    if last:
        b0, b1, a0, a1 = [ref[...] for ref in refs[:4]]
        sums_out(b0, b1, field, a0, a1, image, outs[0])
    else:
        give_next(image, field, dev, *outs)


def sums_out(b0, b1, b2, a0, a1, a2, out):
    pairs = [(b0, a0), (b0, a1), (b0, a2), (b1, a1), (b1, a2), (b2, a2), (b0, b0), (b1, b0), (b2, b0)]
    rows = []
    for x, y in pairs:
        prod = blocks(x * y)
        while len(prod) > 1:
            prod = [prod[k] + prod[k + 1] for k in range(0, len(prod), 2)]
        rows.append(jnp.sum(prod[0], axis=0, keepdims=True))
    rows.append(jnp.zeros((16 - len(rows), BLK), F32))
    totals = jnp.sum(jnp.concatenate(rows, axis=0), axis=1, keepdims=True)
    sub = lax.broadcasted_iota(jnp.int32, (16, 16), 0)
    col = lax.broadcasted_iota(jnp.int32, (16, 16), 1)
    row = jnp.sum(jnp.where(sub == col, totals, 0.0), axis=0, keepdims=True)
    out[...] = jnp.broadcast_to(row[None], out.shape)


def pack_kernel(q_own, q_near, *refs):
    out = refs[-1]
    fields = [refs[3 * f : 3 * f + 3] for f in range(3)]
    per = q_own.shape[0]
    for f in range(3):
        for r, (c, a) in enumerate([(0, 1)] + OTHERS):
            tile = fields[f][c][a, 0:4, :]
            for b, part in enumerate(blocks(tile)):
                out[r * per + b, 3 * f : 3 * f + 3, :] = part[0:3]
    for b in range(per):
        out[b, 9:12, :] = q_own[b, 0:3, :]
    for n in range(q_near.shape[0]):
        out[per + n, 9:12, :] = q_near[n, 0:3, :]
    for n in range(out.shape[0]):
        out[n, 12:16, :] = jnp.zeros((4, BLK), F32)


def grid_kernel(
    lists_v, mask_v, corr, frame, packed, bgg, g_out,
    tcol, rho, acc, lists, long, mask_s, sem, sem_long,
):
    copy = pltpu.make_async_copy(lists_v, lists, sem)
    copy.start()
    cells = g_out.shape[2]
    columns = cells // GRID_ROWS
    bands, sectors = lax.axis_size("lat"), lax.axis_size("lon")
    cell = lax.broadcasted_iota(jnp.int32, (8, cells), 1)
    row = lax.broadcasted_iota(jnp.int32, (8, cells), 0)
    frac_lat = ((cell // columns).astype(F32) + 0.5) / GRID_ROWS
    frac_lon = ((cell % columns).astype(F32) + 0.5) / columns
    band, sector = frame[0:1, 6:7], frame[1:2, 6:7]
    sinlat = -0.9 + 1.8 * (band + frac_lat) / bands
    longitude = 2.0 * math.pi * (sector + frac_lon) / sectors
    coslat = jnp.sqrt(1.0 - sinlat * sinlat)
    point = jnp.where(row == 0, coslat * jnp.cos(longitude), coslat * jnp.sin(longitude))
    point = jnp.where(row == 2, sinlat, point)
    set_columns(blocks(to_frame(point, 0, frame[...])), tcol)
    acc[...] = jnp.zeros(acc.shape, F32)
    copy.wait()
    count = lists[1, 0]
    short = jnp.minimum(count, KEPT)

    @pl.when(count > KEPT)
    def _():
        long_list(mask_v, 1 + len(OTHERS), long, mask_s, sem_long)


    def one(entry, weight, out):
        near = packed[entry >> 3]
        fill_rows(near[9:12], tcol, entry & 7, out)
        v = jnp.concatenate(parts_of(near * weight), axis=0).astype(BF16)
        v = jnp.concatenate([v, v], axis=1)
        got = lax.dot_general(v, out[...], NT, preferred_element_type=F32)
        return got[0:16] + got[16:32] + got[32:48]

    def group(i, _):
        found = []
        for k in range(GROUP):
            p = i * GROUP + k
            weight = jnp.where(p < short, 1.0, 0.0).astype(F32)
            found.append(one(lists[0, p], weight, rho.at[k]))
        for k in range(GROUP):
            acc[lists[0, i * GROUP + k] & 7] += found[k]
        return 0

    lax.fori_loop(0, (short + GROUP - 1) // GROUP, group, 0)

    def extra(p, _):
        entry = long[0, p]
        acc[entry & 7] += one(entry, 1.0, rho.at[0])
        return 0

    lax.fori_loop(short, count, extra, 0)
    total = jnp.concatenate([acc[t] for t in range(acc.shape[0])], axis=1)
    dev = jnp.concatenate([bgg[0], bgg[1], bgg[2]], axis=0)
    for f in range(3):
        g_out[f] = dev * mix(corr, total[3 * f : 3 * f + 3])


def unsort_kernel(rank, b1, b2, w_out):
    slots = rank.shape[1]
    vals = jnp.concatenate([b1[...], b2[...], jnp.zeros((10, slots), F32)], axis=0)
    back = lax.dot_general(split3(vals), onehot_of(rank[...], slots), NN, preferred_element_type=F32)
    back = back[0:16] + back[16:32] + back[32:48]
    w_out[0] = back[0:3]
    w_out[1] = back[3:6]


def final_kernel(parts, innov, w, g, w_out, g_out, w_buf, g_buf, sems):
    sums = parts[...]
    while sums.shape[0] > 1:
        half = sums.shape[0] // 2
        sums = sums[:half] + sums[half:]
    sums = sums[0]
    lane = lax.broadcasted_iota(jnp.int32, sums.shape, 1)
    m00, m01, m02, m11, m12, m22, g0, g1, g2 = [
        jnp.sum(jnp.where(lane == k, sums, 0.0), axis=1, keepdims=True) for k in range(9)
    ]
    l10, l20 = m01 / m00, m02 / m00
    d1 = m11 - l10 * m01
    e12 = m12 - l10 * m02
    ok1 = d1 > 1e-6 * m11
    safe1 = jnp.where(ok1, d1, 1.0)
    l21 = jnp.where(ok1, e12 / safe1, 0.0)
    d2 = m22 - l20 * m02 - l21 * e12
    ok2 = ok1 & (d2 > 1e-6 * m22)
    y1 = g1 - l10 * g0
    y2 = g2 - l20 * g0 - l21 * y1
    c2 = jnp.where(ok2, y2 / jnp.where(ok2, d2, 1.0), 0.0)
    c1 = jnp.where(ok1, y1 / safe1, 0.0) - l21 * c2
    c0 = g0 / m00 - l10 * c1 - l20 * c2
    for k in range(3):
        w_buf[k] = c0 * innov[k : k + 1, :] + c1 * w[0, k : k + 1] + c2 * w[1, k : k + 1]
        g_buf[k] = c0 * g[0, k : k + 1] + c1 * g[1, k : k + 1] + c2 * g[2, k : k + 1]
    copies = [
        pltpu.make_async_copy(w_buf, w_out, sems.at[0]),
        pltpu.make_async_copy(g_buf, g_out, sems.at[1]),
    ]
    for copy in copies:
        copy.start()
    for copy in copies:
        copy.wait()


def swap(x, axis, first):
    count = lax.axis_size(axis)
    pairs = []
    for i in range(first, count, 2):
        pairs += [(i, (i + 1) % count), ((i + 1) % count, i)]
    return lax.ppermute(x, axis, pairs)


def frames(bands, sectors):
    table = np.zeros((bands, sectors, 8, 8), np.float64)
    half = 0.3 / bands
    for i in range(bands):
        s = -0.9 + 1.8 * (i + 0.5) / bands
        c = math.sqrt(1.0 - s * s)
        for j in range(sectors):
            lam = 2.0 * math.pi * (j + 0.5) / sectors
            cl, sl = math.cos(lam), math.sin(lam)
            table[i, j, :3, :3] = np.array([[-sl, cl, 0.0], [-s * cl, -s * sl, c], [c * cl, c * sl, s]]) / half
            table[i, j, :, 3:6] = [c * cl, c * sl, s]
            table[i, j, :5, 6] = [i, j, -sl, cl, 2 * (j % 2) - 1]
    return table.astype(np.float32)


VM = pl.BlockSpec(memory_space=pltpu.VMEM)
SM = pl.BlockSpec(memory_space=pltpu.SMEM)
HB = pl.BlockSpec(memory_space=pltpu.HBM)
LISTS = pltpu.VMEM((8, BLK), jnp.int32)
PAIR = pltpu.VMEM((BLK, 2 * BLK), BF16)


def arr(*shape, dtype=F32):
    return jax.ShapeDtypeStruct(shape, dtype)


def call(kernel, name, ins, outs, scratch, flops, out_specs=None, vmem=VLIM):
    return pl.pallas_call(
        kernel,
        out_shape=outs,
        in_specs=ins,
        out_specs=[VM] * len(outs) if out_specs is None else out_specs,
        scratch_shapes=scratch,
        name=name,
        compiler_params=pltpu.CompilerParams(vmem_limit_bytes=vmem),
        cost_estimate=pl.CostEstimate(flops=flops, bytes_accessed=1 << 20, transcendentals=0),
    )


def tie(first, *rest):
    return lax.optimization_barrier((first, *rest))[0]


def per_device(tile_counts, obs_pos, innovation, bg_std_obs, obs_std, channel_corr, bg_std_grid):
    bands, sectors = lax.axis_size("lat"), lax.axis_size("lon")
    slots = obs_pos.shape[3]
    cells = bg_std_grid.shape[3]
    per = slots // BLK
    grids = cells // BLK
    table = pltpu.with_memory_space_constraint(jnp.asarray(frames(bands, sectors)), pltpu.HBM)

    def flat(x):
        return pltpu.with_memory_space_constraint(x.reshape(3, 1, x.shape[3]), pltpu.HBM)

    obs_in = pltpu.VMEM((3, 1, slots), F32)
    three = arr(3, slots)
    hb, dev, var, b0, rank, frame, bounds, innov, bgg, corr = call(
        sort_kernel,
        "sort",
        [SM] + [HB] * 7,
        [arr(8, slots), three, three, three, arr(1, slots), arr(8, 8), arr(8, BLK), three]
        + [arr(3, 1, cells), arr(3, 3)],
        [obs_in] * 4 + [pltpu.SemaphoreType.DMA((7,))],
        10**8,
    )(
        tile_counts, table, flat(obs_pos), flat(innovation), flat(bg_std_obs), flat(obs_std),
        flat(bg_std_grid), pltpu.with_memory_space_constraint(channel_corr, pltpu.HBM),
    )

    def exchange(block, beside, after):
        one, two = swap(block, "lon", 0), swap(block, "lon", 1)
        first = beside()
        mid = tie(jnp.stack([one, block, two]), first)
        three, four = swap(mid, "lat", 0), swap(mid, "lat", 1)
        second = after(first)
        three, four, second = lax.optimization_barrier((three, four, second))
        return (mid, three, four), first, second

    off = per * (per - 1) // 2

    def own_first():
        return call(
            own_first_kernel,
            "own_first",
            [VM] * 3,
            [
                arr(per, 8, BLK),
                arr(per, 3, BLK, BLK),
                arr(8, BLK, dtype=jnp.int32),
                arr(per + EARLY + UNROLL, BLK, 2 * BLK, dtype=BF16),
                arr(per, 16, 2 * BLK, dtype=BF16),
                arr(per, 8, BLK),
            ],
            [LISTS, pltpu.SemaphoreType.DMA],
            10**9,
            [VM, VM, SM, VM, VM, VM],
        )(frame, hb, bounds)

    def own_second(filled):
        return call(
            own_second_kernel,
            "own_second",
            [SM] + [VM] * 4,
            [arr(off - EARLY + UNROLL, BLK, 2 * BLK, dtype=BF16), arr(per, 8, BLK)],
            [],
            10**9,
        )(filled[2], filled[0], filled[1], filled[4], filled[5])

    def own_times(u):
        return call(
            own_times_kernel,
            "own_times",
            [SM] + [VM] * 3,
            [arr(per, 8, BLK)],
            [pltpu.VMEM((per, 16, 2 * BLK), BF16)],
            10**8,
        )(*filled[2:4], late[0], u)[0]

    near0, filled, late = exchange(hb, own_first, own_second)
    q_own, tcol = filled[:2]
    full = 8 * per * per
    long_scratch = [LISTS, pltpu.VMEM((16, BLK), jnp.int32), pltpu.SMEM((16, BLK), jnp.int32)]
    long_scratch += [pltpu.SemaphoreType.DMA] * 2
    near_scratch = [
        pltpu.VMEM((8 * per, 16, 2 * BLK), BF16),
        pltpu.VMEM((per, 8, BLK), F32),
        PAIR,
    ]
    next_outs = [three, three, arr(4, slots)]
    q_near, lists, long, cache_near, a0, b1, u1 = call(
        near_first_kernel,
        "near_first",
        [VM] * 11,
        [
            arr(8 * per, 8, BLK),
            arr(8, BLK, dtype=jnp.int32),
            arr(1, 10 * BLK, dtype=jnp.int32),
            arr(min(full, KEPT) + UNROLL, BLK, 2 * BLK, dtype=BF16),
        ]
        + next_outs,
        near_scratch + long_scratch,
        10**9,
        [VM, SM, SM, VM, VM, VM, VM],
    )(frame, bounds, corr, tcol, *near0, late[1], dev, var, b0)

    def near_times(halo, acc, field, *earlier):
        last = len(earlier) > 0
        outs = [arr(bands * sectors, 1, 16)] if last else next_outs
        return call(
            functools.partial(near_times_kernel, last),
            "near_times",
            [SM] * 2 + [VM] * (11 + len(earlier)),
            outs,
            near_scratch,
            10**8,
        )(lists, long, corr, cache_near, q_near, tcol, acc, *halo, dev, var, field, *earlier)

    def list_cells(_):
        return call(
            cells_list_kernel,
            "cells_list",
            [VM] * 5,
            [arr(8, BLK, dtype=jnp.int32), arr(16, BLK, dtype=jnp.int32)],
            [],
            10**8,
        )(frame, bounds, *near0)

    near1, acc, cells_lists = exchange(u1, lambda: own_times(u1), list_cells)
    a1, b2, u2 = near_times(near1, acc, b1)
    near2, acc, _ = exchange(u2, lambda: own_times(u2), lambda acc: acc)
    (copies,) = near_times(near2, acc, b2, b0, b1, a0, a1)
    (packed,) = call(
        pack_kernel, "pack", [VM] * 11, [arr(9 * per, 16, BLK)], [], 10**7
    )(q_own, q_near, *near0, *near1, *near2)
    copies, packed = lax.optimization_barrier((copies, packed))
    parts = lax.all_to_all(copies, ("lat", "lon"), 0, 0, tiled=True)
    (parts_g,) = call(
        grid_kernel,
        "grid",
        [VM] * 6,
        [arr(3, 3, cells)],
        [
            pltpu.VMEM((cells // BLK, 3, BLK, BLK), F32),
            pltpu.VMEM((GROUP, BLK, 2 * BLK), BF16),
            pltpu.VMEM((cells // BLK, 16, BLK), F32),
            pltpu.SMEM((8, BLK), jnp.int32),
            pltpu.SMEM((1, 10 * BLK), jnp.int32),
            pltpu.SMEM((16, BLK), jnp.int32),
        ]
        + [pltpu.SemaphoreType.DMA] * 2,
        10**9,
    )(*cells_lists, corr, frame, packed, bgg)
    (parts_w,) = call(unsort_kernel, "unsort", [VM] * 3, [arr(2, 3, slots)], [], 10**8)(rank, b1, b2)
    weights, increment = call(
        final_kernel,
        "final",
        [VM] * 4,
        [arr(3, 1, slots), arr(3, 1, cells)],
        [obs_in, pltpu.VMEM((3, 1, cells), F32), pltpu.SemaphoreType.DMA((2,))],
        10**6,
        [HB, HB],
    )(parts, innov, parts_w, parts_g)
    return weights.reshape(1, 1, 3, slots), increment.reshape(1, 1, 3, cells)


def solution(mesh):
    spec = P("lat", "lon", None, None)
    return jax.shard_map(
        per_device,
        mesh=mesh,
        in_specs=(P("lat", "lon"), spec, spec, spec, spec, P(), spec),
        out_specs=(spec, spec),
        check_vma=False,
    )
```

```python
import functools
import math

import jax
import jax.numpy as jnp
import numpy as np
from jax import lax
from jax.experimental import pallas as pl
from jax.experimental.pallas import tpu as pltpu
from jax.sharding import PartitionSpec as P

OBS_TILE = 512
GRID_ROWS = 16
BLK = 128
SHIFT = 0.5
FAR = 64.0
NT = (((1,), (1,)), ((), ()))
NN = (((1,), (0,)), ((), ()))
F32 = jnp.float32
BF16 = jnp.bfloat16
VLIM = 8 * 1024 * 1024
UNROLL = 16
ROWS = 32
GROUP = 4
KEPT = 96
EARLY = 14
CELLS = 512


def split3(x):
    hi = x.astype(BF16)
    rest = x - hi.astype(F32)
    mid = rest.astype(BF16)
    low = (rest - mid.astype(F32)).astype(BF16)
    return jnp.concatenate([hi, mid, low], axis=0)


def col_of(row):
    return jnp.transpose(jnp.broadcast_to(row, (8, row.shape[1])))[:, 0:1]


def rank_of(key, slots):
    col = col_of(key)
    parts = []
    for j in range(slots // BLK):
        kj = key[:, j * BLK : (j + 1) * BLK]
        total = jnp.zeros((8, BLK), F32)
        for i in range(slots // BLK):
            ki = jnp.broadcast_to(col[i * BLK : (i + 1) * BLK, :], (BLK, BLK))
            if i < j:
                before = ki <= kj
            elif i > j:
                before = ki < kj
            else:
                first = lax.broadcasted_iota(jnp.int32, (BLK, BLK), 0) < lax.broadcasted_iota(
                    jnp.int32, (BLK, BLK), 1
                )
                before = (ki < kj) | ((ki == kj) & first)
            ones = jnp.where(before, 1.0, 0.0).astype(F32)
            total = total + jnp.sum(ones.reshape(BLK // 8, 8, BLK), axis=0)
        parts.append(jnp.sum(total, axis=0, keepdims=True))
    return jnp.concatenate(parts, axis=1)


def onehot_of(rank, slots):
    place = lax.broadcasted_iota(jnp.int32, (slots, slots), 0).astype(F32)
    return jnp.where(place == rank, 1.0, 0.0).astype(BF16)


def angle_of(x):
    x2 = x * x
    return x * (1.0 + x2 * (1.0 / 6.0 + x2 * (3.0 / 40.0 + x2 * (15.0 / 336.0))))


def sort_kernel(
    count, table, pos_in, innov_in, bg_in, std_in, bgg_in, corr_in,
    hb_out, dev_out, var_out, b0_out, rank_out, frame_out, bounds_out, innov_out, bgg_out, corr_out,
    pos, innov, bg, std, sems,
):
    bands, sectors = lax.axis_size("lat"), lax.axis_size("lon")
    band, sector = lax.axis_index("lat"), lax.axis_index("lon")
    pairs = [
        (table.at[band, sector], frame_out),
        (pos_in, pos),
        (innov_in, innov),
        (bg_in, bg),
        (std_in, std),
        (bgg_in, bgg_out),
        (corr_in, corr_out),
    ]
    copies = [pltpu.make_async_copy(x, y, sems.at[k]) for k, (x, y) in enumerate(pairs)]
    for copy in copies:
        copy.start()
    copies[0].wait()
    copies[1].wait()

    def rows(ref):
        return jnp.concatenate([ref[0], ref[1], ref[2]], axis=0)

    slots = pos.shape[2]
    per = slots // BLK
    frame = frame_out[...]
    live_n = count[0, 0] * OBS_TILE
    lane = lax.broadcasted_iota(jnp.int32, (1, slots), 1)
    live = lane < live_n
    px, py, pz = pos[0], pos[1], pos[2]
    key = jnp.where(live, pz, 10.0)
    first = rank_of(key, slots)
    strip = jnp.where(first * 2.0 >= live_n.astype(F32), 8.0, 0.0)
    east = frame[2:3, 6:7] * px + frame[3:4, 6:7] * py
    sine = east * lax.rsqrt(jnp.maximum(px * px + py * py, 1e-6))
    rank = rank_of(jnp.where(live, strip + sine, 100.0), slots)
    rank_out[...] = rank
    for copy in copies[2:]:
        copy.wait()
    maskf = jnp.where(live, 1.0, 0.0).astype(F32)
    where3 = jnp.where(live, rows(pos), FAR)
    dev = rows(bg) * maskf
    start = rows(innov) * maskf
    innov_out[...] = start
    var = rows(std)
    var = var * var * maskf
    sine = jnp.where(live, sine, 0.0)
    vals = jnp.concatenate([where3, dev, start, var, sine, jnp.zeros((3, slots), F32)], axis=0)
    got = lax.dot_general(split3(vals), onehot_of(rank, slots), NT, preferred_element_type=F32)
    got = got[0:16] + got[16:32] + got[32:48]
    dev, start = got[3:6], got[6:9]
    dev_out[...] = dev
    b0_out[...] = start
    var_out[...] = got[9:12]

    z = jnp.concatenate(blocks(got[2:3]), axis=0)
    angle = angle_of(jnp.concatenate(blocks(got[12:13]), axis=0))
    bounds = [
        jnp.min(z, axis=1, keepdims=True),
        jnp.max(z, axis=1, keepdims=True),
        jnp.min(angle, axis=1, keepdims=True),
        jnp.max(angle, axis=1, keepdims=True),
    ]
    sub = lax.broadcasted_iota(jnp.int32, (per, BLK), 0)
    col = lax.broadcasted_iota(jnp.int32, (per, BLK), 1)

    def spread(x, index):
        return jnp.sum(jnp.where(sub == index, x, 0.0), axis=0, keepdims=True)

    as_source = [spread(x, col & 7) for x in bounds]
    pad = jnp.zeros((1, slots - 4 * BLK), F32)
    hb_out[...] = jnp.concatenate(
        [dev * start, got[0:3], jnp.concatenate(as_source + [pad], axis=1), jnp.zeros((1, slots), F32)],
        axis=0,
    )
    as_target = [spread(x, col >> 3) for x in bounds]
    lane = lax.broadcasted_iota(jnp.int32, (1, BLK), 1)
    t = ((lane - 64) >> 3).astype(F32)
    tall = 1.0 * BLK * GRID_ROWS / CELLS
    floor = -0.9 + 1.8 * band.astype(F32) / bands
    step = 1.8 / bands / GRID_ROWS
    half_width = math.pi / sectors
    grid = [
        floor + step * (t * tall + 0.25),
        floor + step * (t * tall + tall - 0.25),
        jnp.full((1, BLK), -half_width, F32),
        jnp.full((1, BLK), half_width, F32),
    ]
    grid_end = 64 + 8 * (CELLS // BLK)
    rows = [
        jnp.where(lane < 64, x, jnp.where(lane < grid_end, g, 100.0)) for x, g in zip(as_target, grid)
    ]
    bounds_out[...] = jnp.concatenate(rows + [jnp.zeros((4, BLK), F32)], axis=0)


def blocks(wide):
    return [wide[:, b * BLK : (b + 1) * BLK] for b in range(wide.shape[1] // BLK)]


def active_blocks(source, target, bands):
    slo, shi, wlo, whi = source
    tlo, thi, vlo, vhi = target

    def radius(z):
        return jnp.sqrt(jnp.maximum(1.0 - z * z, 0.0))

    below, above = jnp.minimum(shi, thi), jnp.maximum(slo, tlo)
    fall = radius(below) - radius(above)
    apart = above - below
    lat = jnp.where(apart > 0.0, apart * apart + fall * fall, 0.0)
    gap = jnp.maximum(jnp.maximum(wlo, vlo) - jnp.minimum(whi, vhi), 0.0)
    gap2 = gap * gap
    small = radius(jnp.maximum(jnp.abs(slo), jnp.abs(shi))) * radius(
        jnp.maximum(jnp.abs(tlo), jnp.abs(thi))
    )
    bound = lat + gap2 * (1.0 - gap2 * (1.0 / 12.0)) * small
    reach = (0.6 / bands) ** 2
    return (bound < reach * 1.002 + 1e-6) & (tlo < 50.0) & (slo < 50.0)


def source_bounds(tiles, shifts, height):
    rows = []
    for k in range(4):
        parts = []
        for tile, shift in zip(tiles, shifts):
            row = tile[6:7, k * BLK : (k + 1) * BLK]
            parts.append(row + shift if k >= 2 else row)
        parts.append(jnp.full((height - len(tiles), BLK), 100.0, F32))
        rows.append(jnp.concatenate(parts, axis=0))
    return rows


def list_of(active, source, target, regions):
    height = active.shape[0]

    def exact(x, y, dims):
        return lax.dot_general(x.astype(BF16), y.astype(BF16), dims, preferred_element_type=F32)

    def ones(mask):
        return jnp.where(mask, 1.0, 0.0).astype(F32)

    def iota(shape, dim):
        return lax.broadcasted_iota(jnp.int32, shape, dim)

    act = ones(active)
    ahead = ones(iota((BLK, BLK), 0) < iota((BLK, BLK), 1))
    above = ones(iota((height, height), 1) < iota((height, height), 0))
    rows = jnp.sum(act, axis=1, keepdims=True)
    place = exact(act, ahead, NN) + exact(above, jnp.broadcast_to(rows, act.shape), NN)
    count = jnp.broadcast_to(jnp.sum(rows, axis=0, keepdims=True), (1, BLK))
    slot = jnp.where(active & (place < BLK), place, -1.0)
    index = iota((BLK, BLK), 0).astype(F32)
    picks = jnp.concatenate([ones(index == slot[r : r + 1]) for r in range(regions)], axis=1)
    names = [
        jnp.concatenate([x[r : r + 1].astype(F32) for r in range(regions)], axis=1)
        for x in (source, target)
    ]
    names = jnp.concatenate(names + [jnp.zeros((6, regions * BLK), F32)], axis=0)
    found = exact(names, picks, NT)
    entries = found[0:1] * 8.0 + found[1:2]
    return jnp.concatenate([entries, count, jnp.zeros((6, BLK), F32)], axis=0).astype(jnp.int32)


def near_active(tiles, where, frame, bounds):
    turn = 2.0 * math.pi / lax.axis_size("lon") * frame[4:5, 6:7]
    active = active_blocks(
        source_bounds(tiles, [(a - 1) * turn for c, a in where], 16),
        [bounds[k : k + 1, :] for k in range(4)],
        lax.axis_size("lat"),
    )
    lane = lax.broadcasted_iota(jnp.int32, active.shape, 1)
    region = lax.broadcasted_iota(jnp.int32, active.shape, 0)
    return active, lane, (lane & 7) + 8 * region, (lane >> 3) & 7


def entries_of(active, source, target):
    return jnp.where(active, source * 8 + target + 1, 0)


def long_list(mask_v, regions, out, mask_s, sem):
    copy = pltpu.make_async_copy(mask_v, mask_s, sem)
    copy.start()
    copy.wait()

    def step(i, k):
        entry = mask_s[i >> 7, i & 127]
        out[0, k] = entry - 1
        return k + jnp.where(entry > 0, 1, 0)

    lax.fori_loop(0, BLK * regions, step, 0)


def rho_of(tcol, sx, sy, sz):
    dx, dy, dz = tcol[0] - sx, tcol[1] - sy, tcol[2] - sz
    s = dx * dx + dy * dy + dz * dz
    r = lax.rsqrt(jnp.maximum(s, 1e-30))
    z = s * r
    inner = s * (((-0.25 * z + 0.5) * z + 0.625) * z - 5.0 / 3.0) + 1.0
    t = jnp.maximum(2.0 - z, 0.0)
    t = t * t
    u = z + 1.0
    outer = (t * t) * (u * u * (1.0 / 12.0) - 0.125) * r
    return jnp.where(s <= 1.0, inner, outer)


def to_frame(tile, row, frame):
    q = None
    for k in range(3):
        term = frame[:, k : k + 1] * (tile[row + k : row + k + 1, :] - frame[:, 3 + k : 4 + k])
        q = term if q is None else q + term
    return q


def set_columns(targets, tcol):
    part = lax.broadcasted_iota(jnp.int32, (24, 3 * BLK), 0)
    lane = lax.broadcasted_iota(jnp.int32, (24, 3 * BLK), 1)
    pick = jnp.where((part & 7) == lane // BLK, 1.0, 0.0).astype(BF16)
    for t, tile in enumerate(targets):
        turned = jnp.transpose(jnp.concatenate(parts_of(tile), axis=0)).astype(BF16)
        wide = lax.dot_general(turned, pick, NN, preferred_element_type=F32)
        for k in range(3):
            tcol[t, k] = wide[:, k * BLK : (k + 1) * BLK]


def fill_rows(q, tcol, t, out):
    sx, sy, sz = q[0:1], q[1:2], q[2:3]
    for i in range(0, BLK, ROWS):
        rho = rho_of([tcol[t, k, i : i + ROWS] for k in range(3)], sx, sy, sz)
        hi = rho.astype(BF16)
        out[i : i + ROWS, 0:BLK] = hi
        out[i : i + ROWS, BLK : 2 * BLK] = (rho - hi.astype(F32)).astype(BF16)


def fill_pair(entry, q_ref, tcol, out):
    fill_rows(q_ref[entry >> 3], tcol, entry & 7, out)


def parts_of(tile):
    hi = tile.astype(BF16).astype(F32)
    rest = tile - hi
    mid = rest.astype(BF16).astype(F32)
    return [hi, mid, rest - mid]


def set_values(rows, v_ref, first):
    v = jnp.concatenate(parts_of(rows) + [jnp.zeros(rows.shape, F32)], axis=0).astype(BF16)
    for b, part in enumerate(blocks(v)):
        v_ref[first + b, :, 0:BLK] = part
        v_ref[first + b, :, BLK : 2 * BLK] = part


def add_parts(out):
    return out[0:8] + out[8:16]


def total_of(acc):
    wide = jnp.concatenate([acc[t] for t in range(acc.shape[0])], axis=1)
    return wide[0:4] + wide[4:8]


def both_ways(lists, p, slot, cache, v_ref):
    n, t = lists[0, p] >> 3, lists[0, p] & 7
    rho = cache[slot]
    ahead = lax.dot_general(v_ref[n], rho, NT, preferred_element_type=F32)
    back = lax.dot_general(v_ref[t, :, 0:BLK], rho, NN, preferred_element_type=F32)
    return t, add_parts(ahead), n, add_parts(back[:, 0:BLK] + back[:, BLK : 2 * BLK])


def add_both(acc, found):
    for t, ahead, n, back in found:
        acc[t] += ahead
        acc[n] += back


def own_pairs(lists, first, count, slot, q, tcol, cache, v_ref, acc):
    steps = jnp.maximum((count + 1) // 2, 1)

    def fill(i):
        for p in (2 * i, 2 * i + 1):
            fill_pair(lists[0, first + p], q, tcol, cache.at[slot + p])

    def multiply(i):
        add_both(
            acc, [both_ways(lists, first + p, slot + p, cache, v_ref) for p in (2 * i, 2 * i + 1)]
        )

    def step(i, _):
        multiply(i - 1)
        fill(i)
        return 0

    fill(0)
    lax.fori_loop(1, steps, step, 0)
    for k in range(UNROLL):
        cache[slot + count + k] = jnp.zeros(cache.shape[1:], BF16)
    multiply(steps - 1)


def own_first_kernel(
    frame, hb, bounds, q_out, tcol_out, lists_out, cache_out, v_ref, acc, lists_v, sem
):
    tile = hb[...]
    tiles = blocks(to_frame(tile, 3, frame[...]))
    per = len(tiles)
    active = active_blocks(
        source_bounds([tile], [0.0], 8), [bounds[k : k + 1, :] for k in range(4)], lax.axis_size("lat")
    )
    lane = lax.broadcasted_iota(jnp.int32, active.shape, 1)
    source, target = lane & 7, (lane >> 3) & 7
    lists_v[...] = list_of(active & (lane < 64) & (target < source), source, target, 1)
    copy = pltpu.make_async_copy(lists_v, lists_out, sem)
    copy.start()
    set_values(tile[0:4], v_ref, 0)
    for b, part in enumerate(tiles):
        q_out[b] = part
    set_columns(tiles, tcol_out)

    def fill_own(b):
        fill_pair(b * 9, q_out, tcol_out, cache_out.at[b])

    def multiply_own(b):
        acc[b] = add_parts(lax.dot_general(v_ref[b], cache_out[b], NT, preferred_element_type=F32))

    def step_own(b, _):
        multiply_own(b - 1)
        fill_own(b)
        return 0

    fill_own(0)
    lax.fori_loop(1, per, step_own, 0)
    multiply_own(per - 1)
    copy.wait()
    count = jnp.minimum(lists_out[1, 0], EARLY)
    own_pairs(lists_out, 0, count, per, q_out, tcol_out, cache_out, v_ref, acc)


def own_second_kernel(lists, q, tcol, v_ref, acc_in, cache_out, acc):
    acc[...] = acc_in[...]
    count = jnp.maximum(lists[1, 0] - EARLY, 0)

    @pl.when(count > 0)
    def _():
        own_pairs(lists, EARLY, count, 0, q, tcol, cache_out, v_ref, acc)


def own_times_kernel(lists, cache, cache_late, u, acc, v_ref):
    set_values(u[0:4, :], v_ref, 0)
    per = acc.shape[0]
    for b in range(per):
        acc[b] = add_parts(lax.dot_general(v_ref[b], cache[b], NT, preferred_element_type=F32))
    half = UNROLL // 2

    def apply(ref, first, count, slot):
        def group(i, _):
            places = [i * half + k for k in range(half)]
            add_both(acc, [both_ways(lists, first + p, slot + p, ref, v_ref) for p in places])
            return 0

        lax.fori_loop(0, (count + half - 1) // half, group, 0)

    count = lists[1, 0]
    apply(cache, 0, jnp.minimum(count, EARLY), per)
    apply(cache_late, EARLY, jnp.maximum(count - EARLY, 0), 0)


OTHERS = [(0, 0), (0, 2), (1, 0), (1, 1), (1, 2), (2, 0), (2, 1), (2, 2)]


def near_first_kernel(
    frame, bounds, corr, tcol, mid, three, four, acc_own, dev, var, field,
    q_out, lists_out, long_out, cache_out, img_out, nxt_out, u_out,
    v_ref, acc, pair, lists_v, mask_v, mask_s, sem, sem_long,
):
    halo = (mid, three, four)
    per = mid.shape[2] // BLK
    turned = frame[...]
    tiles = [halo[c][a] for c, a in OTHERS]
    regions = len(tiles)
    active, lane, source, target = near_active(tiles, OTHERS, turned, bounds)
    active = active & (lane < 64)
    lists_v[...] = list_of(active, source, target, regions)
    copy = pltpu.make_async_copy(lists_v, lists_out, sem)
    copy.start()
    for r in range(regions):
        for b, part in enumerate(blocks(to_frame(tiles[r], 3, turned))):
            q_out[r * per + b] = part
        set_values(tiles[r][0:4], v_ref, r * per)
    acc[...] = acc_own[...]
    copy.wait()
    count = lists_out[1, 0]

    @pl.when(count > KEPT)
    def _():
        mask_v[...] = entries_of(active, source, target)
        long_list(mask_v, regions, long_out, mask_s, sem_long)

    kept = jnp.minimum(count, cache_out.shape[0] - UNROLL)
    steps = jnp.maximum((kept + 1) // 2, 1)

    def fill(i):
        for p in (2 * i, 2 * i + 1):
            fill_pair(lists_out[0, p], q_out, tcol, cache_out.at[p])

    def multiply(i):
        found = []
        for p in (2 * i, 2 * i + 1):
            n = lists_out[0, p] >> 3
            found.append(lax.dot_general(v_ref[n], cache_out[p], NT, preferred_element_type=F32))
        for k in range(2):
            acc[lists_out[0, 2 * i + k] & 7] += add_parts(found[k])

    def step(i, _):
        multiply(i - 1)
        fill(i)
        return 0

    fill(0)
    lax.fori_loop(1, steps, step, 0)
    for k in range(UNROLL):
        cache_out[kept + k] = jnp.zeros(cache_out.shape[1:], BF16)
    multiply(steps - 1)
    extra_pairs(kept, count, long_out, q_out, tcol, v_ref, acc, pair)
    field = field[...]
    dev = dev[...]
    image = dev * mix(corr, total_of(acc)) + var[...] * field
    give_next(image, field, dev, img_out, nxt_out, u_out)


def cells_list_kernel(frame, bounds, mid, three, four, lists_out, mask_out):
    halo = (mid, three, four)
    where = [(0, 1)] + OTHERS
    tiles = [halo[c][a] for c, a in where]
    active, lane, source, target = near_active(tiles, where, frame[...], bounds)
    active = active & (lane >= 64)
    lists_out[...] = list_of(active, source, target, len(where))
    mask_out[...] = entries_of(active, source, target)


def mix(corr, total):
    out = None
    for c in range(3):
        term = corr[:, c : c + 1] * total[c : c + 1, :]
        out = term if out is None else out + term
    return out


def extra_pairs(kept, count, long, q_ref, tcol, v_ref, acc, pair):
    def extra(p, _):
        entry = long[0, p]
        fill_pair(entry, q_ref, tcol, pair)
        out = lax.dot_general(v_ref[entry >> 3], pair[...], NT, preferred_element_type=F32)
        acc[entry & 7] += add_parts(out)
        return 0

    lax.fori_loop(kept, count, extra, 0)


def give_next(image, field, dev, img_out, nxt_out, u_out):
    nxt = image - SHIFT * field
    img_out[...] = image
    nxt_out[...] = nxt
    u_out[...] = jnp.concatenate([dev * nxt, jnp.zeros((1, nxt.shape[1]), F32)], axis=0)


def near_times_kernel(
    last, lists, long, corr, cache, q_ref, tcol, acc_own, um, us, un, dev, var, field, *refs
):
    refs, (v_ref, acc, pair) = refs[:-3], refs[-3:]
    outs = refs[-1:] if last else refs
    halo = (um, us, un)
    per = acc.shape[0]
    for k, (c, a) in enumerate(OTHERS):
        set_values(halo[c][a, 0:4, :], v_ref, k * per)
    acc[...] = acc_own[...]
    count = lists[1, 0]
    kept = jnp.minimum(count, cache.shape[0] - UNROLL)

    def group(i, _):
        found = []
        for k in range(UNROLL):
            p = i * UNROLL + k
            n = lists[0, p] >> 3
            found.append(lax.dot_general(v_ref[n], cache[p], NT, preferred_element_type=F32))
        for k in range(UNROLL):
            acc[lists[0, i * UNROLL + k] & 7] += add_parts(found[k])
        return 0

    lax.fori_loop(0, (kept + UNROLL - 1) // UNROLL, group, 0)

    extra_pairs(kept, count, long, q_ref, tcol, v_ref, acc, pair)
    field = field[...]
    dev = dev[...]
    image = dev * mix(corr, total_of(acc)) + var[...] * field
    if last:
        b0, b1, a0, a1 = [ref[...] for ref in refs[:4]]
        sums_out(b0, b1, field, a0, a1, image, outs[0])
    else:
        give_next(image, field, dev, *outs)


def sums_out(b0, b1, b2, a0, a1, a2, out):
    pairs = [(b0, a0), (b0, a1), (b0, a2), (b1, a1), (b1, a2), (b2, a2), (b0, b0), (b1, b0), (b2, b0)]
    rows = []
    for x, y in pairs:
        prod = blocks(x * y)
        while len(prod) > 1:
            prod = [prod[k] + prod[k + 1] for k in range(0, len(prod), 2)]
        rows.append(jnp.sum(prod[0], axis=0, keepdims=True))
    rows.append(jnp.zeros((16 - len(rows), BLK), F32))
    totals = jnp.sum(jnp.concatenate(rows, axis=0), axis=1, keepdims=True)
    sub = lax.broadcasted_iota(jnp.int32, (16, 16), 0)
    col = lax.broadcasted_iota(jnp.int32, (16, 16), 1)
    row = jnp.sum(jnp.where(sub == col, totals, 0.0), axis=0, keepdims=True)
    out[...] = jnp.broadcast_to(row[None], out.shape)


def pack_kernel(q_own, q_near, *refs):
    out = refs[-1]
    fields = [refs[3 * f : 3 * f + 3] for f in range(3)]
    per = q_own.shape[0]
    for f in range(3):
        for r, (c, a) in enumerate([(0, 1)] + OTHERS):
            tile = fields[f][c][a, 0:4, :]
            for b, part in enumerate(blocks(tile)):
                out[r * per + b, 3 * f : 3 * f + 3, :] = part[0:3]
    for b in range(per):
        out[b, 9:12, :] = q_own[b, 0:3, :]
    for n in range(q_near.shape[0]):
        out[per + n, 9:12, :] = q_near[n, 0:3, :]
    for n in range(out.shape[0]):
        out[n, 12:16, :] = jnp.zeros((4, BLK), F32)


def grid_kernel(
    lists_v, mask_v, corr, frame, packed, bgg, g_out,
    tcol, rho, acc, lists, long, mask_s, sem, sem_long,
):
    copy = pltpu.make_async_copy(lists_v, lists, sem)
    copy.start()
    cells = g_out.shape[2]
    columns = cells // GRID_ROWS
    bands, sectors = lax.axis_size("lat"), lax.axis_size("lon")
    cell = lax.broadcasted_iota(jnp.int32, (8, cells), 1)
    row = lax.broadcasted_iota(jnp.int32, (8, cells), 0)
    frac_lat = ((cell // columns).astype(F32) + 0.5) / GRID_ROWS
    frac_lon = ((cell % columns).astype(F32) + 0.5) / columns
    band, sector = frame[0:1, 6:7], frame[1:2, 6:7]
    sinlat = -0.9 + 1.8 * (band + frac_lat) / bands
    longitude = 2.0 * math.pi * (sector + frac_lon) / sectors
    coslat = jnp.sqrt(1.0 - sinlat * sinlat)
    point = jnp.where(row == 0, coslat * jnp.cos(longitude), coslat * jnp.sin(longitude))
    point = jnp.where(row == 2, sinlat, point)
    set_columns(blocks(to_frame(point, 0, frame[...])), tcol)
    acc[...] = jnp.zeros(acc.shape, F32)
    copy.wait()
    count = lists[1, 0]
    short = jnp.minimum(count, KEPT)

    @pl.when(count > KEPT)
    def _():
        long_list(mask_v, 1 + len(OTHERS), long, mask_s, sem_long)


    def one(entry, weight, out):
        near = packed[entry >> 3]
        fill_rows(near[9:12], tcol, entry & 7, out)
        v = jnp.concatenate(parts_of(near * weight), axis=0).astype(BF16)
        v = jnp.concatenate([v, v], axis=1)
        got = lax.dot_general(v, out[...], NT, preferred_element_type=F32)
        return got[0:16] + got[16:32] + got[32:48]

    def group(i, _):
        found = []
        for k in range(GROUP):
            p = i * GROUP + k
            weight = jnp.where(p < short, 1.0, 0.0).astype(F32)
            found.append(one(lists[0, p], weight, rho.at[k]))
        for k in range(GROUP):
            acc[lists[0, i * GROUP + k] & 7] += found[k]
        return 0

    lax.fori_loop(0, (short + GROUP - 1) // GROUP, group, 0)

    def extra(p, _):
        entry = long[0, p]
        acc[entry & 7] += one(entry, 1.0, rho.at[0])
        return 0

    lax.fori_loop(short, count, extra, 0)
    total = jnp.concatenate([acc[t] for t in range(acc.shape[0])], axis=1)
    dev = jnp.concatenate([bgg[0], bgg[1], bgg[2]], axis=0)
    for f in range(3):
        g_out[f] = dev * mix(corr, total[3 * f : 3 * f + 3])


def unsort_kernel(rank, b1, b2, w_out):
    slots = rank.shape[1]
    vals = jnp.concatenate([b1[...], b2[...], jnp.zeros((10, slots), F32)], axis=0)
    back = lax.dot_general(split3(vals), onehot_of(rank[...], slots), NN, preferred_element_type=F32)
    back = back[0:16] + back[16:32] + back[32:48]
    w_out[0] = back[0:3]
    w_out[1] = back[3:6]


def final_kernel(parts, innov, w, g, w_out, g_out, w_buf, g_buf, sems):
    sums = parts[...]
    while sums.shape[0] > 1:
        half = sums.shape[0] // 2
        sums = sums[:half] + sums[half:]
    sums = sums[0]
    lane = lax.broadcasted_iota(jnp.int32, sums.shape, 1)
    m00, m01, m02, m11, m12, m22, g0, g1, g2 = [
        jnp.sum(jnp.where(lane == k, sums, 0.0), axis=1, keepdims=True) for k in range(9)
    ]
    l10, l20 = m01 / m00, m02 / m00
    d1 = m11 - l10 * m01
    e12 = m12 - l10 * m02
    ok1 = d1 > 1e-6 * m11
    safe1 = jnp.where(ok1, d1, 1.0)
    l21 = jnp.where(ok1, e12 / safe1, 0.0)
    d2 = m22 - l20 * m02 - l21 * e12
    ok2 = ok1 & (d2 > 1e-6 * m22)
    y1 = g1 - l10 * g0
    y2 = g2 - l20 * g0 - l21 * y1
    c2 = jnp.where(ok2, y2 / jnp.where(ok2, d2, 1.0), 0.0)
    c1 = jnp.where(ok1, y1 / safe1, 0.0) - l21 * c2
    c0 = g0 / m00 - l10 * c1 - l20 * c2
    for k in range(3):
        w_buf[k] = c0 * innov[k : k + 1, :] + c1 * w[0, k : k + 1] + c2 * w[1, k : k + 1]
        g_buf[k] = c0 * g[0, k : k + 1] + c1 * g[1, k : k + 1] + c2 * g[2, k : k + 1]
    copies = [
        pltpu.make_async_copy(w_buf, w_out, sems.at[0]),
        pltpu.make_async_copy(g_buf, g_out, sems.at[1]),
    ]
    for copy in copies:
        copy.start()
    for copy in copies:
        copy.wait()


def swap(x, axis, first):
    count = lax.axis_size(axis)
    pairs = []
    for i in range(first, count, 2):
        pairs += [(i, (i + 1) % count), ((i + 1) % count, i)]
    return lax.ppermute(x, axis, pairs)


def frames(bands, sectors):
    table = np.zeros((bands, sectors, 8, 8), np.float64)
    half = 0.3 / bands
    for i in range(bands):
        s = -0.9 + 1.8 * (i + 0.5) / bands
        c = math.sqrt(1.0 - s * s)
        for j in range(sectors):
            lam = 2.0 * math.pi * (j + 0.5) / sectors
            cl, sl = math.cos(lam), math.sin(lam)
            table[i, j, :3, :3] = np.array([[-sl, cl, 0.0], [-s * cl, -s * sl, c], [c * cl, c * sl, s]]) / half
            table[i, j, :, 3:6] = [c * cl, c * sl, s]
            table[i, j, :5, 6] = [i, j, -sl, cl, 2 * (j % 2) - 1]
    return table.astype(np.float32)


VM = pl.BlockSpec(memory_space=pltpu.VMEM)
SM = pl.BlockSpec(memory_space=pltpu.SMEM)
HB = pl.BlockSpec(memory_space=pltpu.HBM)
LISTS = pltpu.VMEM((8, BLK), jnp.int32)
PAIR = pltpu.VMEM((BLK, 2 * BLK), BF16)


def arr(*shape, dtype=F32):
    return jax.ShapeDtypeStruct(shape, dtype)


def call(kernel, name, ins, outs, scratch, flops, out_specs=None, vmem=VLIM):
    return pl.pallas_call(
        kernel,
        out_shape=outs,
        in_specs=ins,
        out_specs=[VM] * len(outs) if out_specs is None else out_specs,
        scratch_shapes=scratch,
        name=name,
        compiler_params=pltpu.CompilerParams(vmem_limit_bytes=vmem),
        cost_estimate=pl.CostEstimate(flops=flops, bytes_accessed=1 << 20, transcendentals=0),
    )


def tie(first, *rest):
    return lax.optimization_barrier((first, *rest))[0]


def per_device(tile_counts, obs_pos, innovation, bg_std_obs, obs_std, channel_corr, bg_std_grid):
    bands, sectors = lax.axis_size("lat"), lax.axis_size("lon")
    slots = obs_pos.shape[3]
    cells = bg_std_grid.shape[3]
    per = slots // BLK
    grids = cells // BLK
    table = pltpu.with_memory_space_constraint(jnp.asarray(frames(bands, sectors)), pltpu.HBM)

    def flat(x):
        return pltpu.with_memory_space_constraint(x.reshape(3, 1, x.shape[3]), pltpu.HBM)

    obs_in = pltpu.VMEM((3, 1, slots), F32)
    three = arr(3, slots)
    hb, dev, var, b0, rank, frame, bounds, innov, bgg, corr = call(
        sort_kernel,
        "sort",
        [SM] + [HB] * 7,
        [arr(8, slots), three, three, three, arr(1, slots), arr(8, 8), arr(8, BLK), three]
        + [arr(3, 1, cells), arr(3, 3)],
        [obs_in] * 4 + [pltpu.SemaphoreType.DMA((7,))],
        10**8,
    )(
        tile_counts, table, flat(obs_pos), flat(innovation), flat(bg_std_obs), flat(obs_std),
        flat(bg_std_grid), pltpu.with_memory_space_constraint(channel_corr, pltpu.HBM),
    )

    def exchange(block, beside, after):
        one, two = swap(block, "lon", 0), swap(block, "lon", 1)
        first = beside()
        mid = tie(jnp.stack([one, block, two]), first)
        three, four = swap(mid, "lat", 0), swap(mid, "lat", 1)
        second = after(first)
        three, four, second = lax.optimization_barrier((three, four, second))
        return (mid, three, four), first, second

    off = per * (per - 1) // 2

    def own_first():
        return call(
            own_first_kernel,
            "own_first",
            [VM] * 3,
            [
                arr(per, 8, BLK),
                arr(per, 3, BLK, BLK),
                arr(8, BLK, dtype=jnp.int32),
                arr(per + EARLY + UNROLL, BLK, 2 * BLK, dtype=BF16),
                arr(per, 16, 2 * BLK, dtype=BF16),
                arr(per, 8, BLK),
            ],
            [LISTS, pltpu.SemaphoreType.DMA],
            10**9,
            [VM, VM, SM, VM, VM, VM],
        )(frame, hb, bounds)

    def own_second(filled):
        return call(
            own_second_kernel,
            "own_second",
            [SM] + [VM] * 4,
            [arr(off - EARLY + UNROLL, BLK, 2 * BLK, dtype=BF16), arr(per, 8, BLK)],
            [],
            10**9,
        )(filled[2], filled[0], filled[1], filled[4], filled[5])

    def own_times(u):
        return call(
            own_times_kernel,
            "own_times",
            [SM] + [VM] * 3,
            [arr(per, 8, BLK)],
            [pltpu.VMEM((per, 16, 2 * BLK), BF16)],
            10**8,
        )(*filled[2:4], late[0], u)[0]

    near0, filled, late = exchange(hb, own_first, own_second)
    q_own, tcol = filled[:2]
    full = 8 * per * per
    long_scratch = [LISTS, pltpu.VMEM((16, BLK), jnp.int32), pltpu.SMEM((16, BLK), jnp.int32)]
    long_scratch += [pltpu.SemaphoreType.DMA] * 2
    near_scratch = [
        pltpu.VMEM((8 * per, 16, 2 * BLK), BF16),
        pltpu.VMEM((per, 8, BLK), F32),
        PAIR,
    ]
    next_outs = [three, three, arr(4, slots)]
    q_near, lists, long, cache_near, a0, b1, u1 = call(
        near_first_kernel,
        "near_first",
        [VM] * 11,
        [
            arr(8 * per, 8, BLK),
            arr(8, BLK, dtype=jnp.int32),
            arr(1, 10 * BLK, dtype=jnp.int32),
            arr(min(full, KEPT) + UNROLL, BLK, 2 * BLK, dtype=BF16),
        ]
        + next_outs,
        near_scratch + long_scratch,
        10**9,
        [VM, SM, SM, VM, VM, VM, VM],
    )(frame, bounds, corr, tcol, *near0, late[1], dev, var, b0)

    def near_times(halo, acc, field, *earlier):
        last = len(earlier) > 0
        outs = [arr(bands * sectors, 1, 16)] if last else next_outs
        return call(
            functools.partial(near_times_kernel, last),
            "near_times",
            [SM] * 2 + [VM] * (11 + len(earlier)),
            outs,
            near_scratch,
            10**8,
        )(lists, long, corr, cache_near, q_near, tcol, acc, *halo, dev, var, field, *earlier)

    def list_cells(_):
        return call(
            cells_list_kernel,
            "cells_list",
            [VM] * 5,
            [arr(8, BLK, dtype=jnp.int32), arr(16, BLK, dtype=jnp.int32)],
            [],
            10**8,
        )(frame, bounds, *near0)

    near1, acc, cells_lists = exchange(u1, lambda: own_times(u1), list_cells)
    a1, b2, u2 = near_times(near1, acc, b1)
    near2, acc, _ = exchange(u2, lambda: own_times(u2), lambda acc: acc)
    (copies,) = near_times(near2, acc, b2, b0, b1, a0, a1)
    (packed,) = call(
        pack_kernel, "pack", [VM] * 11, [arr(9 * per, 16, BLK)], [], 10**7
    )(q_own, q_near, *near0, *near1, *near2)
    copies, packed = lax.optimization_barrier((copies, packed))
    parts = lax.all_to_all(copies, ("lat", "lon"), 0, 0, tiled=True)
    (parts_g,) = call(
        grid_kernel,
        "grid",
        [VM] * 6,
        [arr(3, 3, cells)],
        [
            pltpu.VMEM((cells // BLK, 3, BLK, BLK), F32),
            pltpu.VMEM((GROUP, BLK, 2 * BLK), BF16),
            pltpu.VMEM((cells // BLK, 16, BLK), F32),
            pltpu.SMEM((8, BLK), jnp.int32),
            pltpu.SMEM((1, 10 * BLK), jnp.int32),
            pltpu.SMEM((16, BLK), jnp.int32),
        ]
        + [pltpu.SemaphoreType.DMA] * 2,
        10**9,
    )(*cells_lists, corr, frame, packed, bgg)
    (parts_w,) = call(unsort_kernel, "unsort", [VM] * 3, [arr(2, 3, slots)], [], 10**8)(rank, b1, b2)
    weights, increment = call(
        final_kernel,
        "final",
        [VM] * 4,
        [arr(3, 1, slots), arr(3, 1, cells)],
        [obs_in, pltpu.VMEM((3, 1, cells), F32), pltpu.SemaphoreType.DMA((2,))],
        10**6,
        [HB, HB],
    )(parts, innov, parts_w, parts_g)
    return weights.reshape(1, 1, 3, slots), increment.reshape(1, 1, 3, cells)


def solution(mesh):
    spec = P("lat", "lon", None, None)
    return jax.shard_map(
        per_device,
        mesh=mesh,
        in_specs=(P("lat", "lon"), spec, spec, spec, spec, P(), spec),
        out_specs=(spec, spec),
        check_vma=False,
    )
```

```python
import functools
import math

import jax
import jax.numpy as jnp
import numpy as np
from jax import lax
from jax.experimental import pallas as pl
from jax.experimental.pallas import tpu as pltpu
from jax.sharding import PartitionSpec as P

OBS_TILE = 512
GRID_ROWS = 16
BLK = 128
SHIFT = 0.5
FAR = 64.0
NT = (((1,), (1,)), ((), ()))
NN = (((1,), (0,)), ((), ()))
F32 = jnp.float32
BF16 = jnp.bfloat16
VLIM = 8 * 1024 * 1024
UNROLL = 16
ROWS = 32
GROUP = 4
KEPT = 96
EARLY = 10
CELLS = 512


def split3(x):
    hi = x.astype(BF16)
    rest = x - hi.astype(F32)
    mid = rest.astype(BF16)
    low = (rest - mid.astype(F32)).astype(BF16)
    return jnp.concatenate([hi, mid, low], axis=0)


def col_of(row):
    return jnp.transpose(jnp.broadcast_to(row, (8, row.shape[1])))[:, 0:1]


def rank_of(key, slots):
    col = col_of(key)
    parts = []
    for j in range(slots // BLK):
        kj = key[:, j * BLK : (j + 1) * BLK]
        total = jnp.zeros((8, BLK), F32)
        for i in range(slots // BLK):
            ki = jnp.broadcast_to(col[i * BLK : (i + 1) * BLK, :], (BLK, BLK))
            if i < j:
                before = ki <= kj
            elif i > j:
                before = ki < kj
            else:
                first = lax.broadcasted_iota(jnp.int32, (BLK, BLK), 0) < lax.broadcasted_iota(
                    jnp.int32, (BLK, BLK), 1
                )
                before = (ki < kj) | ((ki == kj) & first)
            ones = jnp.where(before, 1.0, 0.0).astype(F32)
            total = total + jnp.sum(ones.reshape(BLK // 8, 8, BLK), axis=0)
        parts.append(jnp.sum(total, axis=0, keepdims=True))
    return jnp.concatenate(parts, axis=1)


def onehot_of(rank, slots):
    place = lax.broadcasted_iota(jnp.int32, (slots, slots), 0).astype(F32)
    return jnp.where(place == rank, 1.0, 0.0).astype(BF16)


def angle_of(x):
    x2 = x * x
    return x * (1.0 + x2 * (1.0 / 6.0 + x2 * (3.0 / 40.0 + x2 * (15.0 / 336.0))))


def sort_kernel(
    count, table, pos_in, innov_in, bg_in, std_in, bgg_in, corr_in,
    hb_out, dev_out, var_out, b0_out, rank_out, frame_out, bounds_out, innov_out, bgg_out, corr_out,
    pos, innov, bg, std, sems,
):
    bands, sectors = lax.axis_size("lat"), lax.axis_size("lon")
    band, sector = lax.axis_index("lat"), lax.axis_index("lon")
    pairs = [
        (table.at[band, sector], frame_out),
        (pos_in, pos),
        (innov_in, innov),
        (bg_in, bg),
        (std_in, std),
        (bgg_in, bgg_out),
        (corr_in, corr_out),
    ]
    copies = [pltpu.make_async_copy(x, y, sems.at[k]) for k, (x, y) in enumerate(pairs)]
    for copy in copies:
        copy.start()
    copies[0].wait()
    copies[1].wait()

    def rows(ref):
        return jnp.concatenate([ref[0], ref[1], ref[2]], axis=0)

    slots = pos.shape[2]
    per = slots // BLK
    frame = frame_out[...]
    live_n = count[0, 0] * OBS_TILE
    lane = lax.broadcasted_iota(jnp.int32, (1, slots), 1)
    live = lane < live_n
    px, py, pz = pos[0], pos[1], pos[2]
    key = jnp.where(live, pz, 10.0)
    first = rank_of(key, slots)
    strip = jnp.where(first * 2.0 >= live_n.astype(F32), 8.0, 0.0)
    east = frame[2:3, 6:7] * px + frame[3:4, 6:7] * py
    sine = east * lax.rsqrt(jnp.maximum(px * px + py * py, 1e-6))
    rank = rank_of(jnp.where(live, strip + sine, 100.0), slots)
    rank_out[...] = rank
    for copy in copies[2:]:
        copy.wait()
    maskf = jnp.where(live, 1.0, 0.0).astype(F32)
    where3 = jnp.where(live, rows(pos), FAR)
    dev = rows(bg) * maskf
    start = rows(innov) * maskf
    innov_out[...] = start
    var = rows(std)
    var = var * var * maskf
    sine = jnp.where(live, sine, 0.0)
    vals = jnp.concatenate([where3, dev, start, var, sine, jnp.zeros((3, slots), F32)], axis=0)
    got = lax.dot_general(split3(vals), onehot_of(rank, slots), NT, preferred_element_type=F32)
    got = got[0:16] + got[16:32] + got[32:48]
    dev, start = got[3:6], got[6:9]
    dev_out[...] = dev
    b0_out[...] = start
    var_out[...] = got[9:12]

    z = jnp.concatenate(blocks(got[2:3]), axis=0)
    angle = angle_of(jnp.concatenate(blocks(got[12:13]), axis=0))
    bounds = [
        jnp.min(z, axis=1, keepdims=True),
        jnp.max(z, axis=1, keepdims=True),
        jnp.min(angle, axis=1, keepdims=True),
        jnp.max(angle, axis=1, keepdims=True),
    ]
    sub = lax.broadcasted_iota(jnp.int32, (per, BLK), 0)
    col = lax.broadcasted_iota(jnp.int32, (per, BLK), 1)

    def spread(x, index):
        return jnp.sum(jnp.where(sub == index, x, 0.0), axis=0, keepdims=True)

    as_source = [spread(x, col & 7) for x in bounds]
    pad = jnp.zeros((1, slots - 4 * BLK), F32)
    hb_out[...] = jnp.concatenate(
        [dev * start, got[0:3], jnp.concatenate(as_source + [pad], axis=1), jnp.zeros((1, slots), F32)],
        axis=0,
    )
    as_target = [spread(x, col >> 3) for x in bounds]
    lane = lax.broadcasted_iota(jnp.int32, (1, BLK), 1)
    t = ((lane - 64) >> 3).astype(F32)
    tall = 1.0 * BLK * GRID_ROWS / CELLS
    floor = -0.9 + 1.8 * band.astype(F32) / bands
    step = 1.8 / bands / GRID_ROWS
    half_width = math.pi / sectors
    grid = [
        floor + step * (t * tall + 0.25),
        floor + step * (t * tall + tall - 0.25),
        jnp.full((1, BLK), -half_width, F32),
        jnp.full((1, BLK), half_width, F32),
    ]
    grid_end = 64 + 8 * (CELLS // BLK)
    rows = [
        jnp.where(lane < 64, x, jnp.where(lane < grid_end, g, 100.0)) for x, g in zip(as_target, grid)
    ]
    bounds_out[...] = jnp.concatenate(rows + [jnp.zeros((4, BLK), F32)], axis=0)


def blocks(wide):
    return [wide[:, b * BLK : (b + 1) * BLK] for b in range(wide.shape[1] // BLK)]


def active_blocks(source, target, bands):
    slo, shi, wlo, whi = source
    tlo, thi, vlo, vhi = target

    def radius(z):
        return jnp.sqrt(jnp.maximum(1.0 - z * z, 0.0))

    below, above = jnp.minimum(shi, thi), jnp.maximum(slo, tlo)
    fall = radius(below) - radius(above)
    apart = above - below
    lat = jnp.where(apart > 0.0, apart * apart + fall * fall, 0.0)
    gap = jnp.maximum(jnp.maximum(wlo, vlo) - jnp.minimum(whi, vhi), 0.0)
    gap2 = gap * gap
    small = radius(jnp.maximum(jnp.abs(slo), jnp.abs(shi))) * radius(
        jnp.maximum(jnp.abs(tlo), jnp.abs(thi))
    )
    bound = lat + gap2 * (1.0 - gap2 * (1.0 / 12.0)) * small
    reach = (0.6 / bands) ** 2
    return (bound < reach * 1.002 + 1e-6) & (tlo < 50.0) & (slo < 50.0)


def source_bounds(tiles, shifts, height):
    rows = []
    for k in range(4):
        parts = []
        for tile, shift in zip(tiles, shifts):
            row = tile[6:7, k * BLK : (k + 1) * BLK]
            parts.append(row + shift if k >= 2 else row)
        parts.append(jnp.full((height - len(tiles), BLK), 100.0, F32))
        rows.append(jnp.concatenate(parts, axis=0))
    return rows


def list_of(active, source, target, regions):
    height = active.shape[0]

    def exact(x, y, dims):
        return lax.dot_general(x.astype(BF16), y.astype(BF16), dims, preferred_element_type=F32)

    def ones(mask):
        return jnp.where(mask, 1.0, 0.0).astype(F32)

    def iota(shape, dim):
        return lax.broadcasted_iota(jnp.int32, shape, dim)

    act = ones(active)
    ahead = ones(iota((BLK, BLK), 0) < iota((BLK, BLK), 1))
    above = ones(iota((height, height), 1) < iota((height, height), 0))
    rows = jnp.sum(act, axis=1, keepdims=True)
    place = exact(act, ahead, NN) + exact(above, jnp.broadcast_to(rows, act.shape), NN)
    count = jnp.broadcast_to(jnp.sum(rows, axis=0, keepdims=True), (1, BLK))
    slot = jnp.where(active & (place < BLK), place, -1.0)
    index = iota((BLK, BLK), 0).astype(F32)
    picks = jnp.concatenate([ones(index == slot[r : r + 1]) for r in range(regions)], axis=1)
    names = [
        jnp.concatenate([x[r : r + 1].astype(F32) for r in range(regions)], axis=1)
        for x in (source, target)
    ]
    names = jnp.concatenate(names + [jnp.zeros((6, regions * BLK), F32)], axis=0)
    found = exact(names, picks, NT)
    entries = found[0:1] * 8.0 + found[1:2]
    return jnp.concatenate([entries, count, jnp.zeros((6, BLK), F32)], axis=0).astype(jnp.int32)


def near_active(tiles, where, frame, bounds):
    turn = 2.0 * math.pi / lax.axis_size("lon") * frame[4:5, 6:7]
    active = active_blocks(
        source_bounds(tiles, [(a - 1) * turn for c, a in where], 16),
        [bounds[k : k + 1, :] for k in range(4)],
        lax.axis_size("lat"),
    )
    lane = lax.broadcasted_iota(jnp.int32, active.shape, 1)
    region = lax.broadcasted_iota(jnp.int32, active.shape, 0)
    return active, lane, (lane & 7) + 8 * region, (lane >> 3) & 7


def entries_of(active, source, target):
    return jnp.where(active, source * 8 + target + 1, 0)


def long_list(mask_v, regions, out, mask_s, sem):
    copy = pltpu.make_async_copy(mask_v, mask_s, sem)
    copy.start()
    copy.wait()

    def step(i, k):
        entry = mask_s[i >> 7, i & 127]
        out[0, k] = entry - 1
        return k + jnp.where(entry > 0, 1, 0)

    lax.fori_loop(0, BLK * regions, step, 0)


def rho_of(tcol, sx, sy, sz):
    dx, dy, dz = tcol[0] - sx, tcol[1] - sy, tcol[2] - sz
    s = dx * dx + dy * dy + dz * dz
    r = lax.rsqrt(jnp.maximum(s, 1e-30))
    z = s * r
    inner = s * (((-0.25 * z + 0.5) * z + 0.625) * z - 5.0 / 3.0) + 1.0
    t = jnp.maximum(2.0 - z, 0.0)
    t = t * t
    u = z + 1.0
    outer = (t * t) * (u * u * (1.0 / 12.0) - 0.125) * r
    return jnp.where(s <= 1.0, inner, outer)


def to_frame(tile, row, frame):
    q = None
    for k in range(3):
        term = frame[:, k : k + 1] * (tile[row + k : row + k + 1, :] - frame[:, 3 + k : 4 + k])
        q = term if q is None else q + term
    return q


def set_columns(targets, tcol):
    part = lax.broadcasted_iota(jnp.int32, (24, 3 * BLK), 0)
    lane = lax.broadcasted_iota(jnp.int32, (24, 3 * BLK), 1)
    pick = jnp.where((part & 7) == lane // BLK, 1.0, 0.0).astype(BF16)
    for t, tile in enumerate(targets):
        turned = jnp.transpose(jnp.concatenate(parts_of(tile), axis=0)).astype(BF16)
        wide = lax.dot_general(turned, pick, NN, preferred_element_type=F32)
        for k in range(3):
            tcol[t, k] = wide[:, k * BLK : (k + 1) * BLK]


def fill_rows(q, tcol, t, out):
    sx, sy, sz = q[0:1], q[1:2], q[2:3]
    for i in range(0, BLK, ROWS):
        rho = rho_of([tcol[t, k, i : i + ROWS] for k in range(3)], sx, sy, sz)
        hi = rho.astype(BF16)
        out[i : i + ROWS, 0:BLK] = hi
        out[i : i + ROWS, BLK : 2 * BLK] = (rho - hi.astype(F32)).astype(BF16)


def fill_pair(entry, q_ref, tcol, out):
    fill_rows(q_ref[entry >> 3], tcol, entry & 7, out)


def parts_of(tile):
    hi = tile.astype(BF16).astype(F32)
    rest = tile - hi
    mid = rest.astype(BF16).astype(F32)
    return [hi, mid, rest - mid]


def set_values(rows, v_ref, first):
    v = jnp.concatenate(parts_of(rows) + [jnp.zeros(rows.shape, F32)], axis=0).astype(BF16)
    for b, part in enumerate(blocks(v)):
        v_ref[first + b, :, 0:BLK] = part
        v_ref[first + b, :, BLK : 2 * BLK] = part


def add_parts(out):
    return out[0:8] + out[8:16]


def total_of(acc):
    wide = jnp.concatenate([acc[t] for t in range(acc.shape[0])], axis=1)
    return wide[0:4] + wide[4:8]


def both_ways(lists, p, slot, cache, v_ref):
    n, t = lists[0, p] >> 3, lists[0, p] & 7
    rho = cache[slot]
    ahead = lax.dot_general(v_ref[n], rho, NT, preferred_element_type=F32)
    back = lax.dot_general(v_ref[t, :, 0:BLK], rho, NN, preferred_element_type=F32)
    return t, add_parts(ahead), n, add_parts(back[:, 0:BLK] + back[:, BLK : 2 * BLK])


def add_both(acc, found):
    for t, ahead, n, back in found:
        acc[t] += ahead
        acc[n] += back


def own_pairs(lists, first, count, slot, q, tcol, cache, v_ref, acc):
    steps = jnp.maximum((count + 1) // 2, 1)

    def fill(i):
        for p in (2 * i, 2 * i + 1):
            fill_pair(lists[0, first + p], q, tcol, cache.at[slot + p])

    def multiply(i):
        add_both(
            acc, [both_ways(lists, first + p, slot + p, cache, v_ref) for p in (2 * i, 2 * i + 1)]
        )

    def step(i, _):
        multiply(i - 1)
        fill(i)
        return 0

    fill(0)
    lax.fori_loop(1, steps, step, 0)
    for k in range(UNROLL):
        cache[slot + count + k] = jnp.zeros(cache.shape[1:], BF16)
    multiply(steps - 1)


def own_first_kernel(
    frame, hb, bounds, q_out, tcol_out, lists_out, cache_out, v_ref, acc, lists_v, sem
):
    tile = hb[...]
    tiles = blocks(to_frame(tile, 3, frame[...]))
    per = len(tiles)
    active = active_blocks(
        source_bounds([tile], [0.0], 8), [bounds[k : k + 1, :] for k in range(4)], lax.axis_size("lat")
    )
    lane = lax.broadcasted_iota(jnp.int32, active.shape, 1)
    source, target = lane & 7, (lane >> 3) & 7
    lists_v[...] = list_of(active & (lane < 64) & (target < source), source, target, 1)
    copy = pltpu.make_async_copy(lists_v, lists_out, sem)
    copy.start()
    set_values(tile[0:4], v_ref, 0)
    for b, part in enumerate(tiles):
        q_out[b] = part
    set_columns(tiles, tcol_out)

    def fill_own(b):
        fill_pair(b * 9, q_out, tcol_out, cache_out.at[b])

    def multiply_own(b):
        acc[b] = add_parts(lax.dot_general(v_ref[b], cache_out[b], NT, preferred_element_type=F32))

    def step_own(b, _):
        multiply_own(b - 1)
        fill_own(b)
        return 0

    fill_own(0)
    lax.fori_loop(1, per, step_own, 0)
    multiply_own(per - 1)
    copy.wait()
    count = jnp.minimum(lists_out[1, 0], EARLY)
    own_pairs(lists_out, 0, count, per, q_out, tcol_out, cache_out, v_ref, acc)


def own_second_kernel(lists, q, tcol, v_ref, acc_in, cache_out, acc):
    acc[...] = acc_in[...]
    count = jnp.maximum(lists[1, 0] - EARLY, 0)
    own_pairs(lists, EARLY, count, 0, q, tcol, cache_out, v_ref, acc)


def own_times_kernel(lists, cache, cache_late, u, acc, v_ref):
    set_values(u[0:4, :], v_ref, 0)
    per = acc.shape[0]
    for b in range(per):
        acc[b] = add_parts(lax.dot_general(v_ref[b], cache[b], NT, preferred_element_type=F32))
    half = UNROLL // 2

    def apply(ref, first, count, slot):
        def group(i, _):
            places = [i * half + k for k in range(half)]
            add_both(acc, [both_ways(lists, first + p, slot + p, ref, v_ref) for p in places])
            return 0

        lax.fori_loop(0, (count + half - 1) // half, group, 0)

    count = lists[1, 0]
    apply(cache, 0, jnp.minimum(count, EARLY), per)
    apply(cache_late, EARLY, jnp.maximum(count - EARLY, 0), 0)


OTHERS = [(0, 0), (0, 2), (1, 0), (1, 1), (1, 2), (2, 0), (2, 1), (2, 2)]


def near_first_kernel(
    frame, bounds, corr, tcol, mid, three, four, acc_own, dev, var, field,
    q_out, lists_out, long_out, cache_out, img_out, nxt_out, u_out,
    v_ref, acc, pair, lists_v, mask_v, mask_s, sem, sem_long,
):
    halo = (mid, three, four)
    per = mid.shape[2] // BLK
    turned = frame[...]
    tiles = [halo[c][a] for c, a in OTHERS]
    regions = len(tiles)
    active, lane, source, target = near_active(tiles, OTHERS, turned, bounds)
    active = active & (lane < 64)
    lists_v[...] = list_of(active, source, target, regions)
    copy = pltpu.make_async_copy(lists_v, lists_out, sem)
    copy.start()
    for r in range(regions):
        for b, part in enumerate(blocks(to_frame(tiles[r], 3, turned))):
            q_out[r * per + b] = part
        set_values(tiles[r][0:4], v_ref, r * per)
    acc[...] = acc_own[...]
    copy.wait()
    count = lists_out[1, 0]

    @pl.when(count > KEPT)
    def _():
        mask_v[...] = entries_of(active, source, target)
        long_list(mask_v, regions, long_out, mask_s, sem_long)

    kept = jnp.minimum(count, cache_out.shape[0] - UNROLL)
    steps = jnp.maximum((kept + 1) // 2, 1)

    def fill(i):
        for p in (2 * i, 2 * i + 1):
            fill_pair(lists_out[0, p], q_out, tcol, cache_out.at[p])

    def multiply(i):
        found = []
        for p in (2 * i, 2 * i + 1):
            n = lists_out[0, p] >> 3
            found.append(lax.dot_general(v_ref[n], cache_out[p], NT, preferred_element_type=F32))
        for k in range(2):
            acc[lists_out[0, 2 * i + k] & 7] += add_parts(found[k])

    def step(i, _):
        multiply(i - 1)
        fill(i)
        return 0

    fill(0)
    lax.fori_loop(1, steps, step, 0)
    for k in range(UNROLL):
        cache_out[kept + k] = jnp.zeros(cache_out.shape[1:], BF16)
    multiply(steps - 1)
    extra_pairs(kept, count, long_out, q_out, tcol, v_ref, acc, pair)
    field = field[...]
    dev = dev[...]
    image = dev * mix(corr, total_of(acc)) + var[...] * field
    give_next(image, field, dev, img_out, nxt_out, u_out)


def cells_list_kernel(frame, bounds, mid, three, four, lists_out, mask_out):
    halo = (mid, three, four)
    where = [(0, 1)] + OTHERS
    tiles = [halo[c][a] for c, a in where]
    active, lane, source, target = near_active(tiles, where, frame[...], bounds)
    active = active & (lane >= 64)
    lists_out[...] = list_of(active, source, target, len(where))
    mask_out[...] = entries_of(active, source, target)


def mix(corr, total):
    out = None
    for c in range(3):
        term = corr[:, c : c + 1] * total[c : c + 1, :]
        out = term if out is None else out + term
    return out


def extra_pairs(kept, count, long, q_ref, tcol, v_ref, acc, pair):
    def extra(p, _):
        entry = long[0, p]
        fill_pair(entry, q_ref, tcol, pair)
        out = lax.dot_general(v_ref[entry >> 3], pair[...], NT, preferred_element_type=F32)
        acc[entry & 7] += add_parts(out)
        return 0

    lax.fori_loop(kept, count, extra, 0)


def give_next(image, field, dev, img_out, nxt_out, u_out):
    nxt = image - SHIFT * field
    img_out[...] = image
    nxt_out[...] = nxt
    u_out[...] = jnp.concatenate([dev * nxt, jnp.zeros((1, nxt.shape[1]), F32)], axis=0)


def near_times_kernel(
    last, lists, long, corr, cache, q_ref, tcol, acc_own, um, us, un, dev, var, field, *refs
):
    refs, (v_ref, acc, pair) = refs[:-3], refs[-3:]
    outs = refs[-1:] if last else refs
    halo = (um, us, un)
    per = acc.shape[0]
    for k, (c, a) in enumerate(OTHERS):
        set_values(halo[c][a, 0:4, :], v_ref, k * per)
    acc[...] = acc_own[...]
    count = lists[1, 0]
    kept = jnp.minimum(count, cache.shape[0] - UNROLL)

    def group(i, _):
        found = []
        for k in range(UNROLL):
            p = i * UNROLL + k
            n = lists[0, p] >> 3
            found.append(lax.dot_general(v_ref[n], cache[p], NT, preferred_element_type=F32))
        for k in range(UNROLL):
            acc[lists[0, i * UNROLL + k] & 7] += add_parts(found[k])
        return 0

    lax.fori_loop(0, (kept + UNROLL - 1) // UNROLL, group, 0)

    extra_pairs(kept, count, long, q_ref, tcol, v_ref, acc, pair)
    field = field[...]
    dev = dev[...]
    image = dev * mix(corr, total_of(acc)) + var[...] * field
    if last:
        b0, b1, a0, a1 = [ref[...] for ref in refs[:4]]
        sums_out(b0, b1, field, a0, a1, image, outs[0])
    else:
        give_next(image, field, dev, *outs)


def sums_out(b0, b1, b2, a0, a1, a2, out):
    pairs = [(b0, a0), (b0, a1), (b0, a2), (b1, a1), (b1, a2), (b2, a2), (b0, b0), (b1, b0), (b2, b0)]
    rows = []
    for x, y in pairs:
        prod = blocks(x * y)
        while len(prod) > 1:
            prod = [prod[k] + prod[k + 1] for k in range(0, len(prod), 2)]
        rows.append(jnp.sum(prod[0], axis=0, keepdims=True))
    rows.append(jnp.zeros((16 - len(rows), BLK), F32))
    totals = jnp.sum(jnp.concatenate(rows, axis=0), axis=1, keepdims=True)
    sub = lax.broadcasted_iota(jnp.int32, (16, 16), 0)
    col = lax.broadcasted_iota(jnp.int32, (16, 16), 1)
    row = jnp.sum(jnp.where(sub == col, totals, 0.0), axis=0, keepdims=True)
    out[...] = jnp.broadcast_to(row[None], out.shape)


def pack_kernel(q_own, q_near, *refs):
    out = refs[-1]
    fields = [refs[3 * f : 3 * f + 3] for f in range(3)]
    per = q_own.shape[0]
    for f in range(3):
        for r, (c, a) in enumerate([(0, 1)] + OTHERS):
            tile = fields[f][c][a, 0:4, :]
            for b, part in enumerate(blocks(tile)):
                out[r * per + b, 3 * f : 3 * f + 3, :] = part[0:3]
    for b in range(per):
        out[b, 9:12, :] = q_own[b, 0:3, :]
    for n in range(q_near.shape[0]):
        out[per + n, 9:12, :] = q_near[n, 0:3, :]
    for n in range(out.shape[0]):
        out[n, 12:16, :] = jnp.zeros((4, BLK), F32)


def grid_kernel(
    lists_v, mask_v, corr, frame, packed, bgg, g_out,
    tcol, rho, acc, lists, long, mask_s, sem, sem_long,
):
    copy = pltpu.make_async_copy(lists_v, lists, sem)
    copy.start()
    cells = g_out.shape[2]
    columns = cells // GRID_ROWS
    bands, sectors = lax.axis_size("lat"), lax.axis_size("lon")
    cell = lax.broadcasted_iota(jnp.int32, (8, cells), 1)
    row = lax.broadcasted_iota(jnp.int32, (8, cells), 0)
    frac_lat = ((cell // columns).astype(F32) + 0.5) / GRID_ROWS
    frac_lon = ((cell % columns).astype(F32) + 0.5) / columns
    band, sector = frame[0:1, 6:7], frame[1:2, 6:7]
    sinlat = -0.9 + 1.8 * (band + frac_lat) / bands
    longitude = 2.0 * math.pi * (sector + frac_lon) / sectors
    coslat = jnp.sqrt(1.0 - sinlat * sinlat)
    point = jnp.where(row == 0, coslat * jnp.cos(longitude), coslat * jnp.sin(longitude))
    point = jnp.where(row == 2, sinlat, point)
    set_columns(blocks(to_frame(point, 0, frame[...])), tcol)
    acc[...] = jnp.zeros(acc.shape, F32)
    copy.wait()
    count = lists[1, 0]
    short = jnp.minimum(count, KEPT)

    @pl.when(count > KEPT)
    def _():
        long_list(mask_v, 1 + len(OTHERS), long, mask_s, sem_long)


    def one(entry, weight, out):
        near = packed[entry >> 3]
        fill_rows(near[9:12], tcol, entry & 7, out)
        v = jnp.concatenate(parts_of(near * weight), axis=0).astype(BF16)
        v = jnp.concatenate([v, v], axis=1)
        got = lax.dot_general(v, out[...], NT, preferred_element_type=F32)
        return got[0:16] + got[16:32] + got[32:48]

    def group(i, _):
        found = []
        for k in range(GROUP):
            p = i * GROUP + k
            weight = jnp.where(p < short, 1.0, 0.0).astype(F32)
            found.append(one(lists[0, p], weight, rho.at[k]))
        for k in range(GROUP):
            acc[lists[0, i * GROUP + k] & 7] += found[k]
        return 0

    lax.fori_loop(0, (short + GROUP - 1) // GROUP, group, 0)

    def extra(p, _):
        entry = long[0, p]
        acc[entry & 7] += one(entry, 1.0, rho.at[0])
        return 0

    lax.fori_loop(short, count, extra, 0)
    total = jnp.concatenate([acc[t] for t in range(acc.shape[0])], axis=1)
    dev = jnp.concatenate([bgg[0], bgg[1], bgg[2]], axis=0)
    for f in range(3):
        g_out[f] = dev * mix(corr, total[3 * f : 3 * f + 3])


def unsort_kernel(rank, b1, b2, w_out):
    slots = rank.shape[1]
    vals = jnp.concatenate([b1[...], b2[...], jnp.zeros((10, slots), F32)], axis=0)
    back = lax.dot_general(split3(vals), onehot_of(rank[...], slots), NN, preferred_element_type=F32)
    back = back[0:16] + back[16:32] + back[32:48]
    w_out[0] = back[0:3]
    w_out[1] = back[3:6]


def final_kernel(parts, innov, w, g, w_out, g_out, w_buf, g_buf, sems):
    sums = parts[...]
    while sums.shape[0] > 1:
        half = sums.shape[0] // 2
        sums = sums[:half] + sums[half:]
    sums = sums[0]
    lane = lax.broadcasted_iota(jnp.int32, sums.shape, 1)
    m00, m01, m02, m11, m12, m22, g0, g1, g2 = [
        jnp.sum(jnp.where(lane == k, sums, 0.0), axis=1, keepdims=True) for k in range(9)
    ]
    l10, l20 = m01 / m00, m02 / m00
    d1 = m11 - l10 * m01
    e12 = m12 - l10 * m02
    ok1 = d1 > 1e-6 * m11
    safe1 = jnp.where(ok1, d1, 1.0)
    l21 = jnp.where(ok1, e12 / safe1, 0.0)
    d2 = m22 - l20 * m02 - l21 * e12
    ok2 = ok1 & (d2 > 1e-6 * m22)
    y1 = g1 - l10 * g0
    y2 = g2 - l20 * g0 - l21 * y1
    c2 = jnp.where(ok2, y2 / jnp.where(ok2, d2, 1.0), 0.0)
    c1 = jnp.where(ok1, y1 / safe1, 0.0) - l21 * c2
    c0 = g0 / m00 - l10 * c1 - l20 * c2
    for k in range(3):
        w_buf[k] = c0 * innov[k : k + 1, :] + c1 * w[0, k : k + 1] + c2 * w[1, k : k + 1]
        g_buf[k] = c0 * g[0, k : k + 1] + c1 * g[1, k : k + 1] + c2 * g[2, k : k + 1]
    copies = [
        pltpu.make_async_copy(w_buf, w_out, sems.at[0]),
        pltpu.make_async_copy(g_buf, g_out, sems.at[1]),
    ]
    for copy in copies:
        copy.start()
    for copy in copies:
        copy.wait()


def swap(x, axis, first):
    count = lax.axis_size(axis)
    pairs = []
    for i in range(first, count, 2):
        pairs += [(i, (i + 1) % count), ((i + 1) % count, i)]
    return lax.ppermute(x, axis, pairs)


def frames(bands, sectors):
    table = np.zeros((bands, sectors, 8, 8), np.float64)
    half = 0.3 / bands
    for i in range(bands):
        s = -0.9 + 1.8 * (i + 0.5) / bands
        c = math.sqrt(1.0 - s * s)
        for j in range(sectors):
            lam = 2.0 * math.pi * (j + 0.5) / sectors
            cl, sl = math.cos(lam), math.sin(lam)
            table[i, j, :3, :3] = np.array([[-sl, cl, 0.0], [-s * cl, -s * sl, c], [c * cl, c * sl, s]]) / half
            table[i, j, :, 3:6] = [c * cl, c * sl, s]
            table[i, j, :5, 6] = [i, j, -sl, cl, 2 * (j % 2) - 1]
    return table.astype(np.float32)


VM = pl.BlockSpec(memory_space=pltpu.VMEM)
SM = pl.BlockSpec(memory_space=pltpu.SMEM)
HB = pl.BlockSpec(memory_space=pltpu.HBM)
LISTS = pltpu.VMEM((8, BLK), jnp.int32)
PAIR = pltpu.VMEM((BLK, 2 * BLK), BF16)


def arr(*shape, dtype=F32):
    return jax.ShapeDtypeStruct(shape, dtype)


def call(kernel, name, ins, outs, scratch, flops, out_specs=None, vmem=VLIM):
    return pl.pallas_call(
        kernel,
        out_shape=outs,
        in_specs=ins,
        out_specs=[VM] * len(outs) if out_specs is None else out_specs,
        scratch_shapes=scratch,
        name=name,
        compiler_params=pltpu.CompilerParams(vmem_limit_bytes=vmem),
        cost_estimate=pl.CostEstimate(flops=flops, bytes_accessed=1 << 20, transcendentals=0),
    )


def tie(first, *rest):
    return lax.optimization_barrier((first, *rest))[0]


def per_device(tile_counts, obs_pos, innovation, bg_std_obs, obs_std, channel_corr, bg_std_grid):
    bands, sectors = lax.axis_size("lat"), lax.axis_size("lon")
    slots = obs_pos.shape[3]
    cells = bg_std_grid.shape[3]
    per = slots // BLK
    grids = cells // BLK
    table = pltpu.with_memory_space_constraint(jnp.asarray(frames(bands, sectors)), pltpu.HBM)

    def flat(x):
        return pltpu.with_memory_space_constraint(x.reshape(3, 1, x.shape[3]), pltpu.HBM)

    obs_in = pltpu.VMEM((3, 1, slots), F32)
    three = arr(3, slots)
    hb, dev, var, b0, rank, frame, bounds, innov, bgg, corr = call(
        sort_kernel,
        "sort",
        [SM] + [HB] * 7,
        [arr(8, slots), three, three, three, arr(1, slots), arr(8, 8), arr(8, BLK), three]
        + [arr(3, 1, cells), arr(3, 3)],
        [obs_in] * 4 + [pltpu.SemaphoreType.DMA((7,))],
        10**8,
    )(
        tile_counts, table, flat(obs_pos), flat(innovation), flat(bg_std_obs), flat(obs_std),
        flat(bg_std_grid), pltpu.with_memory_space_constraint(channel_corr, pltpu.HBM),
    )

    def exchange(block, beside, after):
        one, two = swap(block, "lon", 0), swap(block, "lon", 1)
        first = beside()
        mid = tie(jnp.stack([one, block, two]), first)
        three, four = swap(mid, "lat", 0), swap(mid, "lat", 1)
        second = after(first)
        three, four, second = lax.optimization_barrier((three, four, second))
        return (mid, three, four), first, second

    off = per * (per - 1) // 2

    def own_first():
        return call(
            own_first_kernel,
            "own_first",
            [VM] * 3,
            [
                arr(per, 8, BLK),
                arr(per, 3, BLK, BLK),
                arr(8, BLK, dtype=jnp.int32),
                arr(per + EARLY + UNROLL, BLK, 2 * BLK, dtype=BF16),
                arr(per, 16, 2 * BLK, dtype=BF16),
                arr(per, 8, BLK),
            ],
            [LISTS, pltpu.SemaphoreType.DMA],
            10**9,
            [VM, VM, SM, VM, VM, VM],
        )(frame, hb, bounds)

    def own_second(filled):
        return call(
            own_second_kernel,
            "own_second",
            [SM] + [VM] * 4,
            [arr(off - EARLY + UNROLL, BLK, 2 * BLK, dtype=BF16), arr(per, 8, BLK)],
            [],
            10**9,
        )(filled[2], filled[0], filled[1], filled[4], filled[5])

    def own_times(u):
        return call(
            own_times_kernel,
            "own_times",
            [SM] + [VM] * 3,
            [arr(per, 8, BLK)],
            [pltpu.VMEM((per, 16, 2 * BLK), BF16)],
            10**8,
        )(*filled[2:4], late[0], u)[0]

    near0, filled, late = exchange(hb, own_first, own_second)
    q_own, tcol = filled[:2]
    full = 8 * per * per
    long_scratch = [LISTS, pltpu.VMEM((16, BLK), jnp.int32), pltpu.SMEM((16, BLK), jnp.int32)]
    long_scratch += [pltpu.SemaphoreType.DMA] * 2
    near_scratch = [
        pltpu.VMEM((8 * per, 16, 2 * BLK), BF16),
        pltpu.VMEM((per, 8, BLK), F32),
        PAIR,
    ]
    next_outs = [three, three, arr(4, slots)]
    q_near, lists, long, cache_near, a0, b1, u1 = call(
        near_first_kernel,
        "near_first",
        [VM] * 11,
        [
            arr(8 * per, 8, BLK),
            arr(8, BLK, dtype=jnp.int32),
            arr(1, 10 * BLK, dtype=jnp.int32),
            arr(min(full, KEPT) + UNROLL, BLK, 2 * BLK, dtype=BF16),
        ]
        + next_outs,
        near_scratch + long_scratch,
        10**9,
        [VM, SM, SM, VM, VM, VM, VM],
    )(frame, bounds, corr, tcol, *near0, late[1], dev, var, b0)

    def near_times(halo, acc, field, *earlier):
        last = len(earlier) > 0
        outs = [arr(bands * sectors, 1, 16)] if last else next_outs
        return call(
            functools.partial(near_times_kernel, last),
            "near_times",
            [SM] * 2 + [VM] * (11 + len(earlier)),
            outs,
            near_scratch,
            10**8,
        )(lists, long, corr, cache_near, q_near, tcol, acc, *halo, dev, var, field, *earlier)

    def list_cells(_):
        return call(
            cells_list_kernel,
            "cells_list",
            [VM] * 5,
            [arr(8, BLK, dtype=jnp.int32), arr(16, BLK, dtype=jnp.int32)],
            [],
            10**8,
        )(frame, bounds, *near0)

    near1, acc, cells_lists = exchange(u1, lambda: own_times(u1), list_cells)
    a1, b2, u2 = near_times(near1, acc, b1)
    near2, acc, _ = exchange(u2, lambda: own_times(u2), lambda acc: acc)
    (copies,) = near_times(near2, acc, b2, b0, b1, a0, a1)
    (packed,) = call(
        pack_kernel, "pack", [VM] * 11, [arr(9 * per, 16, BLK)], [], 10**7
    )(q_own, q_near, *near0, *near1, *near2)
    copies, packed = lax.optimization_barrier((copies, packed))
    parts = lax.all_to_all(copies, ("lat", "lon"), 0, 0, tiled=True)
    (parts_g,) = call(
        grid_kernel,
        "grid",
        [VM] * 6,
        [arr(3, 3, cells)],
        [
            pltpu.VMEM((cells // BLK, 3, BLK, BLK), F32),
            pltpu.VMEM((GROUP, BLK, 2 * BLK), BF16),
            pltpu.VMEM((cells // BLK, 16, BLK), F32),
            pltpu.SMEM((8, BLK), jnp.int32),
            pltpu.SMEM((1, 10 * BLK), jnp.int32),
            pltpu.SMEM((16, BLK), jnp.int32),
        ]
        + [pltpu.SemaphoreType.DMA] * 2,
        10**9,
    )(*cells_lists, corr, frame, packed, bgg)
    (parts_w,) = call(unsort_kernel, "unsort", [VM] * 3, [arr(2, 3, slots)], [], 10**8)(rank, b1, b2)
    weights, increment = call(
        final_kernel,
        "final",
        [VM] * 4,
        [arr(3, 1, slots), arr(3, 1, cells)],
        [obs_in, pltpu.VMEM((3, 1, cells), F32), pltpu.SemaphoreType.DMA((2,))],
        10**6,
        [HB, HB],
    )(parts, innov, parts_w, parts_g)
    return weights.reshape(1, 1, 3, slots), increment.reshape(1, 1, 3, cells)


def solution(mesh):
    spec = P("lat", "lon", None, None)
    return jax.shard_map(
        per_device,
        mesh=mesh,
        in_specs=(P("lat", "lon"), spec, spec, spec, spec, P(), spec),
        out_specs=(spec, spec),
        check_vma=False,
    )
```
